32 devices in a mesh: section: 2 (over core), wide: 4 (over y, x), narrow: 4 (over z).
Axes of the slice: x: 2, y: 2, z: 4, core: 2. Of those that a mesh axis runs over, the one named last changes fastest.
Arguments:
- hidden_in: bfloat16 [2, 1024, 3072], P(None, 'wide', 'narrow'), may hold values from -64 to 64
- row_kind: int32 [2, 1024], replicated, may hold values from 0 to 3, as said below
- positions: int32 [3, 2, 1024], replicated, may hold values from 0 to 44, as said below
- timesteps: int32 [2], replicated, may hold values from 0 to 999
- stale_cache: bfloat16 [2, 2, 1024, 48, 128], P('section', None, 'narrow', 'wide'), may hold values from -8 to 8
- w_qkv: bfloat16 [2, 3072, 9216], P('section', 'narrow', 'wide'), may hold values from -0.109375 to 0.109375
- qk_norm: float32 [2, 4, 64], P('section'), may hold values from -6 to 6, as said below
- w_out: bfloat16 [2, 3072, 3072], P('section', 'wide', 'narrow'), may hold values from -0.109375 to 0.109375
- ada_weight: bfloat16 [2, 2, 512, 6, 3072], P('section', None, None, None, 'narrow'), may hold values from -0.25 to 0.25
- w_up: bfloat16 [2, 3072, 12288], P('section', 'narrow', 'wide'), may hold values from -0.109375 to 0.109375
- w_down: bfloat16 [2, 12288, 3072], P('section', 'wide', 'narrow'), may hold values from -0.0546875 to 0.0546875
Outputs:
- layer_out: bfloat16 [2, 2, 1024, 3072], P('section', None, 'wide', 'narrow')
- new_cache: bfloat16 [2, 2, 1024, 48, 128], P('section', None, 'narrow', 'wide')
The draws below stay inside these ranges and needn't reach their ends.
Inputs may be any that keep to these rules, and one draw needn't show every extreme that they name: `row_kind`: kind is 2 times the request (0 or 1) plus 1 for a text row. In each patch the rows of request 0 come first and those of request 1 follow, each request holding 1024/4 rows or more; text rows stand only in patch 0, as the first 128 rows of each request's block. `positions`: rows 0, 1, 2 are frame (below 13), height (below 30) and width (below 45); text rows have all three zero. `qk_norm`: rows are query gain, query bias, key gain, key bias; gains lie in 0.6 to 1.4.
All inputs are finite; a program needn't handle non-finite values.
Results may differ from the reference program's by a relative error of at most 0.019.
Values may be sent and summed in bfloat16 or wider, within the bound.
No kernel may reach another device: no remote copies, remote signals or barrier semaphores. Data moves between devices by JAX's collectives and lax.ppermute only.
A program may use at most 128 MiB of HBM per device.

```python
import jax
import jax.numpy as jnp
from jax import lax

D = 3072
H = 48
HD = 64
FF = 12288
TE = 512
P_SIZE = 2
R = 1024
LF = 13
LH = 30
LW = 45
TXT = 128
LAYERS = 2
N_WIDE = 4
N_NARROW = 4


def draw_hidden_in(key, part):
    noise_key, rough_key = jax.random.split(jax.random.fold_in(key, 23), 2)
    column_place = jnp.arange(D, dtype=jnp.float32) / D
    rough = jax.random.uniform(rough_key, (D,), jnp.float32, 0.7, 1.3)
    noise = jnp.clip(jax.random.normal(noise_key, (P_SIZE, R, D), jnp.float32), -6.0, 6.0)
    values = noise * 5.0 ** column_place * rough
    return values.astype(jnp.bfloat16)


def row_layout(key):
    base = jax.random.fold_in(key, 101)
    split_key, frame_key, height_key, across_key = jax.random.split(base, 4)
    splits = jax.random.randint(split_key, (P_SIZE,), R // 4, 3 * R // 4 + 1)
    index_row = jnp.arange(R, dtype=jnp.int32)[None, :]
    later = (index_row >= splits[:, None]).astype(jnp.int32)
    first_patch = (jnp.arange(P_SIZE, dtype=jnp.int32) == 0)[:, None]
    text_rows = first_patch & ((index_row < TXT) | (index_row >= splits[:, None]) & (index_row < splits[:, None] + TXT))
    text_int = text_rows.astype(jnp.int32)
    kinds = 2 * later + text_int
    frames = jax.random.randint(frame_key, (P_SIZE, R), 0, LF)
    heights = jax.random.randint(height_key, (P_SIZE, R), 0, LH)
    acrosses = jax.random.randint(across_key, (P_SIZE, R), 0, LW)
    last_row = index_row == R - 1
    frames = jnp.where(last_row, LF - 1, frames)
    heights = jnp.where(last_row, LH - 1, heights)
    acrosses = jnp.where(last_row, LW - 1, acrosses)
    located = jnp.stack([frames, heights, acrosses], axis=0) * (1 - text_int)[None]
    return (kinds.astype(jnp.int32), located.astype(jnp.int32))


def draw_row_kind(key, part):
    return row_layout(key)[0]


def draw_positions(key, part):
    return row_layout(key)[1]


def draw_qk_norm(key, part):
    gain_key, bias_key = jax.random.split(jax.random.fold_in(key, 7), 2)
    gains = jax.random.uniform(gain_key, (LAYERS, 2, HD), jnp.float32, 0.6, 1.4)
    biases = jnp.clip(0.5 * jax.random.normal(bias_key, (LAYERS, 2, HD), jnp.float32), -2.0, 2.0)
    stacked = jnp.stack([gains[:, 0], biases[:, 0], gains[:, 1], biases[:, 1]], axis=1)
    return stacked.astype(jnp.float32)


def draw_stale_cache(key, part):
    key_key, value_key, sign_key = jax.random.split(jax.random.fold_in(key, 41), 3)
    key_part = jnp.clip(jax.random.normal(key_key, (LAYERS, P_SIZE, R, H, HD), jnp.float32), -4.0, 4.0)
    value_noise = jnp.clip(jax.random.normal(value_key, (LAYERS, P_SIZE, R, H, HD), jnp.float32), -4.0, 4.0)
    block_signs = jnp.where(jax.random.bernoulli(sign_key, 0.5, (LAYERS, P_SIZE, 16, 1, H, HD)), 1.0, -1.0)
    row_signs = jnp.broadcast_to(block_signs, (LAYERS, P_SIZE, 16, R // 16, H, HD)).reshape(LAYERS, P_SIZE, R, H, HD)
    value_part = value_noise + 4.0 * row_signs
    return jnp.concatenate([key_part, value_part], axis=-1).astype(jnp.bfloat16)


def level_of(key, dims, cuts, low, top_value):
    level = 1.0
    for position, shards_of in cuts:
        steps = jax.random.uniform(jax.random.fold_in(jax.random.fold_in(key, 6), position), (shards_of,), jnp.float32, low / len(cuts), top_value / len(cuts))
        level = level * jnp.repeat(jnp.exp(steps), dims[position] // shards_of).reshape((-1,) + (1,) * (len(dims) - 1 - position))
    return level


def scatter_about(own_key, shape, scale, bound, cuts=(), held_as=jnp.bfloat16):
    result = scale * jax.random.normal(own_key, shape, jnp.float32)
    if cuts:
        result = result * level_of(own_key, shape, cuts, -0.22, 0.18)
    return jnp.clip(result, -bound, bound).astype(held_as)


def setup_inputs(seed: int = 0) -> dict:
    key_of = jax.random.split(jax.random.key(seed), 12)
    hidden_in = draw_hidden_in(jax.random.fold_in(key_of[11], 71), 0)
    row_kind = draw_row_kind(jax.random.fold_in(key_of[11], 71), 0)
    positions = draw_positions(jax.random.fold_in(key_of[11], 71), 0)
    timesteps = jax.random.randint(key_of[3], (2,), 0, 1000).astype(jnp.int32)
    stale_cache = draw_stale_cache(jax.random.fold_in(key_of[11], 71), 0)
    w_qkv = scatter_about(key_of[5], (LAYERS, D, 3 * D), D ** -0.5, 0.109375, ((0, 2), (1, 4), (2, 4)))
    qk_norm = draw_qk_norm(jax.random.fold_in(key_of[11], 71), 0)
    w_out = scatter_about(key_of[7], (LAYERS, D, D), D ** -0.5, 0.109375, ((0, 2), (1, 4), (2, 4)))
    ada_weight = scatter_about(key_of[8], (LAYERS, 2, TE, 6, D), TE ** -0.5, 0.25, ((0, 2), (4, 4)))
    w_up = scatter_about(key_of[9], (LAYERS, D, FF), D ** -0.5, 0.109375, ((0, 2), (1, 4), (2, 4)))
    w_down = scatter_about(key_of[10], (LAYERS, FF, D), FF ** -0.5, 0.0546875, ((0, 2), (1, 4), (2, 4)))
    return {"hidden_in": hidden_in, "row_kind": row_kind, "positions": positions, "timesteps": timesteps, "stale_cache": stale_cache, "w_qkv": w_qkv, "qk_norm": qk_norm, "w_out": w_out, "ada_weight": ada_weight, "w_up": w_up, "w_down": w_down}


EPS_ROW = 1e-05
EPS_HEAD = 1e-06

def time_features(timesteps, feature_count):
    half_count = feature_count // 2
    frequency = jnp.exp(-jnp.log(10000.0) * jnp.arange(half_count, dtype=jnp.float32) / half_count)
    angle = timesteps.astype(jnp.float32)[:, None] * frequency[None, :]
    return jnp.concatenate([jnp.cos(angle), jnp.sin(angle)], axis=1)

def rotary_angles(row_positions, head_dim):
    dim_frame = head_dim // 4
    dim_plane = head_dim // 8 * 3
    pieces = []
    for axis_pos, span_dims in ((0, dim_frame), (1, dim_plane), (2, dim_plane)):
        frequency = 10000.0 ** (-jnp.arange(0, span_dims, 2, dtype=jnp.float32) / span_dims)
        pieces.append(row_positions[axis_pos].astype(jnp.float32)[:, None] * frequency[None, :])
    return jnp.concatenate(pieces, axis=1)

def rotate(values, angles):
    row_count, head_count, head_dim = values.shape
    paired = values.reshape(row_count, head_count, head_dim // 2, 2)
    former = paired[..., 0]
    latter = paired[..., 1]
    cosine = jnp.cos(angles)[:, None, :]
    sine = jnp.sin(angles)[:, None, :]
    turned = jnp.stack([former * cosine - latter * sine, latter * cosine + former * sine], axis=-1)
    return turned.reshape(row_count, head_count, head_dim)

def head_norm(values, gain, offset):
    center = values - lax.optimization_barrier(jnp.mean(values, axis=-1, keepdims=True))
    spread = lax.optimization_barrier(jnp.mean(center * center, axis=-1, keepdims=True))
    return center * lax.rsqrt(spread + EPS_HEAD) * gain + offset

def row_norm(values):
    row_mean = lax.optimization_barrier(jnp.mean(values, axis=1, keepdims=True))
    center = values - row_mean
    variance = lax.optimization_barrier(jnp.mean(center * center, axis=1, keepdims=True))
    return center * lax.rsqrt(variance + EPS_ROW)

def blocked_dot(left, right, block_count):
    block_size = left.shape[1] // block_count
    total = jnp.zeros((left.shape[0], right.shape[1]), jnp.float32)
    for block_index in range(block_count):
        term = jnp.dot(left[:, block_index * block_size:(block_index + 1) * block_size], right[block_index * block_size:(block_index + 1) * block_size], preferred_element_type=jnp.float32)
        total = total + lax.optimization_barrier(term.astype(jnp.bfloat16)).astype(jnp.float32)
    return total

def attend(queries, query_kinds, cache_now, row_kind):
    keys_flat = cache_now.reshape(P_SIZE * R, H, 2 * HD)
    allowed = (query_kinds // 2)[:, None] == (row_kind // 2).reshape(-1)[None, :]
    query_heads = jnp.transpose(queries, (1, 0, 2))
    key_heads = jnp.transpose(keys_flat, (1, 0, 2))

    def one_head(operands):
        head_queries, head_keys = operands
        scores = jnp.dot(head_queries, head_keys[:, :HD].T, preferred_element_type=jnp.float32) * HD ** (-0.5)
        masked = jnp.where(allowed, scores, -1e+30)
        top = lax.optimization_barrier(jnp.max(masked, axis=1, keepdims=True))
        weights = jnp.where(allowed, jnp.exp(masked - top), 0.0)
        total = lax.optimization_barrier(jnp.sum(weights, axis=1, keepdims=True))
        mixed = jnp.dot(weights.astype(jnp.bfloat16), head_keys[:, HD:], preferred_element_type=jnp.float32)
        return mixed / total
    mixed_heads = lax.map(one_head, (query_heads, key_heads))
    return jnp.transpose(mixed_heads, (1, 0, 2)).reshape(R, H * HD).astype(jnp.bfloat16)

def reference(hidden_in, row_kind, positions, timesteps, stale_cache, w_qkv, qk_norm, w_out, ada_weight, w_up, w_down):
    activated = jax.nn.silu(time_features(timesteps, TE)).astype(jnp.bfloat16)
    all_outputs = []
    all_caches = []
    previous = [hidden_in[patch_index] for patch_index in range(P_SIZE)]
    for layer in range(LAYERS):
        modulation = jnp.einsum('re,kesd->krsd', activated.astype(jnp.float32), ada_weight[layer].astype(jnp.float32))
        tables = modulation.reshape(2, 4, 3, D)
        cache_now = stale_cache[layer]
        norms = qk_norm[layer]
        layer_outs = []
        for patch_index in range(P_SIZE):
            x_in = previous[patch_index].astype(jnp.float32)
            kinds = row_kind[patch_index]
            first_mod = tables[0][kinds]
            entry_rows = (row_norm(x_in) * (1.0 + first_mod[:, 1]) + first_mod[:, 0]).astype(jnp.bfloat16)
            qkv = blocked_dot(entry_rows, w_qkv[layer], N_NARROW).reshape(R, H, 3, HD)
            angles = rotary_angles(positions[:, patch_index], HD)
            queries = rotate(head_norm(qkv[:, :, 0], norms[0], norms[1]), angles).astype(jnp.bfloat16)
            fresh_keys = rotate(head_norm(qkv[:, :, 1], norms[2], norms[3]), angles).astype(jnp.bfloat16)
            fresh_values = qkv[:, :, 2].astype(jnp.bfloat16)
            cache_now = cache_now.at[patch_index].set(jnp.concatenate([fresh_keys, fresh_values], axis=-1))
            attended = attend(queries, kinds, cache_now, row_kind)
            projected = blocked_dot(attended, w_out[layer], N_WIDE)
            after_attn = x_in + first_mod[:, 2] * projected
            second_mod = tables[1][kinds]
            entry_second = (row_norm(after_attn) * (1.0 + second_mod[:, 1]) + second_mod[:, 0]).astype(jnp.bfloat16)
            up_sum = blocked_dot(entry_second, w_up[layer], N_NARROW)
            hidden_act = jax.nn.gelu(up_sum, approximate=True).astype(jnp.bfloat16)
            down_sum = blocked_dot(hidden_act, w_down[layer], N_WIDE)
            layer_outs.append((after_attn + second_mod[:, 2] * down_sum).astype(jnp.bfloat16))
        previous = layer_outs
        all_outputs.append(jnp.stack(layer_outs))
        all_caches.append(cache_now)
    return (jnp.stack(all_outputs), jnp.stack(all_caches))
```

```python
import functools

import jax
import jax.numpy as jnp
from jax import lax
from jax.experimental import pallas as pl
from jax.experimental.pallas import tpu as pltpu
from jax.sharding import PartitionSpec as P

EPS_ROW = 1e-05
EPS_HEAD = 1e-06
FAR = -1e30
LOG2E = 1.4426950408889634
BF = jnp.bfloat16
F32 = jnp.float32


def time_features(timesteps, feature_count):
    half_count = feature_count // 2
    frequency = jnp.exp(-jnp.log(10000.0) * jnp.arange(half_count, dtype=F32) / half_count)
    angle = timesteps.astype(F32)[:, None] * frequency[None, :]
    return jnp.concatenate([jnp.cos(angle), jnp.sin(angle)], axis=1)


def rotary_tables(row_positions, head_dim):
    dim_frame = head_dim // 4
    dim_plane = head_dim // 8 * 3
    pieces = []
    for axis_pos, span_dims in ((0, dim_frame), (1, dim_plane), (2, dim_plane)):
        frequency = 10000.0 ** (-jnp.arange(0, span_dims, 2, dtype=F32) / span_dims)
        pieces.append(row_positions[axis_pos].astype(F32)[:, None] * jnp.repeat(frequency, 2)[None, :])
    angles = jnp.concatenate(pieces, axis=1)
    sign = jnp.where(jnp.arange(head_dim) % 2 == 0, -1.0, 1.0).astype(F32)
    cosine = jnp.cos(angles)
    sine = jnp.sin(angles) * sign[None, :]
    return jnp.concatenate([cosine, cosine], axis=1), jnp.concatenate([sine, sine], axis=1)


def prepare_kernel(heads, head_dim, qkv_ref, cos_ref, sin_ref, kind_ref, norm_ref, q_ref, pair_ref):
    pair = 2 * head_dim
    rows = qkv_ref.shape[0]
    lane = lax.broadcasted_iota(jnp.int32, (rows, pair), 1)
    first = lane < head_dim
    even = lane % 2 == 0
    request = kind_ref[...] // 2
    mask_part = jnp.where(lane == head_dim + request, 1.0, 0.0)
    cosine = cos_ref[...]
    sine = sin_ref[...]
    gain = norm_ref[0:1, :]
    bias = norm_ref[1:2, :]
    for h in range(heads):
        base = 3 * head_dim * h
        both = qkv_ref[:, base : base + pair].astype(F32)
        key_value = qkv_ref[:, base + head_dim : base + head_dim + pair].astype(F32)
        mean_q = jnp.sum(jnp.where(first, both, 0.0), axis=1, keepdims=True) / head_dim
        mean_k = jnp.sum(jnp.where(first, 0.0, both), axis=1, keepdims=True) / head_dim
        center = both - jnp.where(first, mean_q, mean_k)
        square = center * center
        var_q = jnp.sum(jnp.where(first, square, 0.0), axis=1, keepdims=True) / head_dim
        var_k = jnp.sum(jnp.where(first, 0.0, square), axis=1, keepdims=True) / head_dim
        scale = jnp.where(first, lax.rsqrt(var_q + EPS_HEAD), lax.rsqrt(var_k + EPS_HEAD))
        normed = center * scale * gain + bias
        swapped = jnp.where(even, pltpu.roll(normed, pair - 1, 1), pltpu.roll(normed, 1, 1))
        turned = normed * cosine + swapped * sine
        q_ref[h] = jnp.where(first, turned, mask_part).astype(BF)
        pair_ref[h] = jnp.where(first, pltpu.roll(turned, head_dim, 1), key_value).astype(BF)


def prepare(qkv, cosine, sine, kinds, norm_rows, heads, head_dim):
    rows, width = qkv.shape
    block = min(256, rows)
    pair = 2 * head_dim
    return pl.pallas_call(
        functools.partial(prepare_kernel, heads, head_dim),
        grid=(rows // block,),
        in_specs=[
            pl.BlockSpec((block, width), lambda i: (i, 0)),
            pl.BlockSpec((block, pair), lambda i: (i, 0)),
            pl.BlockSpec((block, pair), lambda i: (i, 0)),
            pl.BlockSpec((block, 1), lambda i: (i, 0)),
            pl.BlockSpec((2, pair), lambda i: (0, 0)),
        ],
        out_specs=[
            pl.BlockSpec((heads, block, pair), lambda i: (0, i, 0)),
            pl.BlockSpec((heads, block, pair), lambda i: (0, i, 0)),
        ],
        out_shape=[
            jax.ShapeDtypeStruct((heads, rows, pair), BF),
            jax.ShapeDtypeStruct((heads, rows, pair), BF),
        ],
        compiler_params=pltpu.CompilerParams(vmem_limit_bytes=48 * 1024 * 1024),
        name="prepare",
    )(qkv, cosine, sine, kinds[:, None], norm_rows)


def attend_kernel(heads, head_dim, q_ref, own_ref, other_ref, own_mask_ref, other_mask_ref, out_ref):
    pair = 2 * head_dim
    keys_count = own_ref.shape[1]
    lane = lax.broadcasted_iota(jnp.int32, (keys_count, pair), 1)
    first = lane < head_dim
    one = jnp.where(lane == 0, 1.0, 0.0).astype(BF)
    factor = LOG2E * head_dim ** (-0.5)
    pieces = []
    for h in range(heads):
        queries = q_ref[h]
        own = own_ref[h]
        other = other_ref[h]
        contract = (((1,), (1,)), ((), ()))
        scores_a = lax.dot_general(
            queries, jnp.where(first, own, own_mask_ref[...]), contract, preferred_element_type=F32
        )
        scores_b = lax.dot_general(
            queries, jnp.where(first, other, other_mask_ref[...]), contract, preferred_element_type=F32
        )
        top = jnp.maximum(
            jnp.max(scores_a, axis=1, keepdims=True), jnp.max(scores_b, axis=1, keepdims=True)
        )
        weights_a = jnp.exp2((scores_a - top) * factor).astype(BF)
        weights_b = jnp.exp2((scores_b - top) * factor).astype(BF)
        mixed = jnp.dot(weights_a, jnp.where(first, one, own), preferred_element_type=F32)
        mixed += jnp.dot(weights_b, jnp.where(first, one, other), preferred_element_type=F32)
        pieces.append(mixed[:, head_dim:] / mixed[:, 0:1])
    out_ref[...] = jnp.concatenate(pieces, axis=1).astype(BF)


def attend(queries, own, other, own_mask, other_mask, head_dim):
    heads, rows, pair = queries.shape
    keys_count = own.shape[1]
    block = min(256, rows)
    whole = pl.BlockSpec((heads, keys_count, pair), lambda i: (0, 0, 0))
    mask = pl.BlockSpec((keys_count, pair), lambda i: (0, 0))
    return pl.pallas_call(
        functools.partial(attend_kernel, heads, head_dim),
        grid=(rows // block,),
        in_specs=[pl.BlockSpec((heads, block, pair), lambda i: (0, i, 0)), whole, whole, mask, mask],
        out_specs=pl.BlockSpec((block, heads * head_dim), lambda i: (i, 0)),
        out_shape=jax.ShapeDtypeStruct((rows, heads * head_dim), BF),
        compiler_params=pltpu.CompilerParams(vmem_limit_bytes=48 * 1024 * 1024),
        name="attend",
    )(queries, own, other, own_mask, other_mask)


def key_mask(kinds, head_dim):
    lane = jnp.arange(2 * head_dim)[None, :]
    foreign = (lane >= head_dim) & (lane < head_dim + 2) & (lane - head_dim != (kinds // 2)[:, None])
    return jnp.where(foreign, FAR, 0.0).astype(BF)


def pick(table, kinds, part):
    column = kinds[:, None]
    low = jnp.where(column == 0, table[0, part][None], table[1, part][None])
    high = jnp.where(column == 2, table[2, part][None], table[3, part][None])
    return jnp.where(column < 2, low, high)


def exchange(blocks, axis):
    n = lax.axis_size(axis)
    me = lax.axis_index(axis)
    got = jnp.zeros_like(blocks)
    got = lax.dynamic_update_slice_in_dim(
        got, lax.dynamic_slice_in_dim(blocks, me, 1, 0), me, 0
    )
    for step in range(1, n):
        there = (me + step) % n
        back = (me + n - step) % n
        block = lax.dynamic_slice_in_dim(blocks, there, 1, 0)
        block = lax.ppermute(block, axis, [(i, (i + step) % n) for i in range(n)])
        got = lax.dynamic_update_slice_in_dim(got, block, back, 0)
    return got


def per_device(
    hidden_in,
    row_kind,
    positions,
    timesteps,
    stale_cache,
    w_qkv,
    qk_norm,
    w_out,
    ada_weight,
    w_up,
    w_down,
):
    n_wide = lax.axis_size("wide")
    n_narrow = lax.axis_size("narrow")
    wide_idx = lax.axis_index("wide")
    narrow_idx = lax.axis_index("narrow")
    section = lax.axis_index("section")
    patch_count, rows_a, feat_a = hidden_in.shape
    total_rows = rows_a * n_wide
    rows_b = total_rows // n_narrow
    heads_local = stale_cache.shape[3]
    pair = stale_cache.shape[4]
    head_dim = pair // 2
    model_width = feat_a * n_narrow
    by_heads = heads_local % n_narrow == 0
    heads = heads_local // n_narrow if by_heads else heads_local
    lead = section == 0

    def swap(value):
        return lax.ppermute(value, "section", [(0, 1), (1, 0)])

    def both_layers(own):
        other = swap(own)
        return (jnp.where(lead, own, other), jnp.where(lead, other, own))

    qkv_weights = both_layers(w_qkv[0])
    out_weights = both_layers(w_out[0])
    up_weights = both_layers(w_up[0])
    down_weights = both_layers(w_down[0])
    norm_rows = both_layers(qk_norm[0])

    activated = jax.nn.silu(time_features(timesteps, ada_weight.shape[2])).astype(BF)
    modulation = jnp.einsum("re,kesd->krsd", activated, ada_weight[0], preferred_element_type=F32)
    tables = both_layers(modulation.reshape(2, 4, 3, feat_a))

    kinds = lax.dynamic_slice_in_dim(row_kind, section, 1, 0)[0]
    kinds_other = lax.dynamic_slice_in_dim(row_kind, 1 - section, 1, 0)[0]
    own_mask = key_mask(kinds, head_dim)
    other_mask = key_mask(kinds_other, head_dim)
    kinds_a = lax.dynamic_slice_in_dim(kinds, wide_idx * rows_a, rows_a)
    places = lax.dynamic_slice_in_dim(positions, section, 1, 1)[:, 0]
    kinds_q = kinds
    if not by_heads:
        places = lax.dynamic_slice_in_dim(places, narrow_idx * rows_b, rows_b, 1)
        kinds_q = lax.dynamic_slice_in_dim(kinds, narrow_idx * rows_b, rows_b)
    cosine, sine = rotary_tables(places, head_dim)

    def to_heads(rows_part):
        if by_heads:
            blocks = rows_part.reshape(rows_b, n_narrow, heads, pair).transpose(1, 2, 0, 3)
            return exchange(blocks, "narrow").transpose(1, 0, 2, 3).reshape(heads, total_rows, pair)
        return lax.all_gather(rows_part.transpose(1, 0, 2), "narrow", axis=1, tiled=True)

    def to_rows(pairs):
        if by_heads:
            blocks = pairs.reshape(heads, n_narrow, rows_b, pair).transpose(1, 0, 2, 3)
            return exchange(blocks, "narrow").transpose(2, 0, 1, 3).reshape(rows_b, heads_local, pair)
        return pairs.transpose(1, 0, 2)

    stale = to_heads(stale_cache[0, 1])

    def normalize(values):
        moments = lax.psum(
            jnp.stack([jnp.sum(values, axis=1), jnp.sum(values * values, axis=1)]), "narrow"
        )
        row_mean = moments[0] / model_width
        variance = moments[1] / model_width - row_mean * row_mean
        return (values - row_mean[:, None]) * lax.rsqrt(variance + EPS_ROW)[:, None]

    layer_in = lax.dynamic_slice_in_dim(hidden_in, section, 1, 0)[0]
    results = []
    caches = []
    for layer in range(2):
        table = tables[layer]
        x_in = layer_in.astype(F32)
        entry = normalize(x_in) * (1.0 + pick(table[0], kinds_a, 1)) + pick(table[0], kinds_a, 0)
        qkv_terms = jnp.dot(
            lax.all_gather(entry.astype(BF), "wide", axis=0, tiled=True),
            qkv_weights[layer],
            preferred_element_type=F32,
        ).astype(BF)
        qkv = lax.psum_scatter(
            qkv_terms, "narrow", scatter_dimension=1 if by_heads else 0, tiled=True
        )
        norms = norm_rows[layer]
        norm_pair = jnp.stack(
            [jnp.concatenate([norms[0], norms[2]]), jnp.concatenate([norms[1], norms[3]])]
        )
        queries, fresh = prepare(qkv, cosine, sine, kinds_q, norm_pair, heads, head_dim)
        caches.append(to_rows(fresh))
        if not by_heads:
            fresh = lax.all_gather(fresh, "narrow", axis=1, tiled=True)
        if layer == 0:
            other = jnp.where(lead, stale, swap(fresh))
        else:
            other = swap(jnp.where(lead, fresh, stale))
        attended = attend(queries, fresh, other, own_mask, other_mask, head_dim)
        attended = lax.all_gather(attended, "narrow", axis=1 if by_heads else 0, tiled=True)
        proj_terms = jnp.dot(attended, out_weights[layer], preferred_element_type=F32).astype(BF)
        projected = lax.psum_scatter(proj_terms, "wide", scatter_dimension=0, tiled=True)
        after = x_in + pick(table[0], kinds_a, 2) * projected.astype(F32)
        entry = normalize(after) * (1.0 + pick(table[1], kinds_a, 1)) + pick(table[1], kinds_a, 0)
        up_terms = jnp.dot(
            lax.all_gather(entry.astype(BF), "wide", axis=0, tiled=True),
            up_weights[layer],
            preferred_element_type=F32,
        ).astype(BF)
        up_sum = lax.psum_scatter(up_terms, "narrow", scatter_dimension=0, tiled=True)
        inner = jax.nn.gelu(up_sum.astype(F32), approximate=True).astype(BF)
        down_terms = jnp.dot(
            lax.all_gather(inner, "narrow", axis=0, tiled=True),
            down_weights[layer],
            preferred_element_type=F32,
        ).astype(BF)
        down_sum = lax.psum_scatter(down_terms, "wide", scatter_dimension=0, tiled=True)
        layer_in = (after + pick(table[1], kinds_a, 2) * down_sum.astype(F32)).astype(BF)
        results.append(layer_in)

    def by_layer(parts):
        got = swap(jnp.where(lead, parts[1], parts[0]))
        kept = jnp.where(lead, parts[0], parts[1])
        return jnp.stack([jnp.where(lead, kept, got), jnp.where(lead, got, kept)])[None]

    return (by_layer(results), by_layer(caches))


def solution(mesh):
    in_specs = (
        P(None, "wide", "narrow"),
        P(),
        P(),
        P(),
        P("section", None, "narrow", "wide", None),
        P("section", "narrow", "wide"),
        P("section", None, None),
        P("section", "wide", "narrow"),
        P("section", None, None, None, "narrow"),
        P("section", "narrow", "wide"),
        P("section", "wide", "narrow"),
    )
    out_specs = (P("section", None, "wide", "narrow"), P("section", None, "narrow", "wide", None))
    return jax.shard_map(
        per_device, mesh=mesh, in_specs=in_specs, out_specs=out_specs, check_vma=False
    )
```

```python
import functools

import jax
import jax.numpy as jnp
from jax import lax
from jax.experimental import pallas as pl
from jax.experimental.pallas import tpu as pltpu
from jax.sharding import PartitionSpec as P

EPS_ROW = 1e-05
EPS_HEAD = 1e-06
FAR = -1e30
LOG2E = 1.4426950408889634
BF = jnp.bfloat16
F32 = jnp.float32


def time_features(timesteps, feature_count):
    half_count = feature_count // 2
    frequency = jnp.exp(-jnp.log(10000.0) * jnp.arange(half_count, dtype=F32) / half_count)
    angle = timesteps.astype(F32)[:, None] * frequency[None, :]
    return jnp.concatenate([jnp.cos(angle), jnp.sin(angle)], axis=1)


def rotary_tables(row_positions, head_dim):
    dim_frame = head_dim // 4
    dim_plane = head_dim // 8 * 3
    pieces = []
    for axis_pos, span_dims in ((0, dim_frame), (1, dim_plane), (2, dim_plane)):
        frequency = 10000.0 ** (-jnp.arange(0, span_dims, 2, dtype=F32) / span_dims)
        pieces.append(row_positions[axis_pos].astype(F32)[:, None] * jnp.repeat(frequency, 2)[None, :])
    angles = jnp.concatenate(pieces, axis=1)
    sign = jnp.where(jnp.arange(head_dim) % 2 == 0, -1.0, 1.0).astype(F32)
    cosine = jnp.cos(angles)
    sine = jnp.sin(angles) * sign[None, :]
    return jnp.concatenate([cosine, cosine], axis=1), jnp.concatenate([sine, sine], axis=1)


def prepare_kernel(heads, head_dim, qkv_ref, cos_ref, sin_ref, kind_ref, norm_ref, q_ref, pair_ref):
    pair = 2 * head_dim
    rows = qkv_ref.shape[0]
    lane = lax.broadcasted_iota(jnp.int32, (rows, pair), 1)
    first = lane < head_dim
    even = lane % 2 == 0
    request = kind_ref[...] // 2
    mask_part = jnp.where(lane == head_dim + request, 1.0, 0.0)
    cosine = cos_ref[...]
    sine = sin_ref[...]
    gain = norm_ref[0:1, :]
    bias = norm_ref[1:2, :]
    for h in range(heads):
        base = 3 * head_dim * h
        both = qkv_ref[:, base : base + pair].astype(F32)
        key_value = qkv_ref[:, base + head_dim : base + head_dim + pair].astype(F32)
        mean_q = jnp.sum(jnp.where(first, both, 0.0), axis=1, keepdims=True) / head_dim
        mean_k = jnp.sum(jnp.where(first, 0.0, both), axis=1, keepdims=True) / head_dim
        center = both - jnp.where(first, mean_q, mean_k)
        square = center * center
        var_q = jnp.sum(jnp.where(first, square, 0.0), axis=1, keepdims=True) / head_dim
        var_k = jnp.sum(jnp.where(first, 0.0, square), axis=1, keepdims=True) / head_dim
        scale = jnp.where(first, lax.rsqrt(var_q + EPS_HEAD), lax.rsqrt(var_k + EPS_HEAD))
        normed = center * scale * gain + bias
        swapped = jnp.where(even, pltpu.roll(normed, pair - 1, 1), pltpu.roll(normed, 1, 1))
        turned = normed * cosine + swapped * sine
        q_ref[h] = jnp.where(first, turned, mask_part).astype(BF)
        pair_ref[h] = jnp.where(first, pltpu.roll(turned, head_dim, 1), key_value).astype(BF)


def prepare(qkv, cosine, sine, kinds, norm_rows, heads, head_dim):
    rows, width = qkv.shape
    block = min(256, rows)
    pair = 2 * head_dim
    return pl.pallas_call(
        functools.partial(prepare_kernel, heads, head_dim),
        grid=(rows // block,),
        in_specs=[
            pl.BlockSpec((block, width), lambda i: (i, 0)),
            pl.BlockSpec((block, pair), lambda i: (i, 0)),
            pl.BlockSpec((block, pair), lambda i: (i, 0)),
            pl.BlockSpec((block, 1), lambda i: (i, 0)),
            pl.BlockSpec((2, pair), lambda i: (0, 0)),
        ],
        out_specs=[
            pl.BlockSpec((heads, block, pair), lambda i: (0, i, 0)),
            pl.BlockSpec((heads, block, pair), lambda i: (0, i, 0)),
        ],
        out_shape=[
            jax.ShapeDtypeStruct((heads, rows, pair), BF),
            jax.ShapeDtypeStruct((heads, rows, pair), BF),
        ],
        compiler_params=pltpu.CompilerParams(vmem_limit_bytes=48 * 1024 * 1024),
        name="prepare",
    )(qkv, cosine, sine, kinds[:, None], norm_rows)


def attend_kernel(heads, head_dim, q_ref, own_ref, other_ref, own_mask_ref, other_mask_ref, out_ref):
    pair = 2 * head_dim
    keys_count = own_ref.shape[1]
    lane = lax.broadcasted_iota(jnp.int32, (keys_count, pair), 1)
    first = lane < head_dim
    one = jnp.where(lane == 0, 1.0, 0.0).astype(BF)
    factor = LOG2E * head_dim ** (-0.5)
    pieces = []
    for h in range(heads):
        queries = q_ref[h]
        own = own_ref[h]
        other = other_ref[h]
        contract = (((1,), (1,)), ((), ()))
        scores_a = lax.dot_general(
            queries, jnp.where(first, own, own_mask_ref[...]), contract, preferred_element_type=F32
        )
        scores_b = lax.dot_general(
            queries, jnp.where(first, other, other_mask_ref[...]), contract, preferred_element_type=F32
        )
        top = jnp.maximum(
            jnp.max(scores_a, axis=1, keepdims=True), jnp.max(scores_b, axis=1, keepdims=True)
        )
        weights_a = jnp.exp2((scores_a - top) * factor).astype(BF)
        weights_b = jnp.exp2((scores_b - top) * factor).astype(BF)
        mixed = jnp.dot(weights_a, jnp.where(first, one, own), preferred_element_type=F32)
        mixed += jnp.dot(weights_b, jnp.where(first, one, other), preferred_element_type=F32)
        pieces.append(mixed[:, head_dim:] / mixed[:, 0:1])
    out_ref[...] = jnp.concatenate(pieces, axis=1).astype(BF)


def attend(queries, own, other, own_mask, other_mask, head_dim):
    heads, rows, pair = queries.shape
    keys_count = own.shape[1]
    block = min(256, rows)
    whole = pl.BlockSpec((heads, keys_count, pair), lambda i: (0, 0, 0))
    mask = pl.BlockSpec((keys_count, pair), lambda i: (0, 0))
    return pl.pallas_call(
        functools.partial(attend_kernel, heads, head_dim),
        grid=(rows // block,),
        in_specs=[pl.BlockSpec((heads, block, pair), lambda i: (0, i, 0)), whole, whole, mask, mask],
        out_specs=pl.BlockSpec((block, heads * head_dim), lambda i: (i, 0)),
        out_shape=jax.ShapeDtypeStruct((rows, heads * head_dim), BF),
        compiler_params=pltpu.CompilerParams(vmem_limit_bytes=48 * 1024 * 1024),
        name="attend",
    )(queries, own, other, own_mask, other_mask)


def key_mask(kinds, head_dim):
    lane = jnp.arange(2 * head_dim)[None, :]
    foreign = (lane >= head_dim) & (lane < head_dim + 2) & (lane - head_dim != (kinds // 2)[:, None])
    return jnp.where(foreign, FAR, 0.0).astype(BF)


def pick(table, kinds, part):
    column = kinds[:, None]
    low = jnp.where(column == 0, table[0, part][None], table[1, part][None])
    high = jnp.where(column == 2, table[2, part][None], table[3, part][None])
    return jnp.where(column < 2, low, high)


def exchange(blocks, axis):
    n = lax.axis_size(axis)
    me = lax.axis_index(axis)
    got = jnp.zeros_like(blocks)
    got = lax.dynamic_update_slice_in_dim(
        got, lax.dynamic_slice_in_dim(blocks, me, 1, 0), me, 0
    )
    for step in range(1, n):
        there = (me + step) % n
        back = (me + n - step) % n
        block = lax.dynamic_slice_in_dim(blocks, there, 1, 0)
        block = lax.ppermute(block, axis, [(i, (i + step) % n) for i in range(n)])
        got = lax.dynamic_update_slice_in_dim(got, block, back, 0)
    return got


def per_device(
    hidden_in,
    row_kind,
    positions,
    timesteps,
    stale_cache,
    w_qkv,
    qk_norm,
    w_out,
    ada_weight,
    w_up,
    w_down,
):
    operands = (
        hidden_in,
        row_kind,
        positions,
        timesteps,
        stale_cache,
        w_qkv[0],
        qk_norm[0],
        w_out[0],
        ada_weight[0],
        w_up[0],
        w_down[0],
    )
    if stale_cache.shape[3] % lax.axis_size("narrow") == 0:
        return features_whole(*operands)
    return features_split(*operands)


def swap(value):
    return lax.ppermute(value, "section", [(0, 1), (1, 0)])


def by_layer(parts, lead):
    got = swap(jnp.where(lead, parts[1], parts[0]))
    kept = jnp.where(lead, parts[0], parts[1])
    return jnp.stack([jnp.where(lead, kept, got), jnp.where(lead, got, kept)])[None]


def norm_pairs(norms):
    return jnp.stack([jnp.concatenate([norms[0], norms[2]]), jnp.concatenate([norms[1], norms[3]])])


def modulate(values, table, kinds):
    return (values * (1.0 + pick(table, kinds, 1)) + pick(table, kinds, 0)).astype(BF)


def row_norm(values):
    center = values - jnp.mean(values, axis=1, keepdims=True)
    variance = jnp.mean(center * center, axis=1, keepdims=True)
    return center * lax.rsqrt(variance + EPS_ROW)


def features_whole(
    hidden_in,
    row_kind,
    positions,
    timesteps,
    stale_cache,
    w_qkv,
    qk_norm,
    w_out,
    ada_weight,
    w_up,
    w_down,
):
    n_wide = lax.axis_size("wide")
    n_narrow = lax.axis_size("narrow")
    wide_idx = lax.axis_index("wide")
    narrow_idx = lax.axis_index("narrow")
    section = lax.axis_index("section")
    lead = section == 0
    _, rows_a, feat_a = hidden_in.shape
    total_rows = rows_a * n_wide
    rows_b = total_rows // n_narrow
    rows_c = rows_a // n_narrow
    heads_local = stale_cache.shape[3]
    heads = heads_local // n_narrow
    pair = stale_cache.shape[4]
    head_dim = pair // 2
    model_width = feat_a * n_narrow
    both = ("wide", "narrow")

    def weights_for(own, axis):
        parts = jnp.stack(jnp.split(own, n_narrow, axis))
        got = exchange(parts, "narrow")
        joined = jnp.concatenate([got[i] for i in range(n_narrow)], axis=1 - axis)
        other = swap(joined)
        return (jnp.where(lead, joined, other), jnp.where(lead, other, joined))

    def to_rows_c(block):
        got = exchange(block.reshape(n_narrow, rows_c, feat_a), "narrow")
        return got.transpose(1, 0, 2).reshape(rows_c, model_width)

    def from_rows_c(block):
        got = exchange(block.reshape(rows_c, n_narrow, feat_a).transpose(1, 0, 2), "narrow")
        return got.reshape(rows_a, feat_a)

    activated = jax.nn.silu(time_features(timesteps, ada_weight.shape[1])).astype(BF)
    modulation = jnp.einsum("re,kesd->krsd", activated, ada_weight, preferred_element_type=F32)
    modulation = lax.all_gather(modulation.reshape(2, 4, 3, feat_a), ("section", "narrow"), axis=0)
    tables = modulation.reshape(2, n_narrow, 2, 4, 3, feat_a).transpose(0, 2, 3, 4, 1, 5)
    tables = tables.reshape(2, 2, 4, 3, model_width)

    qkv_weights = weights_for(w_qkv, 1)
    out_weights = weights_for(w_out, 0)
    up_weights = weights_for(w_up, 1)
    down_weights = weights_for(w_down, 0)
    own_norms = qk_norm
    other_norms = swap(qk_norm)
    norm_rows = (jnp.where(lead, own_norms, other_norms), jnp.where(lead, other_norms, own_norms))

    kinds = lax.dynamic_slice_in_dim(row_kind, section, 1, 0)[0]
    kinds_other = lax.dynamic_slice_in_dim(row_kind, 1 - section, 1, 0)[0]
    own_mask = key_mask(kinds, head_dim)
    other_mask = key_mask(kinds_other, head_dim)
    kinds_c = lax.dynamic_slice_in_dim(kinds, wide_idx * rows_a + narrow_idx * rows_c, rows_c)
    places = lax.dynamic_slice_in_dim(positions, section, 1, 1)[:, 0]
    cosine, sine = rotary_tables(places, head_dim)

    blocks = stale_cache[0, 1].reshape(rows_b, n_narrow, heads, pair).transpose(1, 2, 0, 3)
    stale = exchange(blocks, "narrow").transpose(1, 0, 2, 3).reshape(heads, total_rows, pair)

    layer_in = to_rows_c(lax.dynamic_slice_in_dim(hidden_in, section, 1, 0)[0])
    results = []
    caches = []
    for layer in range(2):
        table = tables[layer]
        x_in = layer_in.astype(F32)
        entry = modulate(row_norm(x_in), table[0], kinds_c)
        entry = lax.all_gather(entry, both, axis=0, tiled=True)
        qkv = jnp.dot(entry, qkv_weights[layer], preferred_element_type=F32).astype(BF)
        queries, fresh = prepare(
            qkv, cosine, sine, kinds, norm_pairs(norm_rows[layer]), heads, head_dim
        )
        blocks = fresh.reshape(heads, n_narrow, rows_b, pair).transpose(1, 0, 2, 3)
        blocks = exchange(blocks, "narrow").transpose(2, 0, 1, 3)
        caches.append(blocks.reshape(rows_b, heads_local, pair))
        if layer == 0:
            other = jnp.where(lead, stale, swap(fresh))
        else:
            other = swap(jnp.where(lead, fresh, stale))
        attended = attend(queries, fresh, other, own_mask, other_mask, head_dim)
        terms = jnp.dot(attended, out_weights[layer], preferred_element_type=F32).astype(BF)
        projected = lax.psum_scatter(terms, both, scatter_dimension=0, tiled=True)
        after = x_in + pick(table[0], kinds_c, 2) * projected.astype(F32)
        entry = modulate(row_norm(after), table[1], kinds_c)
        entry = lax.all_gather(entry, both, axis=0, tiled=True)
        up = jnp.dot(entry, up_weights[layer], preferred_element_type=F32)
        inner = jax.nn.gelu(up, approximate=True).astype(BF)
        terms = jnp.dot(inner, down_weights[layer], preferred_element_type=F32).astype(BF)
        down = lax.psum_scatter(terms, both, scatter_dimension=0, tiled=True)
        layer_in = (after + pick(table[1], kinds_c, 2) * down.astype(F32)).astype(BF)
        results.append(from_rows_c(layer_in))
    return (by_layer(results, lead), by_layer(caches, lead))


def features_split(
    hidden_in,
    row_kind,
    positions,
    timesteps,
    stale_cache,
    w_qkv,
    qk_norm,
    w_out,
    ada_weight,
    w_up,
    w_down,
):
    n_wide = lax.axis_size("wide")
    n_narrow = lax.axis_size("narrow")
    wide_idx = lax.axis_index("wide")
    narrow_idx = lax.axis_index("narrow")
    section = lax.axis_index("section")
    patch_count, rows_a, feat_a = hidden_in.shape
    total_rows = rows_a * n_wide
    rows_b = total_rows // n_narrow
    heads_local = stale_cache.shape[3]
    pair = stale_cache.shape[4]
    head_dim = pair // 2
    model_width = feat_a * n_narrow
    heads = heads_local
    lead = section == 0

    def both_layers(own):
        other = swap(own)
        return (jnp.where(lead, own, other), jnp.where(lead, other, own))

    qkv_weights = both_layers(w_qkv)
    out_weights = both_layers(w_out)
    up_weights = both_layers(w_up)
    down_weights = both_layers(w_down)
    norm_rows = both_layers(qk_norm)

    activated = jax.nn.silu(time_features(timesteps, ada_weight.shape[1])).astype(BF)
    modulation = jnp.einsum("re,kesd->krsd", activated, ada_weight, preferred_element_type=F32)
    tables = both_layers(modulation.reshape(2, 4, 3, feat_a))

    kinds = lax.dynamic_slice_in_dim(row_kind, section, 1, 0)[0]
    kinds_other = lax.dynamic_slice_in_dim(row_kind, 1 - section, 1, 0)[0]
    own_mask = key_mask(kinds, head_dim)
    other_mask = key_mask(kinds_other, head_dim)
    kinds_a = lax.dynamic_slice_in_dim(kinds, wide_idx * rows_a, rows_a)
    places = lax.dynamic_slice_in_dim(positions, section, 1, 1)[:, 0]
    places = lax.dynamic_slice_in_dim(places, narrow_idx * rows_b, rows_b, 1)
    kinds_q = lax.dynamic_slice_in_dim(kinds, narrow_idx * rows_b, rows_b)
    cosine, sine = rotary_tables(places, head_dim)

    stale = lax.all_gather(stale_cache[0, 1].transpose(1, 0, 2), "narrow", axis=1, tiled=True)

    def normalize(values):
        moments = lax.psum(
            jnp.stack([jnp.sum(values, axis=1), jnp.sum(values * values, axis=1)]), "narrow"
        )
        row_mean = moments[0] / model_width
        variance = moments[1] / model_width - row_mean * row_mean
        return (values - row_mean[:, None]) * lax.rsqrt(variance + EPS_ROW)[:, None]

    layer_in = lax.dynamic_slice_in_dim(hidden_in, section, 1, 0)[0]
    results = []
    caches = []
    for layer in range(2):
        table = tables[layer]
        x_in = layer_in.astype(F32)
        entry = modulate(normalize(x_in), table[0], kinds_a)
        qkv_terms = jnp.dot(
            lax.all_gather(entry, "wide", axis=0, tiled=True),
            qkv_weights[layer],
            preferred_element_type=F32,
        ).astype(BF)
        qkv = lax.psum_scatter(qkv_terms, "narrow", scatter_dimension=0, tiled=True)
        queries, fresh = prepare(
            qkv, cosine, sine, kinds_q, norm_pairs(norm_rows[layer]), heads, head_dim
        )
        caches.append(fresh.transpose(1, 0, 2))
        fresh = lax.all_gather(fresh, "narrow", axis=1, tiled=True)
        if layer == 0:
            other = jnp.where(lead, stale, swap(fresh))
        else:
            other = swap(jnp.where(lead, fresh, stale))
        attended = attend(queries, fresh, other, own_mask, other_mask, head_dim)
        attended = lax.all_gather(attended, "narrow", axis=0, tiled=True)
        proj_terms = jnp.dot(attended, out_weights[layer], preferred_element_type=F32).astype(BF)
        projected = lax.psum_scatter(proj_terms, "wide", scatter_dimension=0, tiled=True)
        after = x_in + pick(table[0], kinds_a, 2) * projected.astype(F32)
        entry = modulate(normalize(after), table[1], kinds_a)
        up_terms = jnp.dot(
            lax.all_gather(entry, "wide", axis=0, tiled=True),
            up_weights[layer],
            preferred_element_type=F32,
        ).astype(BF)
        up_sum = lax.psum_scatter(up_terms, "narrow", scatter_dimension=0, tiled=True)
        inner = jax.nn.gelu(up_sum.astype(F32), approximate=True).astype(BF)
        down_terms = jnp.dot(
            lax.all_gather(inner, "narrow", axis=0, tiled=True),
            down_weights[layer],
            preferred_element_type=F32,
        ).astype(BF)
        down_sum = lax.psum_scatter(down_terms, "wide", scatter_dimension=0, tiled=True)
        layer_in = (after + pick(table[1], kinds_a, 2) * down_sum.astype(F32)).astype(BF)
        results.append(layer_in)

    return (by_layer(results, lead), by_layer(caches, lead))


def solution(mesh):
    in_specs = (
        P(None, "wide", "narrow"),
        P(),
        P(),
        P(),
        P("section", None, "narrow", "wide", None),
        P("section", "narrow", "wide"),
        P("section", None, None),
        P("section", "wide", "narrow"),
        P("section", None, None, None, "narrow"),
        P("section", "narrow", "wide"),
        P("section", "wide", "narrow"),
    )
    out_specs = (P("section", None, "wide", "narrow"), P("section", None, "narrow", "wide", None))
    return jax.shard_map(
        per_device, mesh=mesh, in_specs=in_specs, out_specs=out_specs, check_vma=False
    )
```

```python
import functools

import jax
import jax.numpy as jnp
from jax import lax
from jax.experimental import pallas as pl
from jax.experimental.pallas import tpu as pltpu
from jax.sharding import PartitionSpec as P

EPS_ROW = 1e-05
EPS_HEAD = 1e-06
FAR = -1e30
LOG2E = 1.4426950408889634
BF = jnp.bfloat16
F32 = jnp.float32


def time_features(timesteps, feature_count):
    half_count = feature_count // 2
    frequency = jnp.exp(-jnp.log(10000.0) * jnp.arange(half_count, dtype=F32) / half_count)
    angle = timesteps.astype(F32)[:, None] * frequency[None, :]
    return jnp.concatenate([jnp.cos(angle), jnp.sin(angle)], axis=1)


def rotary_tables(row_positions, head_dim):
    dim_frame = head_dim // 4
    dim_plane = head_dim // 8 * 3
    pieces = []
    for axis_pos, span_dims in ((0, dim_frame), (1, dim_plane), (2, dim_plane)):
        frequency = 10000.0 ** (-jnp.arange(0, span_dims, 2, dtype=F32) / span_dims)
        pieces.append(row_positions[axis_pos].astype(F32)[:, None] * jnp.repeat(frequency, 2)[None, :])
    angles = jnp.concatenate(pieces, axis=1)
    sign = jnp.where(jnp.arange(head_dim) % 2 == 0, -1.0, 1.0).astype(F32)
    cosine = jnp.cos(angles)
    sine = jnp.sin(angles) * sign[None, :]
    return jnp.concatenate([cosine, cosine], axis=1), jnp.concatenate([sine, sine], axis=1)


def prepare_kernel(heads, head_dim, qkv_ref, cos_ref, sin_ref, kind_ref, norm_ref, q_ref, pair_ref):
    pair = 2 * head_dim
    rows = qkv_ref.shape[0]
    lane = lax.broadcasted_iota(jnp.int32, (rows, pair), 1)
    first = lane < head_dim
    even = lane % 2 == 0
    request = kind_ref[...] // 2
    mask_part = jnp.where(lane == head_dim + request, 1.0, 0.0)
    cosine = cos_ref[...]
    sine = sin_ref[...]
    gain = norm_ref[0:1, :]
    bias = norm_ref[1:2, :]
    for h in range(heads):
        base = 3 * head_dim * h
        both = qkv_ref[:, base : base + pair].astype(F32)
        key_value = qkv_ref[:, base + head_dim : base + head_dim + pair].astype(F32)
        mean_q = jnp.sum(jnp.where(first, both, 0.0), axis=1, keepdims=True) / head_dim
        mean_k = jnp.sum(jnp.where(first, 0.0, both), axis=1, keepdims=True) / head_dim
        center = both - jnp.where(first, mean_q, mean_k)
        square = center * center
        var_q = jnp.sum(jnp.where(first, square, 0.0), axis=1, keepdims=True) / head_dim
        var_k = jnp.sum(jnp.where(first, 0.0, square), axis=1, keepdims=True) / head_dim
        scale = jnp.where(first, lax.rsqrt(var_q + EPS_HEAD), lax.rsqrt(var_k + EPS_HEAD))
        normed = center * scale * gain + bias
        swapped = jnp.where(even, pltpu.roll(normed, pair - 1, 1), pltpu.roll(normed, 1, 1))
        turned = normed * cosine + swapped * sine
        q_ref[h] = jnp.where(first, turned, mask_part).astype(BF)
        pair_ref[h] = jnp.where(first, pltpu.roll(turned, head_dim, 1), key_value).astype(BF)


def prepare(qkv, cosine, sine, kinds, norm_rows, heads, head_dim):
    rows, width = qkv.shape
    block = min(256, rows)
    pair = 2 * head_dim
    return pl.pallas_call(
        functools.partial(prepare_kernel, heads, head_dim),
        grid=(rows // block,),
        in_specs=[
            pl.BlockSpec((block, width), lambda i: (i, 0)),
            pl.BlockSpec((block, pair), lambda i: (i, 0)),
            pl.BlockSpec((block, pair), lambda i: (i, 0)),
            pl.BlockSpec((block, 1), lambda i: (i, 0)),
            pl.BlockSpec((2, pair), lambda i: (0, 0)),
        ],
        out_specs=[
            pl.BlockSpec((heads, block, pair), lambda i: (0, i, 0)),
            pl.BlockSpec((heads, block, pair), lambda i: (0, i, 0)),
        ],
        out_shape=[
            jax.ShapeDtypeStruct((heads, rows, pair), BF),
            jax.ShapeDtypeStruct((heads, rows, pair), BF),
        ],
        compiler_params=pltpu.CompilerParams(vmem_limit_bytes=48 * 1024 * 1024),
        name="prepare",
    )(qkv, cosine, sine, kinds[:, None], norm_rows)


def attend_kernel(heads, head_dim, q_ref, own_ref, other_ref, own_mask_ref, other_mask_ref, out_ref):
    pair = 2 * head_dim
    keys_count = own_ref.shape[1]
    lane = lax.broadcasted_iota(jnp.int32, (keys_count, pair), 1)
    first = lane < head_dim
    one = jnp.where(lane == 0, 1.0, 0.0).astype(BF)
    factor = LOG2E * head_dim ** (-0.5)
    pieces = []
    for h in range(heads):
        queries = q_ref[h]
        own = own_ref[h]
        other = other_ref[h]
        contract = (((1,), (1,)), ((), ()))
        scores_a = lax.dot_general(
            queries, jnp.where(first, own, own_mask_ref[...]), contract, preferred_element_type=F32
        )
        scores_b = lax.dot_general(
            queries, jnp.where(first, other, other_mask_ref[...]), contract, preferred_element_type=F32
        )
        top = jnp.maximum(
            jnp.max(scores_a, axis=1, keepdims=True), jnp.max(scores_b, axis=1, keepdims=True)
        )
        weights_a = jnp.exp2((scores_a - top) * factor).astype(BF)
        weights_b = jnp.exp2((scores_b - top) * factor).astype(BF)
        mixed = jnp.dot(weights_a, jnp.where(first, one, own), preferred_element_type=F32)
        mixed += jnp.dot(weights_b, jnp.where(first, one, other), preferred_element_type=F32)
        pieces.append(mixed[:, head_dim:] / mixed[:, 0:1])
    out_ref[...] = jnp.concatenate(pieces, axis=1).astype(BF)


def attend(queries, own, other, own_mask, other_mask, head_dim):
    heads, rows, pair = queries.shape
    keys_count = own.shape[1]
    block = min(256, rows)
    whole = pl.BlockSpec((heads, keys_count, pair), lambda i: (0, 0, 0))
    mask = pl.BlockSpec((keys_count, pair), lambda i: (0, 0))
    return pl.pallas_call(
        functools.partial(attend_kernel, heads, head_dim),
        grid=(rows // block,),
        in_specs=[pl.BlockSpec((heads, block, pair), lambda i: (0, i, 0)), whole, whole, mask, mask],
        out_specs=pl.BlockSpec((block, heads * head_dim), lambda i: (i, 0)),
        out_shape=jax.ShapeDtypeStruct((rows, heads * head_dim), BF),
        compiler_params=pltpu.CompilerParams(vmem_limit_bytes=48 * 1024 * 1024),
        name="attend",
    )(queries, own, other, own_mask, other_mask)


def key_mask(kinds, head_dim):
    lane = jnp.arange(2 * head_dim)[None, :]
    foreign = (lane >= head_dim) & (lane < head_dim + 2) & (lane - head_dim != (kinds // 2)[:, None])
    return jnp.where(foreign, FAR, 0.0).astype(BF)


def pick(table, kinds, part):
    column = kinds[:, None]
    low = jnp.where(column == 0, table[0, part][None], table[1, part][None])
    high = jnp.where(column == 2, table[2, part][None], table[3, part][None])
    return jnp.where(column < 2, low, high)


def exchange(blocks, axis):
    n = lax.axis_size(axis)
    me = lax.axis_index(axis)
    got = jnp.zeros_like(blocks)
    got = lax.dynamic_update_slice_in_dim(
        got, lax.dynamic_slice_in_dim(blocks, me, 1, 0), me, 0
    )
    for step in range(1, n):
        there = (me + step) % n
        back = (me + n - step) % n
        block = lax.dynamic_slice_in_dim(blocks, there, 1, 0)
        block = lax.ppermute(block, axis, [(i, (i + step) % n) for i in range(n)])
        got = lax.dynamic_update_slice_in_dim(got, block, back, 0)
    return got


def per_device(
    hidden_in,
    row_kind,
    positions,
    timesteps,
    stale_cache,
    w_qkv,
    qk_norm,
    w_out,
    ada_weight,
    w_up,
    w_down,
):
    operands = (
        hidden_in,
        row_kind,
        positions,
        timesteps,
        stale_cache,
        w_qkv[0],
        qk_norm[0],
        w_out[0],
        ada_weight[0],
        w_up[0],
        w_down[0],
    )
    n_narrow = lax.axis_size("narrow")
    if n_narrow == lax.axis_size("wide") and stale_cache.shape[3] % n_narrow == 0:
        return in_halves(*operands)
    return features_split(*operands)


def swap(value):
    return lax.ppermute(value, "section", [(0, 1), (1, 0)])


def by_layer(parts, lead):
    got = swap(jnp.where(lead, parts[1], parts[0]))
    kept = jnp.where(lead, parts[0], parts[1])
    return jnp.stack([jnp.where(lead, kept, got), jnp.where(lead, got, kept)])[None]


def norm_pairs(norms):
    return jnp.stack([jnp.concatenate([norms[0], norms[2]]), jnp.concatenate([norms[1], norms[3]])])


def modulate(values, table, kinds):
    return (values * (1.0 + pick(table, kinds, 1)) + pick(table, kinds, 0)).astype(BF)


def wide_pairs(step):
    return [(i, i ^ step) for i in range(lax.axis_size("wide"))]


def gather_wide(block):
    got = [lax.ppermute(block, "wide", wide_pairs(step)) for step in range(1, lax.axis_size("wide"))]
    return jnp.concatenate([block] + got, axis=0)


def scatter_wide(terms):
    total = terms[0].astype(F32)
    for step in range(1, len(terms)):
        total += lax.ppermute(terms[step], "wide", wide_pairs(step)).astype(F32)
    return total


def gather_line(block):
    n = lax.axis_size("narrow")
    me = lax.axis_index("narrow")
    from_left = [block]
    from_right = [block]
    for step in range(1, n):
        right = [(i, i + 1) for i in range(step - 1, n - 1)]
        left = [(i + 1, i) for i in range(0, n - step)]
        from_left.append(lax.ppermute(from_left[-1], "narrow", right))
        from_right.append(lax.ppermute(from_right[-1], "narrow", left))
    return [block] + [
        jnp.where(me >= step, from_left[step], from_right[n - step]) for step in range(1, n)
    ]


def line_norm(values, model_width):
    n = lax.axis_size("narrow")
    width = values.shape[1]
    mean = jnp.mean(values, axis=1)
    center = values - mean[:, None]
    own = jnp.stack([mean, jnp.sum(center * center, axis=1)])
    parts = [own]
    for step in range(1, n):
        parts.append(lax.ppermute(own, "narrow", [(i, (i + step) % n) for i in range(n)]))
    whole_mean = sum(part[0] for part in parts) / n
    spread = sum(part[1] + width * (part[0] - whole_mean) ** 2 for part in parts)
    scale = lax.rsqrt(spread / model_width + EPS_ROW)
    return (values - whole_mean[:, None]) * scale[:, None]


def in_halves(
    hidden_in,
    row_kind,
    positions,
    timesteps,
    stale_cache,
    w_qkv,
    qk_norm,
    w_out,
    ada_weight,
    w_up,
    w_down,
):
    n_wide = lax.axis_size("wide")
    n_narrow = lax.axis_size("narrow")
    wide_idx = lax.axis_index("wide")
    narrow_idx = lax.axis_index("narrow")
    section = lax.axis_index("section")
    lead = section == 0
    _, rows_a, feat_a = hidden_in.shape
    halves = 2
    part = rows_a // halves
    total_rows = rows_a * n_wide
    rows_b = total_rows // n_narrow
    heads_local = stale_cache.shape[3]
    heads = heads_local // n_narrow
    pair = stale_cache.shape[4]
    head_dim = pair // 2
    model_width = feat_a * n_narrow

    def both_layers(own):
        other = swap(own)
        return (jnp.where(lead, own, other), jnp.where(lead, other, own))

    def relative(values):
        blocks = values.reshape(n_wide, halves, part)
        order = [lax.dynamic_index_in_dim(blocks, wide_idx ^ step, 0, False) for step in range(n_wide)]
        return jnp.stack(order, axis=1).reshape(total_rows)

    activated = jax.nn.silu(time_features(timesteps, ada_weight.shape[1])).astype(BF)
    modulation = jnp.einsum("re,kesd->krsd", activated, ada_weight, preferred_element_type=F32)
    tables = both_layers(modulation.reshape(2, 4, 3, feat_a))
    qkv_weights = both_layers(w_qkv)
    norm_rows = both_layers(qk_norm)
    out_weights = both_layers(w_out)
    up_weights = both_layers(w_up)
    down_weights = both_layers(w_down)

    kinds = lax.dynamic_index_in_dim(row_kind, section, 0, False)
    kinds_other = lax.dynamic_index_in_dim(row_kind, 1 - section, 0, False)
    kinds_r = relative(kinds)
    own_mask = key_mask(kinds_r, head_dim)
    other_mask = key_mask(jnp.where(lead, kinds_other, relative(kinds_other)), head_dim)
    kinds_a = lax.dynamic_slice_in_dim(kinds, wide_idx * rows_a, rows_a)
    kinds_h = [kinds_a[h * part : (h + 1) * part] for h in range(halves)]
    places = lax.dynamic_index_in_dim(positions, section, 1, False)
    places = jnp.stack([relative(places[i]) for i in range(3)])
    cosine, sine = rotary_tables(places, head_dim)
    chunk = total_rows // halves

    blocks = stale_cache[0, 1].reshape(rows_b, n_narrow, heads, pair).transpose(1, 2, 0, 3)
    stale = exchange(blocks, "narrow").transpose(1, 0, 2, 3).reshape(heads, total_rows, pair)

    def to_rows(fresh):
        blocks = [f.reshape(heads, n_wide, part, pair) for f in fresh]
        per_narrow = []
        for there in range(n_narrow):
            picked = [lax.dynamic_index_in_dim(b, wide_idx ^ there, 1, False) for b in blocks]
            per_narrow.append(jnp.concatenate(picked, axis=1))
        got = exchange(jnp.stack(per_narrow), "narrow")
        return got.transpose(2, 0, 1, 3).reshape(rows_b, heads_local, pair)

    layer_in = lax.dynamic_index_in_dim(hidden_in, section, 0, False)
    layer_in = [layer_in[h * part : (h + 1) * part] for h in range(halves)]
    results = []
    caches = []
    for layer in range(2):
        table = tables[layer]
        norm_pair = norm_pairs(norm_rows[layer])
        x_in = [block.astype(F32) for block in layer_in]
        queries = []
        fresh = []
        for h in range(halves):
            entry = modulate(line_norm(x_in[h], model_width), table[0], kinds_h[h])
            terms = jnp.dot(gather_wide(entry), qkv_weights[layer], preferred_element_type=F32)
            qkv = lax.psum_scatter(terms.astype(BF), "narrow", scatter_dimension=1, tiled=True)
            rows = slice(h * chunk, (h + 1) * chunk)
            q, pairs = prepare(
                qkv, cosine[rows], sine[rows], kinds_r[rows], norm_pair, heads, head_dim
            )
            queries.append(q)
            fresh.append(pairs)
        caches.append(to_rows(fresh))
        own = jnp.concatenate(fresh, axis=1)
        if layer == 0:
            other = jnp.where(lead, stale, lax.ppermute(own, "section", [(0, 1)]))
        else:
            other = swap(jnp.where(lead, own, stale))
        after = []
        for h in range(halves):
            attended = attend(queries[h], own, other, own_mask, other_mask, head_dim)
            attended = lax.all_gather(attended, "narrow", axis=1, tiled=True)
            terms = jnp.dot(attended, out_weights[layer], preferred_element_type=F32).astype(BF)
            projected = scatter_wide([terms[r * part : (r + 1) * part] for r in range(n_wide)])
            after.append(x_in[h] + pick(table[0], kinds_h[h], 2) * projected)
        inner = []
        for h in range(halves):
            entry = modulate(line_norm(after[h], model_width), table[1], kinds_h[h])
            terms = jnp.dot(gather_wide(entry), up_weights[layer], preferred_element_type=F32)
            up = lax.psum_scatter(terms.astype(BF), "narrow", scatter_dimension=0, tiled=True)
            inner.append(jax.nn.gelu(up.astype(F32), approximate=True).astype(BF))
        layer_in = []
        for h in range(halves):
            gathered = jnp.concatenate(gather_line(inner[h]), axis=0)
            terms = jnp.dot(gathered, down_weights[layer], preferred_element_type=F32).astype(BF)
            size = chunk // n_narrow
            ordered = [
                lax.dynamic_slice_in_dim(terms, (narrow_idx + n_narrow - r) % n_narrow * size, size, 0)
                for r in range(n_narrow)
            ]
            down = scatter_wide(ordered)
            layer_in.append((after[h] + pick(table[1], kinds_h[h], 2) * down).astype(BF))
        results.append(jnp.concatenate(layer_in, axis=0))
    return (by_layer(results, lead), by_layer(caches, lead))


def features_split(
    hidden_in,
    row_kind,
    positions,
    timesteps,
    stale_cache,
    w_qkv,
    qk_norm,
    w_out,
    ada_weight,
    w_up,
    w_down,
):
    n_wide = lax.axis_size("wide")
    n_narrow = lax.axis_size("narrow")
    wide_idx = lax.axis_index("wide")
    narrow_idx = lax.axis_index("narrow")
    section = lax.axis_index("section")
    patch_count, rows_a, feat_a = hidden_in.shape
    total_rows = rows_a * n_wide
    rows_b = total_rows // n_narrow
    heads_local = stale_cache.shape[3]
    pair = stale_cache.shape[4]
    head_dim = pair // 2
    model_width = feat_a * n_narrow
    heads = heads_local
    lead = section == 0

    def both_layers(own):
        other = swap(own)
        return (jnp.where(lead, own, other), jnp.where(lead, other, own))

    qkv_weights = both_layers(w_qkv)
    out_weights = both_layers(w_out)
    up_weights = both_layers(w_up)
    down_weights = both_layers(w_down)
    norm_rows = both_layers(qk_norm)

    activated = jax.nn.silu(time_features(timesteps, ada_weight.shape[1])).astype(BF)
    modulation = jnp.einsum("re,kesd->krsd", activated, ada_weight, preferred_element_type=F32)
    tables = both_layers(modulation.reshape(2, 4, 3, feat_a))

    kinds = lax.dynamic_slice_in_dim(row_kind, section, 1, 0)[0]
    kinds_other = lax.dynamic_slice_in_dim(row_kind, 1 - section, 1, 0)[0]
    own_mask = key_mask(kinds, head_dim)
    other_mask = key_mask(kinds_other, head_dim)
    kinds_a = lax.dynamic_slice_in_dim(kinds, wide_idx * rows_a, rows_a)
    places = lax.dynamic_slice_in_dim(positions, section, 1, 1)[:, 0]
    places = lax.dynamic_slice_in_dim(places, narrow_idx * rows_b, rows_b, 1)
    kinds_q = lax.dynamic_slice_in_dim(kinds, narrow_idx * rows_b, rows_b)
    cosine, sine = rotary_tables(places, head_dim)

    stale = lax.all_gather(stale_cache[0, 1].transpose(1, 0, 2), "narrow", axis=1, tiled=True)

    def normalize(values):
        moments = lax.psum(
            jnp.stack([jnp.sum(values, axis=1), jnp.sum(values * values, axis=1)]), "narrow"
        )
        row_mean = moments[0] / model_width
        variance = moments[1] / model_width - row_mean * row_mean
        return (values - row_mean[:, None]) * lax.rsqrt(variance + EPS_ROW)[:, None]

    layer_in = lax.dynamic_slice_in_dim(hidden_in, section, 1, 0)[0]
    results = []
    caches = []
    for layer in range(2):
        table = tables[layer]
        x_in = layer_in.astype(F32)
        entry = modulate(normalize(x_in), table[0], kinds_a)
        qkv_terms = jnp.dot(
            lax.all_gather(entry, "wide", axis=0, tiled=True),
            qkv_weights[layer],
            preferred_element_type=F32,
        ).astype(BF)
        qkv = lax.psum_scatter(qkv_terms, "narrow", scatter_dimension=0, tiled=True)
        queries, fresh = prepare(
            qkv, cosine, sine, kinds_q, norm_pairs(norm_rows[layer]), heads, head_dim
        )
        caches.append(fresh.transpose(1, 0, 2))
        fresh = lax.all_gather(fresh, "narrow", axis=1, tiled=True)
        if layer == 0:
            other = jnp.where(lead, stale, swap(fresh))
        else:
            other = swap(jnp.where(lead, fresh, stale))
        attended = attend(queries, fresh, other, own_mask, other_mask, head_dim)
        attended = lax.all_gather(attended, "narrow", axis=0, tiled=True)
        proj_terms = jnp.dot(attended, out_weights[layer], preferred_element_type=F32).astype(BF)
        projected = lax.psum_scatter(proj_terms, "wide", scatter_dimension=0, tiled=True)
        after = x_in + pick(table[0], kinds_a, 2) * projected.astype(F32)
        entry = modulate(normalize(after), table[1], kinds_a)
        up_terms = jnp.dot(
            lax.all_gather(entry, "wide", axis=0, tiled=True),
            up_weights[layer],
            preferred_element_type=F32,
        ).astype(BF)
        up_sum = lax.psum_scatter(up_terms, "narrow", scatter_dimension=0, tiled=True)
        inner = jax.nn.gelu(up_sum.astype(F32), approximate=True).astype(BF)
        down_terms = jnp.dot(
            lax.all_gather(inner, "narrow", axis=0, tiled=True),
            down_weights[layer],
            preferred_element_type=F32,
        ).astype(BF)
        down_sum = lax.psum_scatter(down_terms, "wide", scatter_dimension=0, tiled=True)
        layer_in = (after + pick(table[1], kinds_a, 2) * down_sum.astype(F32)).astype(BF)
        results.append(layer_in)

    return (by_layer(results, lead), by_layer(caches, lead))


def solution(mesh):
    in_specs = (
        P(None, "wide", "narrow"),
        P(),
        P(),
        P(),
        P("section", None, "narrow", "wide", None),
        P("section", "narrow", "wide"),
        P("section", None, None),
        P("section", "wide", "narrow"),
        P("section", None, None, None, "narrow"),
        P("section", "narrow", "wide"),
        P("section", "wide", "narrow"),
    )
    out_specs = (P("section", None, "wide", "narrow"), P("section", None, "narrow", "wide", None))
    return jax.shard_map(
        per_device, mesh=mesh, in_specs=in_specs, out_specs=out_specs, check_vma=False
    )
```

```python
import functools

import jax
import jax.numpy as jnp
from jax import lax
from jax.experimental import pallas as pl
from jax.experimental.pallas import tpu as pltpu
from jax.sharding import PartitionSpec as P

EPS_ROW = 1e-05
EPS_HEAD = 1e-06
FAR = -1e30
LOG2E = 1.4426950408889634
BF = jnp.bfloat16
F32 = jnp.float32


def time_features(timesteps, feature_count):
    half_count = feature_count // 2
    frequency = jnp.exp(-jnp.log(10000.0) * jnp.arange(half_count, dtype=F32) / half_count)
    angle = timesteps.astype(F32)[:, None] * frequency[None, :]
    return jnp.concatenate([jnp.cos(angle), jnp.sin(angle)], axis=1)


def rotary_tables(row_positions, head_dim):
    dim_frame = head_dim // 4
    dim_plane = head_dim // 8 * 3
    pieces = []
    for axis_pos, span_dims in ((0, dim_frame), (1, dim_plane), (2, dim_plane)):
        frequency = 10000.0 ** (-jnp.arange(0, span_dims, 2, dtype=F32) / span_dims)
        pieces.append(row_positions[axis_pos].astype(F32)[:, None] * jnp.repeat(frequency, 2)[None, :])
    angles = jnp.concatenate(pieces, axis=1)
    sign = jnp.where(jnp.arange(head_dim) % 2 == 0, -1.0, 1.0).astype(F32)
    cosine = jnp.cos(angles)
    sine = jnp.sin(angles) * sign[None, :]
    return jnp.concatenate([cosine, cosine], axis=1), jnp.concatenate([sine, sine], axis=1)


def prepare_kernel(heads, head_dim, qkv_ref, cos_ref, sin_ref, kind_ref, norm_ref, q_ref, pair_ref):
    pair = 2 * head_dim
    rows = qkv_ref.shape[0]
    lane = lax.broadcasted_iota(jnp.int32, (rows, pair), 1)
    first = lane < head_dim
    even = lane % 2 == 0
    request = kind_ref[...] // 2
    mask_part = jnp.where(lane == head_dim + request, 1.0, 0.0)
    cosine = cos_ref[...]
    sine = sin_ref[...]
    gain = norm_ref[0:1, :]
    bias = norm_ref[1:2, :]
    for h in range(heads):
        base = 3 * head_dim * h
        both = qkv_ref[:, base : base + pair].astype(F32)
        key_value = qkv_ref[:, base + head_dim : base + head_dim + pair].astype(F32)
        mean_q = jnp.sum(jnp.where(first, both, 0.0), axis=1, keepdims=True) / head_dim
        mean_k = jnp.sum(jnp.where(first, 0.0, both), axis=1, keepdims=True) / head_dim
        center = both - jnp.where(first, mean_q, mean_k)
        square = center * center
        var_q = jnp.sum(jnp.where(first, square, 0.0), axis=1, keepdims=True) / head_dim
        var_k = jnp.sum(jnp.where(first, 0.0, square), axis=1, keepdims=True) / head_dim
        scale = jnp.where(first, lax.rsqrt(var_q + EPS_HEAD), lax.rsqrt(var_k + EPS_HEAD))
        normed = center * scale * gain + bias
        swapped = jnp.where(even, pltpu.roll(normed, pair - 1, 1), pltpu.roll(normed, 1, 1))
        turned = normed * cosine + swapped * sine
        q_ref[h] = jnp.where(first, turned, mask_part).astype(BF)
        pair_ref[h] = jnp.where(first, pltpu.roll(turned, head_dim, 1), key_value).astype(BF)


def prepare(qkv, cosine, sine, kinds, norm_rows, heads, head_dim):
    rows, width = qkv.shape
    block = min(256, rows)
    pair = 2 * head_dim
    return pl.pallas_call(
        functools.partial(prepare_kernel, heads, head_dim),
        grid=(rows // block,),
        in_specs=[
            pl.BlockSpec((block, width), lambda i: (i, 0)),
            pl.BlockSpec((block, pair), lambda i: (i, 0)),
            pl.BlockSpec((block, pair), lambda i: (i, 0)),
            pl.BlockSpec((block, 1), lambda i: (i, 0)),
            pl.BlockSpec((2, pair), lambda i: (0, 0)),
        ],
        out_specs=[
            pl.BlockSpec((heads, block, pair), lambda i: (0, i, 0)),
            pl.BlockSpec((heads, block, pair), lambda i: (0, i, 0)),
        ],
        out_shape=[
            jax.ShapeDtypeStruct((heads, rows, pair), BF),
            jax.ShapeDtypeStruct((heads, rows, pair), BF),
        ],
        compiler_params=pltpu.CompilerParams(vmem_limit_bytes=48 * 1024 * 1024),
        name="prepare",
    )(qkv, cosine, sine, kinds[:, None], norm_rows)


def attend_kernel(heads, head_dim, q_ref, own_ref, other_ref, own_mask_ref, other_mask_ref, out_ref):
    pair = 2 * head_dim
    keys_count = own_ref.shape[1]
    lane = lax.broadcasted_iota(jnp.int32, (keys_count, pair), 1)
    first = lane < head_dim
    one = jnp.where(lane == 0, 1.0, 0.0).astype(BF)
    factor = LOG2E * head_dim ** (-0.5)
    pieces = []
    for h in range(heads):
        queries = q_ref[h]
        own = own_ref[h]
        other = other_ref[h]
        contract = (((1,), (1,)), ((), ()))
        scores_a = lax.dot_general(
            queries, jnp.where(first, own, own_mask_ref[...]), contract, preferred_element_type=F32
        )
        scores_b = lax.dot_general(
            queries, jnp.where(first, other, other_mask_ref[...]), contract, preferred_element_type=F32
        )
        top = jnp.maximum(
            jnp.max(scores_a, axis=1, keepdims=True), jnp.max(scores_b, axis=1, keepdims=True)
        )
        weights_a = jnp.exp2((scores_a - top) * factor).astype(BF)
        weights_b = jnp.exp2((scores_b - top) * factor).astype(BF)
        mixed = jnp.dot(weights_a, jnp.where(first, one, own), preferred_element_type=F32)
        mixed += jnp.dot(weights_b, jnp.where(first, one, other), preferred_element_type=F32)
        pieces.append(mixed[:, head_dim:] / mixed[:, 0:1])
    out_ref[...] = jnp.concatenate(pieces, axis=1).astype(BF)


def attend(queries, own, other, own_mask, other_mask, head_dim):
    heads, rows, pair = queries.shape
    keys_count = own.shape[1]
    block = min(256, rows)
    whole = pl.BlockSpec((heads, keys_count, pair), lambda i: (0, 0, 0))
    mask = pl.BlockSpec((keys_count, pair), lambda i: (0, 0))
    return pl.pallas_call(
        functools.partial(attend_kernel, heads, head_dim),
        grid=(rows // block,),
        in_specs=[pl.BlockSpec((heads, block, pair), lambda i: (0, i, 0)), whole, whole, mask, mask],
        out_specs=pl.BlockSpec((block, heads * head_dim), lambda i: (i, 0)),
        out_shape=jax.ShapeDtypeStruct((rows, heads * head_dim), BF),
        compiler_params=pltpu.CompilerParams(vmem_limit_bytes=48 * 1024 * 1024),
        name="attend",
    )(queries, own, other, own_mask, other_mask)


def key_mask(kinds, head_dim):
    lane = jnp.arange(2 * head_dim)[None, :]
    foreign = (lane >= head_dim) & (lane < head_dim + 2) & (lane - head_dim != (kinds // 2)[:, None])
    return jnp.where(foreign, FAR, 0.0).astype(BF)


def pick(table, kinds, part):
    column = kinds[:, None]
    low = jnp.where(column == 0, table[0, part][None], table[1, part][None])
    high = jnp.where(column == 2, table[2, part][None], table[3, part][None])
    return jnp.where(column < 2, low, high)


def exchange(blocks, axis):
    n = lax.axis_size(axis)
    me = lax.axis_index(axis)
    got = jnp.zeros_like(blocks)
    got = lax.dynamic_update_slice_in_dim(
        got, lax.dynamic_slice_in_dim(blocks, me, 1, 0), me, 0
    )
    for step in range(1, n):
        there = (me + step) % n
        back = (me + n - step) % n
        block = lax.dynamic_slice_in_dim(blocks, there, 1, 0)
        block = lax.ppermute(block, axis, [(i, (i + step) % n) for i in range(n)])
        got = lax.dynamic_update_slice_in_dim(got, block, back, 0)
    return got


def per_device(
    hidden_in,
    row_kind,
    positions,
    timesteps,
    stale_cache,
    w_qkv,
    qk_norm,
    w_out,
    ada_weight,
    w_up,
    w_down,
):
    operands = (
        hidden_in,
        row_kind,
        positions,
        timesteps,
        stale_cache,
        w_qkv[0],
        qk_norm[0],
        w_out[0],
        ada_weight[0],
        w_up[0],
        w_down[0],
    )
    n_narrow = lax.axis_size("narrow")
    if n_narrow == lax.axis_size("wide") and stale_cache.shape[3] % n_narrow == 0:
        return in_halves(*operands)
    return features_split(*operands)


def swap(value):
    return lax.ppermute(value, "section", [(0, 1), (1, 0)])


def by_layer(parts, lead):
    got = swap(jnp.where(lead, parts[1], parts[0]))
    kept = jnp.where(lead, parts[0], parts[1])
    return jnp.stack([jnp.where(lead, kept, got), jnp.where(lead, got, kept)])[None]


def norm_pairs(norms):
    return jnp.stack([jnp.concatenate([norms[0], norms[2]]), jnp.concatenate([norms[1], norms[3]])])


def modulate(values, table, kinds):
    return (values * (1.0 + pick(table, kinds, 1)) + pick(table, kinds, 0)).astype(BF)


def wide_pairs(step):
    return [(i, i ^ step) for i in range(lax.axis_size("wide"))]


def gather_wide(block):
    got = [lax.ppermute(block, "wide", wide_pairs(step)) for step in range(1, lax.axis_size("wide"))]
    return jnp.concatenate([block] + got, axis=0)


def scatter_wide(terms):
    total = terms[0].astype(F32)
    for step in range(1, len(terms)):
        total += lax.ppermute(terms[step], "wide", wide_pairs(step)).astype(F32)
    return total


def gather_line(block):
    n = lax.axis_size("narrow")
    me = lax.axis_index("narrow")
    from_left = [block]
    from_right = [block]
    for step in range(1, n):
        right = [(i, i + 1) for i in range(step - 1, n - 1)]
        left = [(i + 1, i) for i in range(0, n - step)]
        from_left.append(lax.ppermute(from_left[-1], "narrow", right))
        from_right.append(lax.ppermute(from_right[-1], "narrow", left))
    return [block] + [
        jnp.where(me >= step, from_left[step], from_right[n - step]) for step in range(1, n)
    ]


def gather_direct(block):
    n = lax.axis_size("narrow")
    return [block] + [
        lax.ppermute(block, "narrow", [(i, (i + step) % n) for i in range(n)]) for step in range(1, n)
    ]


def line_norm(values, model_width):
    n = lax.axis_size("narrow")
    width = values.shape[1]
    mean = jnp.mean(values, axis=1)
    center = values - mean[:, None]
    own = jnp.stack([mean, jnp.sum(center * center, axis=1)])
    parts = [own]
    for step in range(1, n):
        parts.append(lax.ppermute(own, "narrow", [(i, (i + step) % n) for i in range(n)]))
    whole_mean = sum(part[0] for part in parts) / n
    spread = sum(part[1] + width * (part[0] - whole_mean) ** 2 for part in parts)
    scale = lax.rsqrt(spread / model_width + EPS_ROW)
    return (values - whole_mean[:, None]) * scale[:, None]


def in_halves(
    hidden_in,
    row_kind,
    positions,
    timesteps,
    stale_cache,
    w_qkv,
    qk_norm,
    w_out,
    ada_weight,
    w_up,
    w_down,
):
    n_wide = lax.axis_size("wide")
    n_narrow = lax.axis_size("narrow")
    wide_idx = lax.axis_index("wide")
    narrow_idx = lax.axis_index("narrow")
    section = lax.axis_index("section")
    lead = section == 0
    _, rows_a, feat_a = hidden_in.shape
    halves = 2
    part = rows_a // halves
    total_rows = rows_a * n_wide
    rows_b = total_rows // n_narrow
    heads_local = stale_cache.shape[3]
    heads = heads_local // n_narrow
    pair = stale_cache.shape[4]
    head_dim = pair // 2
    model_width = feat_a * n_narrow

    def both_layers(own):
        other = swap(own)
        return (jnp.where(lead, own, other), jnp.where(lead, other, own))

    def relative(values):
        blocks = values.reshape(n_wide, halves, part)
        order = [lax.dynamic_index_in_dim(blocks, wide_idx ^ step, 0, False) for step in range(n_wide)]
        return jnp.stack(order, axis=1).reshape(total_rows)

    activated = jax.nn.silu(time_features(timesteps, ada_weight.shape[1])).astype(BF)
    modulation = jnp.einsum("re,kesd->krsd", activated, ada_weight, preferred_element_type=F32)
    tables = both_layers(modulation.reshape(2, 4, 3, feat_a))
    qkv_weights = both_layers(w_qkv)
    norm_rows = both_layers(qk_norm)
    out_weights = both_layers(w_out)
    up_weights = both_layers(w_up)
    down_weights = both_layers(w_down)

    kinds = lax.dynamic_index_in_dim(row_kind, section, 0, False)
    kinds_other = lax.dynamic_index_in_dim(row_kind, 1 - section, 0, False)
    kinds_r = relative(kinds)
    own_mask = key_mask(kinds_r, head_dim)
    other_mask = key_mask(jnp.where(lead, kinds_other, relative(kinds_other)), head_dim)
    kinds_a = lax.dynamic_slice_in_dim(kinds, wide_idx * rows_a, rows_a)
    kinds_h = [kinds_a[h * part : (h + 1) * part] for h in range(halves)]
    places = lax.dynamic_index_in_dim(positions, section, 1, False)
    places = jnp.stack([relative(places[i]) for i in range(3)])
    cosine, sine = rotary_tables(places, head_dim)
    chunk = total_rows // halves

    blocks = stale_cache[0, 1].reshape(rows_b, n_narrow, heads, pair).transpose(1, 2, 0, 3)
    stale = exchange(blocks, "narrow").transpose(1, 0, 2, 3).reshape(heads, total_rows, pair)

    def turned(block, axis):
        size = block.shape[axis] // n_narrow
        starts = [(narrow_idx + n_narrow - step) % n_narrow * size for step in range(n_narrow)]
        return [lax.dynamic_slice_in_dim(block, start, size, axis) for start in starts]

    out_weights = [jnp.concatenate(turned(weight, 0), axis=0) for weight in out_weights]

    def to_rows(fresh):
        blocks = [f.reshape(heads, n_wide, part, pair) for f in fresh]
        per_narrow = []
        for there in range(n_narrow):
            picked = [lax.dynamic_index_in_dim(b, wide_idx ^ there, 1, False) for b in blocks]
            per_narrow.append(jnp.concatenate(picked, axis=1))
        got = exchange(jnp.stack(per_narrow), "narrow")
        return got.transpose(2, 0, 1, 3).reshape(rows_b, heads_local, pair)

    layer_in = lax.dynamic_index_in_dim(hidden_in, section, 0, False)
    layer_in = [layer_in[h * part : (h + 1) * part] for h in range(halves)]
    results = []
    caches = []
    for layer in range(2):
        table = tables[layer]
        norm_pair = norm_pairs(norm_rows[layer])
        x_in = [block.astype(F32) for block in layer_in]
        queries = []
        fresh = []
        for h in range(halves):
            entry = modulate(line_norm(x_in[h], model_width), table[0], kinds_h[h])
            terms = jnp.dot(gather_wide(entry), qkv_weights[layer], preferred_element_type=F32)
            qkv = lax.psum_scatter(terms.astype(BF), "narrow", scatter_dimension=1, tiled=True)
            rows = slice(h * chunk, (h + 1) * chunk)
            q, pairs = prepare(
                qkv, cosine[rows], sine[rows], kinds_r[rows], norm_pair, heads, head_dim
            )
            queries.append(q)
            fresh.append(pairs)
        caches.append(to_rows(fresh))
        own = jnp.concatenate(fresh, axis=1)
        if layer == 0:
            other = jnp.where(lead, stale, lax.ppermute(own, "section", [(0, 1)]))
        else:
            other = swap(jnp.where(lead, own, stale))
        after = []
        for h in range(halves):
            attended = attend(queries[h], own, other, own_mask, other_mask, head_dim)
            attended = jnp.concatenate(gather_direct(attended), axis=1)
            terms = jnp.dot(attended, out_weights[layer], preferred_element_type=F32).astype(BF)
            projected = scatter_wide([terms[r * part : (r + 1) * part] for r in range(n_wide)])
            after.append(x_in[h] + pick(table[0], kinds_h[h], 2) * projected)
        up = []
        for h in range(halves):
            entry = modulate(line_norm(after[h], model_width), table[1], kinds_h[h])
            terms = jnp.dot(gather_wide(entry), up_weights[layer], preferred_element_type=F32)
            up.append(lax.psum_scatter(terms.astype(BF), "narrow", scatter_dimension=0, tiled=True))
        first = gather_line(jax.nn.gelu(up[0].astype(F32), approximate=True).astype(BF))
        first, last = lax.optimization_barrier((first, up[1]))
        last = jax.nn.gelu(last.astype(F32), approximate=True).astype(BF)
        gathered = [
            jnp.concatenate(first, axis=0),
            lax.all_gather(last, "narrow", axis=0, tiled=True),
        ]
        layer_in = []
        for h in range(halves):
            terms = jnp.dot(gathered[h], down_weights[layer], preferred_element_type=F32).astype(BF)
            if h == 0:
                down = scatter_wide(turned(terms, 0))
            else:
                down = scatter_wide([terms[r * part : (r + 1) * part] for r in range(n_wide)])
            layer_in.append((after[h] + pick(table[1], kinds_h[h], 2) * down).astype(BF))
        results.append(jnp.concatenate(layer_in, axis=0))
    return (by_layer(results, lead), by_layer(caches, lead))


def features_split(
    hidden_in,
    row_kind,
    positions,
    timesteps,
    stale_cache,
    w_qkv,
    qk_norm,
    w_out,
    ada_weight,
    w_up,
    w_down,
):
    n_wide = lax.axis_size("wide")
    n_narrow = lax.axis_size("narrow")
    wide_idx = lax.axis_index("wide")
    narrow_idx = lax.axis_index("narrow")
    section = lax.axis_index("section")
    patch_count, rows_a, feat_a = hidden_in.shape
    total_rows = rows_a * n_wide
    rows_b = total_rows // n_narrow
    heads_local = stale_cache.shape[3]
    pair = stale_cache.shape[4]
    head_dim = pair // 2
    model_width = feat_a * n_narrow
    heads = heads_local
    lead = section == 0

    def both_layers(own):
        other = swap(own)
        return (jnp.where(lead, own, other), jnp.where(lead, other, own))

    qkv_weights = both_layers(w_qkv)
    out_weights = both_layers(w_out)
    up_weights = both_layers(w_up)
    down_weights = both_layers(w_down)
    norm_rows = both_layers(qk_norm)

    activated = jax.nn.silu(time_features(timesteps, ada_weight.shape[1])).astype(BF)
    modulation = jnp.einsum("re,kesd->krsd", activated, ada_weight, preferred_element_type=F32)
    tables = both_layers(modulation.reshape(2, 4, 3, feat_a))

    kinds = lax.dynamic_slice_in_dim(row_kind, section, 1, 0)[0]
    kinds_other = lax.dynamic_slice_in_dim(row_kind, 1 - section, 1, 0)[0]
    own_mask = key_mask(kinds, head_dim)
    other_mask = key_mask(kinds_other, head_dim)
    kinds_a = lax.dynamic_slice_in_dim(kinds, wide_idx * rows_a, rows_a)
    places = lax.dynamic_slice_in_dim(positions, section, 1, 1)[:, 0]
    places = lax.dynamic_slice_in_dim(places, narrow_idx * rows_b, rows_b, 1)
    kinds_q = lax.dynamic_slice_in_dim(kinds, narrow_idx * rows_b, rows_b)
    cosine, sine = rotary_tables(places, head_dim)

    stale = lax.all_gather(stale_cache[0, 1].transpose(1, 0, 2), "narrow", axis=1, tiled=True)

    def normalize(values):
        moments = lax.psum(
            jnp.stack([jnp.sum(values, axis=1), jnp.sum(values * values, axis=1)]), "narrow"
        )
        row_mean = moments[0] / model_width
        variance = moments[1] / model_width - row_mean * row_mean
        return (values - row_mean[:, None]) * lax.rsqrt(variance + EPS_ROW)[:, None]

    layer_in = lax.dynamic_slice_in_dim(hidden_in, section, 1, 0)[0]
    results = []
    caches = []
    for layer in range(2):
        table = tables[layer]
        x_in = layer_in.astype(F32)
        entry = modulate(normalize(x_in), table[0], kinds_a)
        qkv_terms = jnp.dot(
            lax.all_gather(entry, "wide", axis=0, tiled=True),
            qkv_weights[layer],
            preferred_element_type=F32,
        ).astype(BF)
        qkv = lax.psum_scatter(qkv_terms, "narrow", scatter_dimension=0, tiled=True)
        queries, fresh = prepare(
            qkv, cosine, sine, kinds_q, norm_pairs(norm_rows[layer]), heads, head_dim
        )
        caches.append(fresh.transpose(1, 0, 2))
        fresh = lax.all_gather(fresh, "narrow", axis=1, tiled=True)
        if layer == 0:
            other = jnp.where(lead, stale, swap(fresh))
        else:
            other = swap(jnp.where(lead, fresh, stale))
        attended = attend(queries, fresh, other, own_mask, other_mask, head_dim)
        attended = lax.all_gather(attended, "narrow", axis=0, tiled=True)
        proj_terms = jnp.dot(attended, out_weights[layer], preferred_element_type=F32).astype(BF)
        projected = lax.psum_scatter(proj_terms, "wide", scatter_dimension=0, tiled=True)
        after = x_in + pick(table[0], kinds_a, 2) * projected.astype(F32)
        entry = modulate(normalize(after), table[1], kinds_a)
        up_terms = jnp.dot(
            lax.all_gather(entry, "wide", axis=0, tiled=True),
            up_weights[layer],
            preferred_element_type=F32,
        ).astype(BF)
        up_sum = lax.psum_scatter(up_terms, "narrow", scatter_dimension=0, tiled=True)
        inner = jax.nn.gelu(up_sum.astype(F32), approximate=True).astype(BF)
        down_terms = jnp.dot(
            lax.all_gather(inner, "narrow", axis=0, tiled=True),
            down_weights[layer],
            preferred_element_type=F32,
        ).astype(BF)
        down_sum = lax.psum_scatter(down_terms, "wide", scatter_dimension=0, tiled=True)
        layer_in = (after + pick(table[1], kinds_a, 2) * down_sum.astype(F32)).astype(BF)
        results.append(layer_in)

    return (by_layer(results, lead), by_layer(caches, lead))


def solution(mesh):
    in_specs = (
        P(None, "wide", "narrow"),
        P(),
        P(),
        P(),
        P("section", None, "narrow", "wide", None),
        P("section", "narrow", "wide"),
        P("section", None, None),
        P("section", "wide", "narrow"),
        P("section", None, None, None, "narrow"),
        P("section", "narrow", "wide"),
        P("section", "wide", "narrow"),
    )
    out_specs = (P("section", None, "wide", "narrow"), P("section", None, "narrow", "wide", None))
    return jax.shard_map(
        per_device, mesh=mesh, in_specs=in_specs, out_specs=out_specs, check_vma=False
    )
```

```python
import functools

import jax
import jax.numpy as jnp
from jax import lax
from jax.experimental import pallas as pl
from jax.experimental.pallas import tpu as pltpu
from jax.sharding import PartitionSpec as P

EPS_ROW = 1e-05
EPS_HEAD = 1e-06
FAR = -1e30
LOG2E = 1.4426950408889634
BF = jnp.bfloat16
F32 = jnp.float32


def time_features(timesteps, feature_count):
    half_count = feature_count // 2
    frequency = jnp.exp(-jnp.log(10000.0) * jnp.arange(half_count, dtype=F32) / half_count)
    angle = timesteps.astype(F32)[:, None] * frequency[None, :]
    return jnp.concatenate([jnp.cos(angle), jnp.sin(angle)], axis=1)


def rotary_tables(row_positions, head_dim):
    dim_frame = head_dim // 4
    dim_plane = head_dim // 8 * 3
    pieces = []
    for axis_pos, span_dims in ((0, dim_frame), (1, dim_plane), (2, dim_plane)):
        frequency = 10000.0 ** (-jnp.arange(0, span_dims, 2, dtype=F32) / span_dims)
        pieces.append(row_positions[axis_pos].astype(F32)[:, None] * jnp.repeat(frequency, 2)[None, :])
    angles = jnp.concatenate(pieces, axis=1)
    sign = jnp.where(jnp.arange(head_dim) % 2 == 0, -1.0, 1.0).astype(F32)
    cosine = jnp.cos(angles)
    sine = jnp.sin(angles) * sign[None, :]
    return jnp.concatenate([cosine, cosine], axis=1), jnp.concatenate([sine, sine], axis=1)


def prepare_kernel(heads, head_dim, qkv_ref, cos_ref, sin_ref, kind_ref, norm_ref, q_ref, pair_ref):
    pair = 2 * head_dim
    rows = qkv_ref.shape[0]
    lane = lax.broadcasted_iota(jnp.int32, (rows, pair), 1)
    first = lane < head_dim
    even = lane % 2 == 0
    request = kind_ref[...] // 2
    mask_part = jnp.where(lane == head_dim + request, 1.0, 0.0)
    cosine = cos_ref[...]
    sine = sin_ref[...]
    gain = norm_ref[0:1, :]
    bias = norm_ref[1:2, :]
    for h in range(heads):
        base = 3 * head_dim * h
        both = qkv_ref[:, base : base + pair].astype(F32)
        key_value = qkv_ref[:, base + head_dim : base + head_dim + pair].astype(F32)
        mean_q = jnp.sum(jnp.where(first, both, 0.0), axis=1, keepdims=True) / head_dim
        mean_k = jnp.sum(jnp.where(first, 0.0, both), axis=1, keepdims=True) / head_dim
        center = both - jnp.where(first, mean_q, mean_k)
        square = center * center
        var_q = jnp.sum(jnp.where(first, square, 0.0), axis=1, keepdims=True) / head_dim
        var_k = jnp.sum(jnp.where(first, 0.0, square), axis=1, keepdims=True) / head_dim
        scale = jnp.where(first, lax.rsqrt(var_q + EPS_HEAD), lax.rsqrt(var_k + EPS_HEAD))
        normed = center * scale * gain + bias
        swapped = jnp.where(even, pltpu.roll(normed, pair - 1, 1), pltpu.roll(normed, 1, 1))
        turned = normed * cosine + swapped * sine
        q_ref[h] = jnp.where(first, turned, mask_part).astype(BF)
        pair_ref[h] = jnp.where(first, pltpu.roll(turned, head_dim, 1), key_value).astype(BF)


def prepare(qkv, cosine, sine, kinds, norm_rows, heads, head_dim):
    rows, width = qkv.shape
    block = min(256, rows)
    pair = 2 * head_dim
    return pl.pallas_call(
        functools.partial(prepare_kernel, heads, head_dim),
        grid=(rows // block,),
        in_specs=[
            pl.BlockSpec((block, width), lambda i: (i, 0)),
            pl.BlockSpec((block, pair), lambda i: (i, 0)),
            pl.BlockSpec((block, pair), lambda i: (i, 0)),
            pl.BlockSpec((block, 1), lambda i: (i, 0)),
            pl.BlockSpec((2, pair), lambda i: (0, 0)),
        ],
        out_specs=[
            pl.BlockSpec((heads, block, pair), lambda i: (0, i, 0)),
            pl.BlockSpec((heads, block, pair), lambda i: (0, i, 0)),
        ],
        out_shape=[
            jax.ShapeDtypeStruct((heads, rows, pair), BF),
            jax.ShapeDtypeStruct((heads, rows, pair), BF),
        ],
        compiler_params=pltpu.CompilerParams(vmem_limit_bytes=48 * 1024 * 1024),
        name="prepare",
    )(qkv, cosine, sine, kinds[:, None], norm_rows)


def attend_kernel(heads, head_dim, q_ref, own_ref, other_ref, own_mask_ref, other_mask_ref, out_ref):
    pair = 2 * head_dim
    keys_count = own_ref.shape[1]
    lane = lax.broadcasted_iota(jnp.int32, (keys_count, pair), 1)
    first = lane < head_dim
    one = jnp.where(lane == 0, 1.0, 0.0).astype(BF)
    factor = LOG2E * head_dim ** (-0.5)
    pieces = []
    for h in range(heads):
        queries = q_ref[h]
        own = own_ref[h]
        other = other_ref[h]
        contract = (((1,), (1,)), ((), ()))
        scores_a = lax.dot_general(
            queries, jnp.where(first, own, own_mask_ref[...]), contract, preferred_element_type=F32
        )
        scores_b = lax.dot_general(
            queries, jnp.where(first, other, other_mask_ref[...]), contract, preferred_element_type=F32
        )
        top = jnp.maximum(
            jnp.max(scores_a, axis=1, keepdims=True), jnp.max(scores_b, axis=1, keepdims=True)
        )
        weights_a = jnp.exp2((scores_a - top) * factor).astype(BF)
        weights_b = jnp.exp2((scores_b - top) * factor).astype(BF)
        mixed = jnp.dot(weights_a, jnp.where(first, one, own), preferred_element_type=F32)
        mixed += jnp.dot(weights_b, jnp.where(first, one, other), preferred_element_type=F32)
        pieces.append(mixed[:, head_dim:] / mixed[:, 0:1])
    out_ref[...] = jnp.concatenate(pieces, axis=1).astype(BF)


def attend(queries, own, other, own_mask, other_mask, head_dim):
    heads, rows, pair = queries.shape
    keys_count = own.shape[1]
    block = min(256, rows)
    whole = pl.BlockSpec((heads, keys_count, pair), lambda i: (0, 0, 0))
    mask = pl.BlockSpec((keys_count, pair), lambda i: (0, 0))
    return pl.pallas_call(
        functools.partial(attend_kernel, heads, head_dim),
        grid=(rows // block,),
        in_specs=[pl.BlockSpec((heads, block, pair), lambda i: (0, i, 0)), whole, whole, mask, mask],
        out_specs=pl.BlockSpec((block, heads * head_dim), lambda i: (i, 0)),
        out_shape=jax.ShapeDtypeStruct((rows, heads * head_dim), BF),
        compiler_params=pltpu.CompilerParams(vmem_limit_bytes=48 * 1024 * 1024),
        name="attend",
    )(queries, own, other, own_mask, other_mask)


def key_mask(kinds, head_dim):
    lane = jnp.arange(2 * head_dim)[None, :]
    foreign = (lane >= head_dim) & (lane < head_dim + 2) & (lane - head_dim != (kinds // 2)[:, None])
    return jnp.where(foreign, FAR, 0.0).astype(BF)


def pick(table, kinds, part):
    column = kinds[:, None]
    low = jnp.where(column == 0, table[0, part][None], table[1, part][None])
    high = jnp.where(column == 2, table[2, part][None], table[3, part][None])
    return jnp.where(column < 2, low, high)


def exchange(blocks, axis):
    n = lax.axis_size(axis)
    me = lax.axis_index(axis)
    got = jnp.zeros_like(blocks)
    got = lax.dynamic_update_slice_in_dim(
        got, lax.dynamic_slice_in_dim(blocks, me, 1, 0), me, 0
    )
    for step in range(1, n):
        there = (me + step) % n
        back = (me + n - step) % n
        block = lax.dynamic_slice_in_dim(blocks, there, 1, 0)
        block = lax.ppermute(block, axis, [(i, (i + step) % n) for i in range(n)])
        got = lax.dynamic_update_slice_in_dim(got, block, back, 0)
    return got


def per_device(
    hidden_in,
    row_kind,
    positions,
    timesteps,
    stale_cache,
    w_qkv,
    qk_norm,
    w_out,
    ada_weight,
    w_up,
    w_down,
):
    operands = (
        hidden_in,
        row_kind,
        positions,
        timesteps,
        stale_cache,
        w_qkv[0],
        qk_norm[0],
        w_out[0],
        ada_weight[0],
        w_up[0],
        w_down[0],
    )
    n_narrow = lax.axis_size("narrow")
    if n_narrow == lax.axis_size("wide") and stale_cache.shape[3] % n_narrow == 0:
        return in_halves(*operands)
    return features_split(*operands)


def swap(value):
    return lax.ppermute(value, "section", [(0, 1), (1, 0)])


def by_layer(parts, lead):
    got = swap(jnp.where(lead, parts[1], parts[0]))
    kept = jnp.where(lead, parts[0], parts[1])
    return jnp.stack([jnp.where(lead, kept, got), jnp.where(lead, got, kept)])[None]


def norm_pairs(norms):
    return jnp.stack([jnp.concatenate([norms[0], norms[2]]), jnp.concatenate([norms[1], norms[3]])])


def modulate(values, table, kinds):
    return (values * (1.0 + pick(table, kinds, 1)) + pick(table, kinds, 0)).astype(BF)


def wide_pairs(step):
    return [(i, i ^ step) for i in range(lax.axis_size("wide"))]


def gather_wide(block):
    got = [lax.ppermute(block, "wide", wide_pairs(step)) for step in range(1, lax.axis_size("wide"))]
    return jnp.concatenate([block] + got, axis=0)


def scatter_wide(terms):
    total = terms[0].astype(F32)
    for step in range(1, len(terms)):
        total += lax.ppermute(terms[step], "wide", wide_pairs(step)).astype(F32)
    return total


def gather_direct(block):
    n = lax.axis_size("narrow")
    return [block] + [
        lax.ppermute(block, "narrow", [(i, (i + step) % n) for i in range(n)]) for step in range(1, n)
    ]


def scatter_direct(terms):
    n = lax.axis_size("narrow")
    total = terms[0].astype(F32)
    for step in range(1, n):
        pairs = [(i, (i + n - step) % n) for i in range(n)]
        total += lax.ppermute(terms[step], "narrow", pairs).astype(F32)
    return total


def exchange_of(layer, own, axis):
    n = lax.axis_size("narrow")
    me = lax.axis_index("narrow")
    size = own.shape[axis] // n
    got = []
    for step in range(n):
        block = lax.dynamic_slice_in_dim(own, (me + step) % n * size, size, axis)
        if step:
            pairs = [(layer * n + i, layer * n + (i + step) % n) for i in range(n)]
            block = lax.ppermute(block, ("section", "narrow"), pairs)
        got.append(block)
    joined = jnp.concatenate(got, axis=1 - axis)
    passed = lax.ppermute(joined, "section", [(layer, 1 - layer)])
    return jnp.where(lax.axis_index("section") == layer, joined, passed)


def gather_centered(values):
    mean = jnp.mean(values, axis=1, keepdims=True)
    center = (values - mean).astype(BF)
    high = lax.reduce_precision(mean, 8, 7)
    middle = lax.reduce_precision(mean - high, 8, 7)
    low = mean - high - middle
    lane = jnp.arange(128)[None, :]
    pieces = jnp.where(lane == 0, high, jnp.where(lane == 1, middle, jnp.where(lane == 2, low, 0.0)))
    blocks = gather_direct(jnp.concatenate([center, pieces.astype(BF)], axis=1))
    width = values.shape[1]
    centers = [block[:, :width].astype(F32) for block in blocks]
    means = [jnp.sum(block[:, width : width + 3].astype(F32), axis=1, keepdims=True) for block in blocks]
    return centers, means


def whole_norm(values, table, kinds):
    n = lax.axis_size("narrow")
    width = values.shape[1]
    centers, means = gather_centered(values)
    mean = sum(means) / n
    spread = sum(
        jnp.sum(c * c, axis=1, keepdims=True) + width * (m - mean) ** 2 for c, m in zip(centers, means)
    )
    scale = lax.rsqrt(spread / (n * width) + EPS_ROW)
    normed = jnp.concatenate([(c + (m - mean)) * scale for c, m in zip(centers, means)], axis=1)
    return modulate(normed, table, kinds)


def ordered(*values):
    return lax.optimization_barrier(values)


def in_halves(
    hidden_in,
    row_kind,
    positions,
    timesteps,
    stale_cache,
    w_qkv,
    qk_norm,
    w_out,
    ada_weight,
    w_up,
    w_down,
):
    n_wide = lax.axis_size("wide")
    n_narrow = lax.axis_size("narrow")
    wide_idx = lax.axis_index("wide")
    narrow_idx = lax.axis_index("narrow")
    section = lax.axis_index("section")
    lead = section == 0
    _, rows_a, feat_a = hidden_in.shape
    halves = 2
    part = rows_a // halves
    total_rows = rows_a * n_wide
    rows_b = total_rows // n_narrow
    heads_local = stale_cache.shape[3]
    heads = heads_local // n_narrow
    pair = stale_cache.shape[4]
    head_dim = pair // 2

    def both_layers(own):
        other = swap(own)
        return (jnp.where(lead, own, other), jnp.where(lead, other, own))

    def relative(values):
        blocks = values.reshape(n_wide, halves, part)
        order = [lax.dynamic_index_in_dim(blocks, wide_idx ^ step, 0, False) for step in range(n_wide)]
        return jnp.stack(order, axis=1).reshape(total_rows)

    activated = jax.nn.silu(time_features(timesteps, ada_weight.shape[1])).astype(BF)
    modulation = jnp.einsum("re,kesd->krsd", activated, ada_weight, preferred_element_type=F32)
    modulation = gather_direct(modulation.reshape(2, 4, 3, feat_a))
    tables = both_layers(jnp.concatenate(modulation, axis=-1))
    norm_rows = both_layers(qk_norm)
    size = w_out.shape[0] // n_narrow
    starts = [(narrow_idx + n_narrow - step) % n_narrow * size for step in range(n_narrow)]
    out_weights = both_layers(
        jnp.concatenate([lax.dynamic_slice_in_dim(w_out, start, size, 0) for start in starts], axis=0)
    )

    kinds = lax.dynamic_index_in_dim(row_kind, section, 0, False)
    kinds_other = lax.dynamic_index_in_dim(row_kind, 1 - section, 0, False)
    kinds_r = relative(kinds)
    own_mask = key_mask(kinds_r, head_dim)
    other_mask = key_mask(jnp.where(lead, kinds_other, relative(kinds_other)), head_dim)
    kinds_a = lax.dynamic_slice_in_dim(kinds, wide_idx * rows_a, rows_a)
    kinds_h = [kinds_a[h * part : (h + 1) * part] for h in range(halves)]
    places = lax.dynamic_index_in_dim(positions, section, 1, False)
    places = jnp.stack([relative(places[i]) for i in range(3)])
    cosine, sine = rotary_tables(places, head_dim)
    chunk = total_rows // halves

    blocks = stale_cache[0, 1].reshape(rows_b, n_narrow, heads, pair).transpose(1, 2, 0, 3)
    stale = exchange(blocks, "narrow").transpose(1, 0, 2, 3).reshape(heads, total_rows, pair)

    def to_rows(fresh):
        blocks = [f.reshape(heads, n_wide, part, pair) for f in fresh]
        per_narrow = []
        for there in range(n_narrow):
            picked = [lax.dynamic_index_in_dim(b, wide_idx ^ there, 1, False) for b in blocks]
            per_narrow.append(jnp.concatenate(picked, axis=1))
        got = exchange(jnp.stack(per_narrow), "narrow")
        return got.transpose(2, 0, 1, 3).reshape(rows_b, heads_local, pair)

    def by_wide(terms):
        return [terms[r * part : (r + 1) * part] for r in range(n_wide)]

    layer_in = lax.dynamic_index_in_dim(hidden_in, section, 0, False)
    layer_in = [layer_in[h * part : (h + 1) * part] for h in range(halves)]
    results = []
    caches = []
    qkv_weight = exchange_of(0, w_qkv, 1)
    for layer in range(2):
        table = tables[layer]
        norm_pair = norm_pairs(norm_rows[layer])
        x_in = [block.astype(F32) for block in layer_in]
        queries = []
        fresh = []
        for h in range(halves):
            entry = whole_norm(x_in[h], table[0], kinds_h[h])
            if h == 0 and layer == 0:
                entry, w_up_now = ordered(entry, w_up)
                up_weight = exchange_of(0, w_up_now, 1)
            entry = gather_wide(entry)
            qkv = jnp.dot(entry, qkv_weight, preferred_element_type=F32).astype(BF)
            if h == 0:
                qkv, w_down_now = ordered(qkv, w_down)
                down_weight = exchange_of(layer, w_down_now, 0)
            rows = slice(h * chunk, (h + 1) * chunk)
            q, pairs = prepare(
                qkv, cosine[rows], sine[rows], kinds_r[rows], norm_pair, heads, head_dim
            )
            queries.append(q)
            fresh.append(pairs)
        own, up_weight = ordered(jnp.concatenate(fresh, axis=1), up_weight)
        if layer == 0:
            other = jnp.where(lead, stale, lax.ppermute(own, "section", [(0, 1)]))
        else:
            other = swap(jnp.where(lead, own, stale))
        cache = to_rows(fresh)
        after = []
        for h in range(halves):
            attended = attend(queries[h], own, other, own_mask, other_mask, head_dim)
            attended = jnp.concatenate(gather_direct(attended), axis=1)
            terms = jnp.dot(attended, out_weights[layer], preferred_element_type=F32).astype(BF)
            projected = scatter_wide(by_wide(terms))
            after.append(x_in[h] + pick(table[0][..., :feat_a], kinds_h[h], 2) * projected)
        after[0], down_weight, cache = ordered(after[0], down_weight, cache)
        caches.append(cache)
        layer_in = []
        for h in range(halves):
            entry = whole_norm(after[h], table[1], kinds_h[h])
            if layer == 0 and h == 0:
                entry, w_qkv_now = ordered(entry, w_qkv)
                qkv_weight = exchange_of(1, w_qkv_now, 1)
            entry = gather_wide(entry)
            up = jnp.dot(entry, up_weight, preferred_element_type=F32)
            inner = jax.nn.gelu(up, approximate=True).astype(BF)
            if layer == 0 and h == 1:
                inner, w_up_now, qkv_weight = ordered(inner, w_up, qkv_weight)
                next_up_weight = exchange_of(1, w_up_now, 1)
            terms = jnp.dot(inner, down_weight, preferred_element_type=F32).astype(BF)
            down = scatter_wide(by_wide(terms)).astype(BF)
            down = scatter_direct([down[:, d * feat_a : (d + 1) * feat_a] for d in range(n_narrow)])
            gate = pick(table[1][..., :feat_a], kinds_h[h], 2)
            layer_in.append((after[h] + gate * down).astype(BF))
        results.append(jnp.concatenate(layer_in, axis=0))
        if layer == 0:
            up_weight = next_up_weight
    return (by_layer(results, lead), by_layer(caches, lead))


def features_split(
    hidden_in,
    row_kind,
    positions,
    timesteps,
    stale_cache,
    w_qkv,
    qk_norm,
    w_out,
    ada_weight,
    w_up,
    w_down,
):
    n_wide = lax.axis_size("wide")
    n_narrow = lax.axis_size("narrow")
    wide_idx = lax.axis_index("wide")
    narrow_idx = lax.axis_index("narrow")
    section = lax.axis_index("section")
    patch_count, rows_a, feat_a = hidden_in.shape
    total_rows = rows_a * n_wide
    rows_b = total_rows // n_narrow
    heads_local = stale_cache.shape[3]
    pair = stale_cache.shape[4]
    head_dim = pair // 2
    model_width = feat_a * n_narrow
    heads = heads_local
    lead = section == 0

    def both_layers(own):
        other = swap(own)
        return (jnp.where(lead, own, other), jnp.where(lead, other, own))

    qkv_weights = both_layers(w_qkv)
    out_weights = both_layers(w_out)
    up_weights = both_layers(w_up)
    down_weights = both_layers(w_down)
    norm_rows = both_layers(qk_norm)

    activated = jax.nn.silu(time_features(timesteps, ada_weight.shape[1])).astype(BF)
    modulation = jnp.einsum("re,kesd->krsd", activated, ada_weight, preferred_element_type=F32)
    tables = both_layers(modulation.reshape(2, 4, 3, feat_a))

    kinds = lax.dynamic_slice_in_dim(row_kind, section, 1, 0)[0]
    kinds_other = lax.dynamic_slice_in_dim(row_kind, 1 - section, 1, 0)[0]
    own_mask = key_mask(kinds, head_dim)
    other_mask = key_mask(kinds_other, head_dim)
    kinds_a = lax.dynamic_slice_in_dim(kinds, wide_idx * rows_a, rows_a)
    places = lax.dynamic_slice_in_dim(positions, section, 1, 1)[:, 0]
    places = lax.dynamic_slice_in_dim(places, narrow_idx * rows_b, rows_b, 1)
    kinds_q = lax.dynamic_slice_in_dim(kinds, narrow_idx * rows_b, rows_b)
    cosine, sine = rotary_tables(places, head_dim)

    stale = lax.all_gather(stale_cache[0, 1].transpose(1, 0, 2), "narrow", axis=1, tiled=True)

    def normalize(values):
        moments = lax.psum(
            jnp.stack([jnp.sum(values, axis=1), jnp.sum(values * values, axis=1)]), "narrow"
        )
        row_mean = moments[0] / model_width
        variance = moments[1] / model_width - row_mean * row_mean
        return (values - row_mean[:, None]) * lax.rsqrt(variance + EPS_ROW)[:, None]

    layer_in = lax.dynamic_slice_in_dim(hidden_in, section, 1, 0)[0]
    results = []
    caches = []
    for layer in range(2):
        table = tables[layer]
        x_in = layer_in.astype(F32)
        entry = modulate(normalize(x_in), table[0], kinds_a)
        qkv_terms = jnp.dot(
            lax.all_gather(entry, "wide", axis=0, tiled=True),
            qkv_weights[layer],
            preferred_element_type=F32,
        ).astype(BF)
        qkv = lax.psum_scatter(qkv_terms, "narrow", scatter_dimension=0, tiled=True)
        queries, fresh = prepare(
            qkv, cosine, sine, kinds_q, norm_pairs(norm_rows[layer]), heads, head_dim
        )
        caches.append(fresh.transpose(1, 0, 2))
        fresh = lax.all_gather(fresh, "narrow", axis=1, tiled=True)
        if layer == 0:
            other = jnp.where(lead, stale, swap(fresh))
        else:
            other = swap(jnp.where(lead, fresh, stale))
        attended = attend(queries, fresh, other, own_mask, other_mask, head_dim)
        attended = lax.all_gather(attended, "narrow", axis=0, tiled=True)
        proj_terms = jnp.dot(attended, out_weights[layer], preferred_element_type=F32).astype(BF)
        projected = lax.psum_scatter(proj_terms, "wide", scatter_dimension=0, tiled=True)
        after = x_in + pick(table[0], kinds_a, 2) * projected.astype(F32)
        entry = modulate(normalize(after), table[1], kinds_a)
        up_terms = jnp.dot(
            lax.all_gather(entry, "wide", axis=0, tiled=True),
            up_weights[layer],
            preferred_element_type=F32,
        ).astype(BF)
        up_sum = lax.psum_scatter(up_terms, "narrow", scatter_dimension=0, tiled=True)
        inner = jax.nn.gelu(up_sum.astype(F32), approximate=True).astype(BF)
        down_terms = jnp.dot(
            lax.all_gather(inner, "narrow", axis=0, tiled=True),
            down_weights[layer],
            preferred_element_type=F32,
        ).astype(BF)
        down_sum = lax.psum_scatter(down_terms, "wide", scatter_dimension=0, tiled=True)
        layer_in = (after + pick(table[1], kinds_a, 2) * down_sum.astype(F32)).astype(BF)
        results.append(layer_in)

    return (by_layer(results, lead), by_layer(caches, lead))


def solution(mesh):
    in_specs = (
        P(None, "wide", "narrow"),
        P(),
        P(),
        P(),
        P("section", None, "narrow", "wide", None),
        P("section", "narrow", "wide"),
        P("section", None, None),
        P("section", "wide", "narrow"),
        P("section", None, None, None, "narrow"),
        P("section", "narrow", "wide"),
        P("section", "wide", "narrow"),
    )
    out_specs = (P("section", None, "wide", "narrow"), P("section", None, "narrow", "wide", None))
    return jax.shard_map(
        per_device, mesh=mesh, in_specs=in_specs, out_specs=out_specs, check_vma=False
    )
```

```python
import functools

import jax
import jax.numpy as jnp
from jax import lax
from jax.experimental import pallas as pl
from jax.experimental.pallas import tpu as pltpu
from jax.sharding import PartitionSpec as P

EPS_ROW = 1e-05
EPS_HEAD = 1e-06
FAR = -1e30
LOG2E = 1.4426950408889634
BF = jnp.bfloat16
F32 = jnp.float32


def time_features(timesteps, feature_count):
    half_count = feature_count // 2
    frequency = jnp.exp(-jnp.log(10000.0) * jnp.arange(half_count, dtype=F32) / half_count)
    angle = timesteps.astype(F32)[:, None] * frequency[None, :]
    return jnp.concatenate([jnp.cos(angle), jnp.sin(angle)], axis=1)


def rotary_tables(row_positions, head_dim):
    dim_frame = head_dim // 4
    dim_plane = head_dim // 8 * 3
    pieces = []
    for axis_pos, span_dims in ((0, dim_frame), (1, dim_plane), (2, dim_plane)):
        frequency = 10000.0 ** (-jnp.arange(0, span_dims, 2, dtype=F32) / span_dims)
        pieces.append(row_positions[axis_pos].astype(F32)[:, None] * jnp.repeat(frequency, 2)[None, :])
    angles = jnp.concatenate(pieces, axis=1)
    sign = jnp.where(jnp.arange(head_dim) % 2 == 0, -1.0, 1.0).astype(F32)
    cosine = jnp.cos(angles)
    sine = jnp.sin(angles) * sign[None, :]
    return jnp.concatenate([cosine, cosine], axis=1), jnp.concatenate([sine, sine], axis=1)


def prepare_kernel(heads, head_dim, qkv_ref, cos_ref, sin_ref, kind_ref, norm_ref, q_ref, pair_ref):
    pair = 2 * head_dim
    rows = qkv_ref.shape[0]
    lane = lax.broadcasted_iota(jnp.int32, (rows, pair), 1)
    first = lane < head_dim
    even = lane % 2 == 0
    request = kind_ref[...] // 2
    mask_part = jnp.where(lane == head_dim + request, 1.0, 0.0)
    cosine = cos_ref[...]
    sine = sin_ref[...]
    gain = norm_ref[0:1, :]
    bias = norm_ref[1:2, :]
    for h in range(heads):
        base = 3 * head_dim * h
        both = qkv_ref[:, base : base + pair].astype(F32)
        key_value = qkv_ref[:, base + head_dim : base + head_dim + pair].astype(F32)
        mean_q = jnp.sum(jnp.where(first, both, 0.0), axis=1, keepdims=True) / head_dim
        mean_k = jnp.sum(jnp.where(first, 0.0, both), axis=1, keepdims=True) / head_dim
        center = both - jnp.where(first, mean_q, mean_k)
        square = center * center
        var_q = jnp.sum(jnp.where(first, square, 0.0), axis=1, keepdims=True) / head_dim
        var_k = jnp.sum(jnp.where(first, 0.0, square), axis=1, keepdims=True) / head_dim
        scale = jnp.where(first, lax.rsqrt(var_q + EPS_HEAD), lax.rsqrt(var_k + EPS_HEAD))
        normed = center * scale * gain + bias
        swapped = jnp.where(even, pltpu.roll(normed, pair - 1, 1), pltpu.roll(normed, 1, 1))
        turned = normed * cosine + swapped * sine
        q_ref[h] = jnp.where(first, turned, mask_part).astype(BF)
        pair_ref[h] = jnp.where(first, pltpu.roll(turned, head_dim, 1), key_value).astype(BF)


def prepare(qkv, cosine, sine, kinds, norm_rows, heads, head_dim):
    rows, width = qkv.shape
    block = min(256, rows)
    pair = 2 * head_dim
    return pl.pallas_call(
        functools.partial(prepare_kernel, heads, head_dim),
        grid=(rows // block,),
        in_specs=[
            pl.BlockSpec((block, width), lambda i: (i, 0)),
            pl.BlockSpec((block, pair), lambda i: (i, 0)),
            pl.BlockSpec((block, pair), lambda i: (i, 0)),
            pl.BlockSpec((block, 1), lambda i: (i, 0)),
            pl.BlockSpec((2, pair), lambda i: (0, 0)),
        ],
        out_specs=[
            pl.BlockSpec((heads, block, pair), lambda i: (0, i, 0)),
            pl.BlockSpec((heads, block, pair), lambda i: (0, i, 0)),
        ],
        out_shape=[
            jax.ShapeDtypeStruct((heads, rows, pair), BF),
            jax.ShapeDtypeStruct((heads, rows, pair), BF),
        ],
        compiler_params=pltpu.CompilerParams(vmem_limit_bytes=48 * 1024 * 1024),
        name="prepare",
    )(qkv, cosine, sine, kinds[:, None], norm_rows)


def attend_kernel(heads, head_dim, q_ref, own_ref, other_ref, own_mask_ref, other_mask_ref, out_ref):
    pair = 2 * head_dim
    keys_count = own_ref.shape[1]
    lane = lax.broadcasted_iota(jnp.int32, (keys_count, pair), 1)
    first = lane < head_dim
    one = jnp.where(lane == 0, 1.0, 0.0).astype(BF)
    factor = LOG2E * head_dim ** (-0.5)
    pieces = []
    for h in range(heads):
        queries = q_ref[h]
        own = own_ref[h]
        other = other_ref[h]
        contract = (((1,), (1,)), ((), ()))
        scores_a = lax.dot_general(
            queries, jnp.where(first, own, own_mask_ref[...]), contract, preferred_element_type=F32
        )
        scores_b = lax.dot_general(
            queries, jnp.where(first, other, other_mask_ref[...]), contract, preferred_element_type=F32
        )
        top = jnp.maximum(
            jnp.max(scores_a, axis=1, keepdims=True), jnp.max(scores_b, axis=1, keepdims=True)
        )
        weights_a = jnp.exp2((scores_a - top) * factor).astype(BF)
        weights_b = jnp.exp2((scores_b - top) * factor).astype(BF)
        mixed = jnp.dot(weights_a, jnp.where(first, one, own), preferred_element_type=F32)
        mixed += jnp.dot(weights_b, jnp.where(first, one, other), preferred_element_type=F32)
        pieces.append(mixed[:, head_dim:] / mixed[:, 0:1])
    out_ref[...] = jnp.concatenate(pieces, axis=1).astype(BF)


def attend(queries, own, other, own_mask, other_mask, head_dim):
    heads, rows, pair = queries.shape
    keys_count = own.shape[1]
    block = min(256, rows)
    whole = pl.BlockSpec((heads, keys_count, pair), lambda i: (0, 0, 0))
    mask = pl.BlockSpec((keys_count, pair), lambda i: (0, 0))
    return pl.pallas_call(
        functools.partial(attend_kernel, heads, head_dim),
        grid=(rows // block,),
        in_specs=[pl.BlockSpec((heads, block, pair), lambda i: (0, i, 0)), whole, whole, mask, mask],
        out_specs=pl.BlockSpec((block, heads * head_dim), lambda i: (i, 0)),
        out_shape=jax.ShapeDtypeStruct((rows, heads * head_dim), BF),
        compiler_params=pltpu.CompilerParams(vmem_limit_bytes=48 * 1024 * 1024),
        name="attend",
    )(queries, own, other, own_mask, other_mask)


def key_mask(kinds, head_dim):
    lane = jnp.arange(2 * head_dim)[None, :]
    foreign = (lane >= head_dim) & (lane < head_dim + 2) & (lane - head_dim != (kinds // 2)[:, None])
    return jnp.where(foreign, FAR, 0.0).astype(BF)


def pick(table, kinds, part):
    column = kinds[:, None]
    low = jnp.where(column == 0, table[0, part][None], table[1, part][None])
    high = jnp.where(column == 2, table[2, part][None], table[3, part][None])
    return jnp.where(column < 2, low, high)


def exchange(blocks, axis):
    n = lax.axis_size(axis)
    me = lax.axis_index(axis)
    got = jnp.zeros_like(blocks)
    got = lax.dynamic_update_slice_in_dim(
        got, lax.dynamic_slice_in_dim(blocks, me, 1, 0), me, 0
    )
    for step in range(1, n):
        there = (me + step) % n
        back = (me + n - step) % n
        block = lax.dynamic_slice_in_dim(blocks, there, 1, 0)
        block = lax.ppermute(block, axis, [(i, (i + step) % n) for i in range(n)])
        got = lax.dynamic_update_slice_in_dim(got, block, back, 0)
    return got


def per_device(
    hidden_in,
    row_kind,
    positions,
    timesteps,
    stale_cache,
    w_qkv,
    qk_norm,
    w_out,
    ada_weight,
    w_up,
    w_down,
):
    operands = (
        hidden_in,
        row_kind,
        positions,
        timesteps,
        stale_cache,
        w_qkv[0],
        qk_norm[0],
        w_out[0],
        ada_weight[0],
        w_up[0],
        w_down[0],
    )
    n_narrow = lax.axis_size("narrow")
    if n_narrow == 4 and lax.axis_size("wide") == 4 and stale_cache.shape[3] % n_narrow == 0:
        return in_pairs(*operands)
    return features_split(*operands)


def swap(value):
    return lax.ppermute(value, "section", [(0, 1), (1, 0)])


def by_layer(parts, lead):
    got = swap(jnp.where(lead, parts[1], parts[0]))
    kept = jnp.where(lead, parts[0], parts[1])
    return jnp.stack([jnp.where(lead, kept, got), jnp.where(lead, got, kept)])[None]


def norm_pairs(norms):
    return jnp.stack([jnp.concatenate([norms[0], norms[2]]), jnp.concatenate([norms[1], norms[3]])])


def modulate(values, table, kinds):
    return (values * (1.0 + pick(table, kinds, 1)) + pick(table, kinds, 0)).astype(BF)


def wide_pairs(step):
    return [(i, i ^ step) for i in range(lax.axis_size("wide"))]


def gather_wide(block):
    got = [lax.ppermute(block, "wide", wide_pairs(step)) for step in range(1, lax.axis_size("wide"))]
    return jnp.concatenate([block] + got, axis=0)


def scatter_wide(terms):
    total = terms[0].astype(F32)
    for step in range(1, len(terms)):
        total += lax.ppermute(terms[step], "wide", wide_pairs(step)).astype(F32)
    return total


def gather_direct(block):
    n = lax.axis_size("narrow")
    return [block] + [
        lax.ppermute(block, "narrow", [(i, (i + step) % n) for i in range(n)]) for step in range(1, n)
    ]


def to_mate(value):
    return lax.ppermute(value, "narrow", [(i, i ^ 1) for i in range(lax.axis_size("narrow"))])


def to_partner(value):
    return lax.ppermute(value, "narrow", [(i, i ^ 2) for i in range(lax.axis_size("narrow"))])


def pair_norm(values, table, kinds):
    width = values.shape[1]
    mean = jnp.mean(values, axis=1)
    center = values - mean[:, None]
    own = jnp.stack([mean, jnp.sum(center * center, axis=1)])
    far = to_partner(own)
    whole_mean = 0.5 * (own[0] + far[0])
    spread = own[1] + far[1] + width * ((own[0] - whole_mean) ** 2 + (far[0] - whole_mean) ** 2)
    scale = lax.rsqrt(spread / (2 * width) + EPS_ROW)
    return modulate((values - whole_mean[:, None]) * scale[:, None], table, kinds)


def ordered(*values):
    return lax.optimization_barrier(values)


def in_pairs(
    hidden_in,
    row_kind,
    positions,
    timesteps,
    stale_cache,
    w_qkv,
    qk_norm,
    w_out,
    ada_weight,
    w_up,
    w_down,
):
    n_wide = lax.axis_size("wide")
    n_narrow = lax.axis_size("narrow")
    wide_idx = lax.axis_index("wide")
    narrow_idx = lax.axis_index("narrow")
    section = lax.axis_index("section")
    lead = section == 0
    odd = narrow_idx % 2
    high = narrow_idx // 2
    lower = high == 0
    _, rows_a, feat_a = hidden_in.shape
    halves = 2
    part = rows_a // halves
    total_rows = rows_a * n_wide
    chunk = total_rows // halves
    rows_b = total_rows // n_narrow
    heads_local = stale_cache.shape[3]
    heads = heads_local // n_narrow
    pair = stale_cache.shape[4]
    head_dim = pair // 2
    head_group = [0, 2, 1, 3]

    def both_layers(own):
        other = swap(own)
        return (jnp.where(lead, own, other), jnp.where(lead, other, own))

    def relative(values):
        blocks = values.reshape(n_wide, halves, part)
        order = [lax.dynamic_index_in_dim(blocks, wide_idx ^ step, 0, False) for step in range(n_wide)]
        return jnp.stack(order, axis=1).reshape(total_rows)

    def qkv_part(own, parity):
        size = own.shape[1] // 4
        starts = [(2 * parity + 1 - high) * size, (2 * parity + high) * size]
        return jnp.concatenate([lax.dynamic_slice_in_dim(own, at, size, 1) for at in starts], axis=1)

    def qkv_of(layer, own):
        pairs = [(layer * n_narrow + i, layer * n_narrow + (i ^ 1)) for i in range(n_narrow)]
        got = lax.ppermute(qkv_part(own, 1 - odd), ("section", "narrow"), pairs)
        joined = jnp.concatenate([qkv_part(own, odd), got], axis=0)
        passed = lax.ppermute(joined, "section", [(layer, 1 - layer)])
        return jnp.where(section == layer, joined, passed)

    def up_of(own):
        size = own.shape[1] // 2
        got = to_mate(lax.dynamic_slice_in_dim(own, (1 - odd) * size, size, 1))
        kept = lax.dynamic_slice_in_dim(own, odd * size, size, 1)
        return both_layers(jnp.concatenate([kept, got], axis=0))

    def down_of(own):
        size = own.shape[0] // 2
        got = to_mate(lax.dynamic_slice_in_dim(own, (1 - odd) * size, size, 0))
        kept = lax.dynamic_slice_in_dim(own, odd * size, size, 0)
        return both_layers(jnp.concatenate([kept, got], axis=1))

    layer_in = lax.dynamic_index_in_dim(hidden_in, section, 0, False)
    layer_in = jnp.concatenate([layer_in, to_mate(layer_in)], axis=1)
    layer_in = [layer_in[h * part : (h + 1) * part] for h in range(halves)]
    qkv_weight = qkv_of(0, w_qkv)

    activated = jax.nn.silu(time_features(timesteps, ada_weight.shape[1])).astype(BF)
    modulation = jnp.einsum("re,kesd->krsd", activated, ada_weight, preferred_element_type=F32)
    modulation = modulation.reshape(2, 4, 3, feat_a)
    tables = both_layers(jnp.concatenate([modulation, to_mate(modulation)], axis=-1))
    norm_rows = both_layers(qk_norm)
    size = w_out.shape[0] // n_narrow
    groups = jnp.array(head_group, jnp.int32)
    starts = [groups[(narrow_idx + n_narrow - step) % n_narrow] * size for step in range(n_narrow)]
    out_weights = both_layers(
        jnp.concatenate([lax.dynamic_slice_in_dim(w_out, start, size, 0) for start in starts], axis=0)
    )

    kinds = lax.dynamic_index_in_dim(row_kind, section, 0, False)
    kinds_other = lax.dynamic_index_in_dim(row_kind, 1 - section, 0, False)
    kinds_r = relative(kinds)
    own_mask = key_mask(kinds_r, head_dim)
    other_mask = key_mask(jnp.where(lead, kinds_other, relative(kinds_other)), head_dim)
    kinds_a = lax.dynamic_slice_in_dim(kinds, wide_idx * rows_a, rows_a)
    kinds_h = [kinds_a[h * part : (h + 1) * part] for h in range(halves)]
    places = lax.dynamic_index_in_dim(positions, section, 1, False)
    places = jnp.stack([relative(places[i]) for i in range(3)])
    cosine, sine = rotary_tables(places, head_dim)

    def stale_heads(rows_part):
        blocks = rows_part.reshape(rows_b, n_narrow, heads, pair)
        blocks = jnp.stack([blocks[:, group] for group in head_group]).transpose(0, 2, 1, 3)
        got = exchange(blocks, "narrow")
        return got.transpose(1, 0, 2, 3).reshape(heads, total_rows, pair)

    def to_rows(fresh):
        blocks = [f.reshape(heads, n_wide, part, pair) for f in fresh]
        per_narrow = []
        for there in range(n_narrow):
            picked = [lax.dynamic_index_in_dim(b, wide_idx ^ there, 1, False) for b in blocks]
            per_narrow.append(jnp.concatenate(picked, axis=1))
        got = exchange(jnp.stack(per_narrow), "narrow")
        got = jnp.stack([got[sender] for sender in head_group])
        return got.transpose(2, 0, 1, 3).reshape(rows_b, heads_local, pair)

    def by_wide(terms):
        return [terms[r * part : (r + 1) * part] for r in range(n_wide)]

    results = []
    caches = []
    for layer in range(2):
        table = tables[layer]
        norm_pair = norm_pairs(norm_rows[layer])
        x_in = [block.astype(F32) for block in layer_in]
        queries = []
        fresh = []
        for h in range(halves):
            entry = pair_norm(x_in[h], table[0], kinds_h[h])
            if layer == 0 and h == 0:
                entry, w_up_now, stale = ordered(entry, w_up, stale_cache[0, 1])
                up_weights = up_of(w_up_now)
                stale = stale_heads(stale)
            entry = gather_wide(entry)
            width = qkv_weight.shape[1] // 2
            theirs = jnp.dot(entry, qkv_weight[:, :width], preferred_element_type=F32).astype(BF)
            if layer == 0 and h == 0:
                theirs, w_down_now = ordered(theirs, w_down)
                down_weights = down_of(w_down_now)
            got = to_partner(theirs)
            mine = jnp.dot(entry, qkv_weight[:, width:], preferred_element_type=F32)
            qkv = mine + got.astype(F32)
            rows = slice(h * chunk, (h + 1) * chunk)
            q, pairs = prepare(
                qkv, cosine[rows], sine[rows], kinds_r[rows], norm_pair, heads, head_dim
            )
            queries.append(q)
            fresh.append(pairs)
        own = jnp.concatenate(fresh, axis=1)
        if layer == 0:
            own, *up_weights = ordered(own, *up_weights)
            other = jnp.where(lead, stale, lax.ppermute(own, "section", [(0, 1)]))
        else:
            other = swap(jnp.where(lead, own, stale))
        after = []
        for h in range(halves):
            attended = attend(queries[h], own, other, own_mask, other_mask, head_dim)
            attended = jnp.concatenate(gather_direct(attended), axis=1)
            terms = jnp.dot(attended, out_weights[layer], preferred_element_type=F32).astype(BF)
            if h == 0:
                terms, *fresh = ordered(terms, *fresh)
                cache = to_rows(fresh)
            projected = scatter_wide(by_wide(terms)).astype(BF)
            projected = jnp.concatenate([projected, to_mate(projected)], axis=1).astype(F32)
            after.append(x_in[h] + pick(table[0], kinds_h[h], 2) * projected)
        if layer == 0:
            after[0], *down_weights = ordered(after[0], *down_weights)
        after[1], cache = ordered(after[1], cache)
        caches.append(cache)
        inner = []
        for h in range(halves):
            entry = pair_norm(after[h], table[1], kinds_h[h])
            if layer == 0 and h == 0:
                entry, w_qkv_now = ordered(entry, w_qkv)
                qkv_weight = qkv_of(1, w_qkv_now)
            up = jnp.dot(gather_wide(entry), up_weights[layer], preferred_element_type=F32).astype(BF)
            size = chunk // 2
            got = to_partner(lax.dynamic_slice_in_dim(up, (1 - high) * size, size, 0))
            up = lax.dynamic_slice_in_dim(up, high * size, size, 0).astype(F32) + got.astype(F32)
            inner.append(jax.nn.gelu(up, approximate=True).astype(BF))
        layer_in = []
        for h in range(halves):
            got = to_partner(inner[h])
            mine = jnp.dot(inner[h], down_weights[layer], preferred_element_type=F32).astype(BF)
            theirs = jnp.dot(got, down_weights[layer], preferred_element_type=F32).astype(BF)
            first = jnp.where(lower, mine, theirs)
            second = jnp.where(lower, theirs, mine)
            down = scatter_wide(by_wide(jnp.concatenate([first, second], axis=0))).astype(BF)
            far = to_mate(jnp.concatenate([down[:, feat_a:], down[:, :feat_a]], axis=1))
            down = down.astype(F32) + far.astype(F32)
            layer_in.append((after[h] + pick(table[1], kinds_h[h], 2) * down).astype(BF))
        results.append(jnp.concatenate([block[:, :feat_a] for block in layer_in], axis=0))
    return (by_layer(results, lead), by_layer(caches, lead))


def features_split(
    hidden_in,
    row_kind,
    positions,
    timesteps,
    stale_cache,
    w_qkv,
    qk_norm,
    w_out,
    ada_weight,
    w_up,
    w_down,
):
    n_wide = lax.axis_size("wide")
    n_narrow = lax.axis_size("narrow")
    wide_idx = lax.axis_index("wide")
    narrow_idx = lax.axis_index("narrow")
    section = lax.axis_index("section")
    patch_count, rows_a, feat_a = hidden_in.shape
    total_rows = rows_a * n_wide
    rows_b = total_rows // n_narrow
    heads_local = stale_cache.shape[3]
    pair = stale_cache.shape[4]
    head_dim = pair // 2
    model_width = feat_a * n_narrow
    heads = heads_local
    lead = section == 0

    def both_layers(own):
        other = swap(own)
        return (jnp.where(lead, own, other), jnp.where(lead, other, own))

    qkv_weights = both_layers(w_qkv)
    out_weights = both_layers(w_out)
    up_weights = both_layers(w_up)
    down_weights = both_layers(w_down)
    norm_rows = both_layers(qk_norm)

    activated = jax.nn.silu(time_features(timesteps, ada_weight.shape[1])).astype(BF)
    modulation = jnp.einsum("re,kesd->krsd", activated, ada_weight, preferred_element_type=F32)
    tables = both_layers(modulation.reshape(2, 4, 3, feat_a))

    kinds = lax.dynamic_slice_in_dim(row_kind, section, 1, 0)[0]
    kinds_other = lax.dynamic_slice_in_dim(row_kind, 1 - section, 1, 0)[0]
    own_mask = key_mask(kinds, head_dim)
    other_mask = key_mask(kinds_other, head_dim)
    kinds_a = lax.dynamic_slice_in_dim(kinds, wide_idx * rows_a, rows_a)
    places = lax.dynamic_slice_in_dim(positions, section, 1, 1)[:, 0]
    places = lax.dynamic_slice_in_dim(places, narrow_idx * rows_b, rows_b, 1)
    kinds_q = lax.dynamic_slice_in_dim(kinds, narrow_idx * rows_b, rows_b)
    cosine, sine = rotary_tables(places, head_dim)

    stale = lax.all_gather(stale_cache[0, 1].transpose(1, 0, 2), "narrow", axis=1, tiled=True)

    def normalize(values):
        moments = lax.psum(
            jnp.stack([jnp.sum(values, axis=1), jnp.sum(values * values, axis=1)]), "narrow"
        )
        row_mean = moments[0] / model_width
        variance = moments[1] / model_width - row_mean * row_mean
        return (values - row_mean[:, None]) * lax.rsqrt(variance + EPS_ROW)[:, None]

    layer_in = lax.dynamic_slice_in_dim(hidden_in, section, 1, 0)[0]
    results = []
    caches = []
    for layer in range(2):
        table = tables[layer]
        x_in = layer_in.astype(F32)
        entry = modulate(normalize(x_in), table[0], kinds_a)
        qkv_terms = jnp.dot(
            lax.all_gather(entry, "wide", axis=0, tiled=True),
            qkv_weights[layer],
            preferred_element_type=F32,
        ).astype(BF)
        qkv = lax.psum_scatter(qkv_terms, "narrow", scatter_dimension=0, tiled=True)
        queries, fresh = prepare(
            qkv, cosine, sine, kinds_q, norm_pairs(norm_rows[layer]), heads, head_dim
        )
        caches.append(fresh.transpose(1, 0, 2))
        fresh = lax.all_gather(fresh, "narrow", axis=1, tiled=True)
        if layer == 0:
            other = jnp.where(lead, stale, swap(fresh))
        else:
            other = swap(jnp.where(lead, fresh, stale))
        attended = attend(queries, fresh, other, own_mask, other_mask, head_dim)
        attended = lax.all_gather(attended, "narrow", axis=0, tiled=True)
        proj_terms = jnp.dot(attended, out_weights[layer], preferred_element_type=F32).astype(BF)
        projected = lax.psum_scatter(proj_terms, "wide", scatter_dimension=0, tiled=True)
        after = x_in + pick(table[0], kinds_a, 2) * projected.astype(F32)
        entry = modulate(normalize(after), table[1], kinds_a)
        up_terms = jnp.dot(
            lax.all_gather(entry, "wide", axis=0, tiled=True),
            up_weights[layer],
            preferred_element_type=F32,
        ).astype(BF)
        up_sum = lax.psum_scatter(up_terms, "narrow", scatter_dimension=0, tiled=True)
        inner = jax.nn.gelu(up_sum.astype(F32), approximate=True).astype(BF)
        down_terms = jnp.dot(
            lax.all_gather(inner, "narrow", axis=0, tiled=True),
            down_weights[layer],
            preferred_element_type=F32,
        ).astype(BF)
        down_sum = lax.psum_scatter(down_terms, "wide", scatter_dimension=0, tiled=True)
        layer_in = (after + pick(table[1], kinds_a, 2) * down_sum.astype(F32)).astype(BF)
        results.append(layer_in)

    return (by_layer(results, lead), by_layer(caches, lead))


def solution(mesh):
    in_specs = (
        P(None, "wide", "narrow"),
        P(),
        P(),
        P(),
        P("section", None, "narrow", "wide", None),
        P("section", "narrow", "wide"),
        P("section", None, None),
        P("section", "wide", "narrow"),
        P("section", None, None, None, "narrow"),
        P("section", "narrow", "wide"),
        P("section", "wide", "narrow"),
    )
    out_specs = (P("section", None, "wide", "narrow"), P("section", None, "narrow", "wide", None))
    return jax.shard_map(
        per_device, mesh=mesh, in_specs=in_specs, out_specs=out_specs, check_vma=False
    )
```

```python
import functools

import jax
import jax.numpy as jnp
from jax import lax
from jax.experimental import pallas as pl
from jax.experimental.pallas import tpu as pltpu
from jax.sharding import PartitionSpec as P

EPS_ROW = 1e-05
EPS_HEAD = 1e-06
FAR = -1e30
LOG2E = 1.4426950408889634
BF = jnp.bfloat16
F32 = jnp.float32


def time_features(timesteps, feature_count):
    half_count = feature_count // 2
    frequency = jnp.exp(-jnp.log(10000.0) * jnp.arange(half_count, dtype=F32) / half_count)
    angle = timesteps.astype(F32)[:, None] * frequency[None, :]
    return jnp.concatenate([jnp.cos(angle), jnp.sin(angle)], axis=1)


def rotary_tables(row_positions, head_dim):
    dim_frame = head_dim // 4
    dim_plane = head_dim // 8 * 3
    pieces = []
    for axis_pos, span_dims in ((0, dim_frame), (1, dim_plane), (2, dim_plane)):
        frequency = 10000.0 ** (-jnp.arange(0, span_dims, 2, dtype=F32) / span_dims)
        pieces.append(row_positions[axis_pos].astype(F32)[:, None] * jnp.repeat(frequency, 2)[None, :])
    angles = jnp.concatenate(pieces, axis=1)
    sign = jnp.where(jnp.arange(head_dim) % 2 == 0, -1.0, 1.0).astype(F32)
    cosine = jnp.cos(angles)
    sine = jnp.sin(angles) * sign[None, :]
    return jnp.concatenate([cosine, cosine], axis=1), jnp.concatenate([sine, sine], axis=1)


def prepare_kernel(heads, head_dim, qkv_ref, cos_ref, sin_ref, kind_ref, norm_ref, q_ref, pair_ref):
    pair = 2 * head_dim
    rows = qkv_ref.shape[0]
    lane = lax.broadcasted_iota(jnp.int32, (rows, pair), 1)
    first = lane < head_dim
    even = lane % 2 == 0
    request = kind_ref[...] // 2
    mask_part = jnp.where(lane == head_dim + request, 1.0, 0.0)
    cosine = cos_ref[...]
    sine = sin_ref[...]
    gain = norm_ref[0:1, :]
    bias = norm_ref[1:2, :]
    for h in range(heads):
        base = 3 * head_dim * h
        both = qkv_ref[:, base : base + pair].astype(F32)
        key_value = qkv_ref[:, base + head_dim : base + head_dim + pair].astype(F32)
        mean_q = jnp.sum(jnp.where(first, both, 0.0), axis=1, keepdims=True) / head_dim
        mean_k = jnp.sum(jnp.where(first, 0.0, both), axis=1, keepdims=True) / head_dim
        center = both - jnp.where(first, mean_q, mean_k)
        square = center * center
        var_q = jnp.sum(jnp.where(first, square, 0.0), axis=1, keepdims=True) / head_dim
        var_k = jnp.sum(jnp.where(first, 0.0, square), axis=1, keepdims=True) / head_dim
        scale = jnp.where(first, lax.rsqrt(var_q + EPS_HEAD), lax.rsqrt(var_k + EPS_HEAD))
        normed = center * scale * gain + bias
        swapped = jnp.where(even, pltpu.roll(normed, pair - 1, 1), pltpu.roll(normed, 1, 1))
        turned = normed * cosine + swapped * sine
        q_ref[h] = jnp.where(first, turned, mask_part).astype(BF)
        pair_ref[h] = jnp.where(first, pltpu.roll(turned, head_dim, 1), key_value).astype(BF)


def prepare(qkv, cosine, sine, kinds, norm_rows, heads, head_dim):
    rows, width = qkv.shape
    block = min(256, rows)
    pair = 2 * head_dim
    return pl.pallas_call(
        functools.partial(prepare_kernel, heads, head_dim),
        grid=(rows // block,),
        in_specs=[
            pl.BlockSpec((block, width), lambda i: (i, 0)),
            pl.BlockSpec((block, pair), lambda i: (i, 0)),
            pl.BlockSpec((block, pair), lambda i: (i, 0)),
            pl.BlockSpec((block, 1), lambda i: (i, 0)),
            pl.BlockSpec((2, pair), lambda i: (0, 0)),
        ],
        out_specs=[
            pl.BlockSpec((heads, block, pair), lambda i: (0, i, 0)),
            pl.BlockSpec((heads, block, pair), lambda i: (0, i, 0)),
        ],
        out_shape=[
            jax.ShapeDtypeStruct((heads, rows, pair), BF),
            jax.ShapeDtypeStruct((heads, rows, pair), BF),
        ],
        compiler_params=pltpu.CompilerParams(vmem_limit_bytes=48 * 1024 * 1024),
        name="prepare",
    )(qkv, cosine, sine, kinds[:, None], norm_rows)


def attend_kernel(heads, head_dim, q_ref, own_ref, other_ref, own_mask_ref, other_mask_ref, out_ref):
    pair = 2 * head_dim
    keys_count = own_ref.shape[1]
    lane = lax.broadcasted_iota(jnp.int32, (keys_count, pair), 1)
    first = lane < head_dim
    one = jnp.where(lane == 0, 1.0, 0.0).astype(BF)
    factor = LOG2E * head_dim ** (-0.5)
    pieces = []
    for h in range(heads):
        queries = q_ref[h]
        own = own_ref[h]
        other = other_ref[h]
        contract = (((1,), (1,)), ((), ()))
        scores_a = lax.dot_general(
            queries, jnp.where(first, own, own_mask_ref[...]), contract, preferred_element_type=F32
        )
        scores_b = lax.dot_general(
            queries, jnp.where(first, other, other_mask_ref[...]), contract, preferred_element_type=F32
        )
        top = jnp.maximum(
            jnp.max(scores_a, axis=1, keepdims=True), jnp.max(scores_b, axis=1, keepdims=True)
        )
        weights_a = jnp.exp2((scores_a - top) * factor).astype(BF)
        weights_b = jnp.exp2((scores_b - top) * factor).astype(BF)
        mixed = jnp.dot(weights_a, jnp.where(first, one, own), preferred_element_type=F32)
        mixed += jnp.dot(weights_b, jnp.where(first, one, other), preferred_element_type=F32)
        pieces.append(mixed[:, head_dim:] / mixed[:, 0:1])
    out_ref[...] = jnp.concatenate(pieces, axis=1).astype(BF)


def attend(queries, own, other, own_mask, other_mask, head_dim):
    heads, rows, pair = queries.shape
    keys_count = own.shape[1]
    block = min(256, rows)
    whole = pl.BlockSpec((heads, keys_count, pair), lambda i: (0, 0, 0))
    mask = pl.BlockSpec((keys_count, pair), lambda i: (0, 0))
    return pl.pallas_call(
        functools.partial(attend_kernel, heads, head_dim),
        grid=(rows // block,),
        in_specs=[pl.BlockSpec((heads, block, pair), lambda i: (0, i, 0)), whole, whole, mask, mask],
        out_specs=pl.BlockSpec((block, heads * head_dim), lambda i: (i, 0)),
        out_shape=jax.ShapeDtypeStruct((rows, heads * head_dim), BF),
        compiler_params=pltpu.CompilerParams(vmem_limit_bytes=48 * 1024 * 1024),
        name="attend",
    )(queries, own, other, own_mask, other_mask)


def key_mask(kinds, head_dim):
    lane = jnp.arange(2 * head_dim)[None, :]
    foreign = (lane >= head_dim) & (lane < head_dim + 2) & (lane - head_dim != (kinds // 2)[:, None])
    return jnp.where(foreign, FAR, 0.0).astype(BF)


def pick(table, kinds, part):
    column = kinds[:, None]
    low = jnp.where(column == 0, table[0, part][None], table[1, part][None])
    high = jnp.where(column == 2, table[2, part][None], table[3, part][None])
    return jnp.where(column < 2, low, high)


def exchange(blocks, axis):
    n = lax.axis_size(axis)
    me = lax.axis_index(axis)
    got = jnp.zeros_like(blocks)
    got = lax.dynamic_update_slice_in_dim(
        got, lax.dynamic_slice_in_dim(blocks, me, 1, 0), me, 0
    )
    for step in range(1, n):
        there = (me + step) % n
        back = (me + n - step) % n
        block = lax.dynamic_slice_in_dim(blocks, there, 1, 0)
        block = lax.ppermute(block, axis, [(i, (i + step) % n) for i in range(n)])
        got = lax.dynamic_update_slice_in_dim(got, block, back, 0)
    return got


def per_device(
    hidden_in,
    row_kind,
    positions,
    timesteps,
    stale_cache,
    w_qkv,
    qk_norm,
    w_out,
    ada_weight,
    w_up,
    w_down,
):
    operands = (
        hidden_in,
        row_kind,
        positions,
        timesteps,
        stale_cache,
        w_qkv[0],
        qk_norm[0],
        w_out[0],
        ada_weight[0],
        w_up[0],
        w_down[0],
    )
    n_narrow = lax.axis_size("narrow")
    if n_narrow == 4 and lax.axis_size("wide") == 4 and stale_cache.shape[3] % n_narrow == 0:
        return in_pairs(*operands)
    return features_split(*operands)


def swap(value):
    return lax.ppermute(value, "section", [(0, 1), (1, 0)])


def by_layer(parts, lead):
    got = swap(jnp.where(lead, parts[1], parts[0]))
    kept = jnp.where(lead, parts[0], parts[1])
    return jnp.stack([jnp.where(lead, kept, got), jnp.where(lead, got, kept)])[None]


def norm_pairs(norms):
    return jnp.stack([jnp.concatenate([norms[0], norms[2]]), jnp.concatenate([norms[1], norms[3]])])


def modulate(values, table, kinds):
    return (values * (1.0 + pick(table, kinds, 1)) + pick(table, kinds, 0)).astype(BF)


def wide_pairs(step):
    return [(i, i ^ step) for i in range(lax.axis_size("wide"))]


def gather_wide(block):
    got = [lax.ppermute(block, "wide", wide_pairs(step)) for step in range(1, lax.axis_size("wide"))]
    return jnp.concatenate([block] + got, axis=0)


def scatter_wide(terms):
    total = terms[0].astype(F32)
    for step in range(1, len(terms)):
        total += lax.ppermute(terms[step], "wide", wide_pairs(step)).astype(F32)
    return total


def to_mate(value):
    return lax.ppermute(value, "narrow", [(i, i ^ 1) for i in range(lax.axis_size("narrow"))])


def to_partner(value):
    return lax.ppermute(value, "narrow", [(i, i ^ 2) for i in range(lax.axis_size("narrow"))])


def statistics(values):
    width = values.shape[1]
    mean = jnp.mean(values, axis=1)
    center = values - mean[:, None]
    own = jnp.stack([mean, jnp.sum(center * center, axis=1)])
    far = to_partner(own)
    whole_mean = 0.5 * (own[0] + far[0])
    spread = own[1] + far[1] + width * ((own[0] - whole_mean) ** 2 + (far[0] - whole_mean) ** 2)
    return whole_mean, lax.rsqrt(spread / (2 * width) + EPS_ROW)


def normed(values, moments, table, kinds):
    mean, scale = moments
    return modulate((values - mean[:, None]) * scale[:, None], table, kinds)


def ordered(*values):
    return lax.optimization_barrier(values)


def in_pairs(
    hidden_in,
    row_kind,
    positions,
    timesteps,
    stale_cache,
    w_qkv,
    qk_norm,
    w_out,
    ada_weight,
    w_up,
    w_down,
):
    n_wide = lax.axis_size("wide")
    n_narrow = lax.axis_size("narrow")
    wide_idx = lax.axis_index("wide")
    narrow_idx = lax.axis_index("narrow")
    section = lax.axis_index("section")
    lead = section == 0
    odd = narrow_idx % 2
    high = narrow_idx // 2
    lower = high == 0
    _, rows_a, feat_a = hidden_in.shape
    halves = 2
    part = rows_a // halves
    total_rows = rows_a * n_wide
    chunk = total_rows // halves
    rows_b = total_rows // n_narrow
    heads_local = stale_cache.shape[3]
    heads = heads_local // n_narrow
    pair = stale_cache.shape[4]
    head_dim = pair // 2
    head_group = [0, 2, 1, 3]

    def both_layers(own):
        other = swap(own)
        return (jnp.where(lead, own, other), jnp.where(lead, other, own))

    def relative(values):
        blocks = values.reshape(n_wide, halves, part)
        order = [lax.dynamic_index_in_dim(blocks, wide_idx ^ step, 0, False) for step in range(n_wide)]
        return jnp.stack(order, axis=1).reshape(total_rows)

    def weight_of(layer, kept, sent, axis):
        pairs = [(layer * n_narrow + i, layer * n_narrow + (i ^ 1)) for i in range(n_narrow)]
        got = lax.ppermute(sent, ("section", "narrow"), pairs)
        joined = jnp.concatenate([kept, got], axis=axis)
        return joined, lax.ppermute(joined, "section", [(layer, 1 - layer)])

    def select(layer, weight):
        return jnp.where(section == layer, weight[0], weight[1])

    def two_blocks(own, axis, size, first, second):
        starts = [first * size, second * size]
        return jnp.concatenate([lax.dynamic_slice_in_dim(own, at, size, axis) for at in starts], axis=axis)

    def qkv_of(layer, own):
        size = own.shape[1] // 4
        parts = [two_blocks(own, 1, size, 2 * p + 1 - high, 2 * p + high) for p in (odd, 1 - odd)]
        return weight_of(layer, parts[0], parts[1], 0)

    def out_of(layer, own):
        size = own.shape[0] // 4
        parts = [two_blocks(own, 0, size, 2 * p + high, 2 * p + 1 - high) for p in (odd, 1 - odd)]
        return weight_of(layer, parts[0], parts[1], 1)

    def up_of(layer, own):
        size = own.shape[1] // 2
        parts = [lax.dynamic_slice_in_dim(own, p * size, size, 1) for p in (odd, 1 - odd)]
        return weight_of(layer, parts[0], parts[1], 0)

    def down_of(layer, own):
        size = own.shape[0] // 2
        parts = [lax.dynamic_slice_in_dim(own, p * size, size, 0) for p in (odd, 1 - odd)]
        return weight_of(layer, parts[0], parts[1], 1)

    layer_in = lax.dynamic_index_in_dim(hidden_in, section, 0, False)
    layer_in = jnp.concatenate([layer_in, to_mate(layer_in)], axis=1)
    first_mean, first_scale = statistics(layer_in.astype(F32))
    first_mean, w_qkv_now, stale = ordered(first_mean, w_qkv, stale_cache[0, 1])
    qkv_weight = qkv_of(0, w_qkv_now)
    layer_in = [layer_in[h * part : (h + 1) * part] for h in range(halves)]

    activated = jax.nn.silu(time_features(timesteps, ada_weight.shape[1])).astype(BF)
    modulation = jnp.einsum("re,kesd->krsd", activated, ada_weight, preferred_element_type=F32)
    modulation = modulation.reshape(2, 4, 3, feat_a)
    tables = both_layers(jnp.concatenate([modulation, to_mate(modulation)], axis=-1))
    norm_rows = both_layers(qk_norm)
    kinds = lax.dynamic_index_in_dim(row_kind, section, 0, False)
    kinds_other = lax.dynamic_index_in_dim(row_kind, 1 - section, 0, False)
    kinds_r = relative(kinds)
    own_mask = key_mask(kinds_r, head_dim)
    other_mask = key_mask(jnp.where(lead, kinds_other, relative(kinds_other)), head_dim)
    kinds_a = lax.dynamic_slice_in_dim(kinds, wide_idx * rows_a, rows_a)
    kinds_h = [kinds_a[h * part : (h + 1) * part] for h in range(halves)]
    places = lax.dynamic_index_in_dim(positions, section, 1, False)
    places = jnp.stack([relative(places[i]) for i in range(3)])
    cosine, sine = rotary_tables(places, head_dim)

    def stale_heads(rows_part):
        blocks = rows_part.reshape(rows_b, n_narrow, heads, pair)
        blocks = jnp.stack([blocks[:, group] for group in head_group]).transpose(0, 2, 1, 3)
        got = exchange(blocks, "narrow")
        return got.transpose(1, 0, 2, 3).reshape(heads, total_rows, pair)

    def to_rows(fresh):
        blocks = [f.reshape(heads, n_wide, part, pair) for f in fresh]
        per_narrow = []
        for there in range(n_narrow):
            picked = [lax.dynamic_index_in_dim(b, wide_idx ^ there, 1, False) for b in blocks]
            per_narrow.append(jnp.concatenate(picked, axis=1))
        got = exchange(jnp.stack(per_narrow), "narrow")
        got = jnp.stack([got[sender] for sender in head_group])
        return got.transpose(2, 0, 1, 3).reshape(rows_b, heads_local, pair)

    def summed(terms):
        total = scatter_wide([terms[r * part : (r + 1) * part] for r in range(n_wide)]).astype(BF)
        far = to_mate(jnp.concatenate([total[:, feat_a:], total[:, :feat_a]], axis=1))
        return total.astype(F32) + far.astype(F32)

    stale = stale_heads(stale)
    results = []
    caches = []
    for layer in range(2):
        table = tables[layer]
        norm_pair = norm_pairs(norm_rows[layer])
        x_in = [block.astype(F32) for block in layer_in]
        queries = []
        fresh = []
        for h in range(halves):
            if layer == 0:
                rows = slice(h * part, (h + 1) * part)
                moments = (first_mean[rows], first_scale[rows])
            else:
                moments = statistics(x_in[h])
            entry = normed(x_in[h], moments, table[0], kinds_h[h])
            if layer == 0 and h == 0:
                entry, w_out_now, w_up_now = ordered(entry, w_out, w_up)
                out_weight = out_of(0, w_out_now)
                up_weight = up_of(0, w_up_now)
            terms = jnp.dot(gather_wide(entry), select(layer, qkv_weight), preferred_element_type=F32)
            terms = terms.astype(BF)
            if h == 0:
                terms, w_down_now = ordered(terms, w_down)
                down_weight = down_of(layer, w_down_now)
                if layer == 0:
                    terms, stale = ordered(terms, stale)
            width = terms.shape[1] // 2
            qkv = terms[:, width:].astype(F32) + to_partner(terms[:, :width]).astype(F32)
            rows = slice(h * chunk, (h + 1) * chunk)
            q, pairs = prepare(
                qkv, cosine[rows], sine[rows], kinds_r[rows], norm_pair, heads, head_dim
            )
            queries.append(q)
            fresh.append(pairs)
        own = jnp.concatenate(fresh, axis=1)
        own, *weights = ordered(own, *out_weight, *up_weight)
        out_weight, up_weight = weights[:2], weights[2:]
        if layer == 0:
            other = jnp.where(lead, stale, lax.ppermute(own, "section", [(0, 1)]))
        else:
            other = swap(jnp.where(lead, own, stale))
        after = []
        for h in range(halves):
            attended = attend(queries[h], own, other, own_mask, other_mask, head_dim)
            attended = jnp.concatenate([attended, to_partner(attended)], axis=1)
            terms = jnp.dot(attended, select(layer, out_weight), preferred_element_type=F32).astype(BF)
            if h == 1:
                terms, *fresh = ordered(terms, *fresh)
                cache = to_rows(fresh)
            after.append(x_in[h] + pick(table[0], kinds_h[h], 2) * summed(terms))
        inner = []
        for h in range(halves):
            entry = normed(after[h], statistics(after[h]), table[1], kinds_h[h])
            if layer == 0 and h == 0:
                entry, w_qkv_now = ordered(entry, w_qkv)
                qkv_weight = qkv_of(1, w_qkv_now)
            entry = gather_wide(entry)
            up = jnp.dot(entry, select(layer, up_weight), preferred_element_type=F32).astype(BF)
            size = chunk // 2
            got = to_partner(lax.dynamic_slice_in_dim(up, (1 - high) * size, size, 0))
            up = lax.dynamic_slice_in_dim(up, high * size, size, 0).astype(F32) + got.astype(F32)
            inner.append(jax.nn.gelu(up, approximate=True).astype(BF))
        inner[0], cache, *down_weight = ordered(inner[0], cache, *down_weight)
        caches.append(cache)
        if layer == 0:
            inner[0], w_out_now, w_up_now = ordered(inner[0], w_out, w_up)
            out_weight = out_of(1, w_out_now)
            up_weight = up_of(1, w_up_now)
        layer_in = []
        for h in range(halves):
            got = to_partner(inner[h])
            first = jnp.where(lower, inner[h], got)
            second = jnp.where(lower, got, inner[h])
            whole = jnp.concatenate([first, second], axis=0)
            terms = jnp.dot(whole, select(layer, down_weight), preferred_element_type=F32).astype(BF)
            layer_in.append((after[h] + pick(table[1], kinds_h[h], 2) * summed(terms)).astype(BF))
        results.append(jnp.concatenate([block[:, :feat_a] for block in layer_in], axis=0))
    return (by_layer(results, lead), by_layer(caches, lead))


def features_split(
    hidden_in,
    row_kind,
    positions,
    timesteps,
    stale_cache,
    w_qkv,
    qk_norm,
    w_out,
    ada_weight,
    w_up,
    w_down,
):
    n_wide = lax.axis_size("wide")
    n_narrow = lax.axis_size("narrow")
    wide_idx = lax.axis_index("wide")
    narrow_idx = lax.axis_index("narrow")
    section = lax.axis_index("section")
    patch_count, rows_a, feat_a = hidden_in.shape
    total_rows = rows_a * n_wide
    rows_b = total_rows // n_narrow
    heads_local = stale_cache.shape[3]
    pair = stale_cache.shape[4]
    head_dim = pair // 2
    model_width = feat_a * n_narrow
    heads = heads_local
    lead = section == 0

    def both_layers(own):
        other = swap(own)
        return (jnp.where(lead, own, other), jnp.where(lead, other, own))

    qkv_weights = both_layers(w_qkv)
    out_weights = both_layers(w_out)
    up_weights = both_layers(w_up)
    down_weights = both_layers(w_down)
    norm_rows = both_layers(qk_norm)

    activated = jax.nn.silu(time_features(timesteps, ada_weight.shape[1])).astype(BF)
    modulation = jnp.einsum("re,kesd->krsd", activated, ada_weight, preferred_element_type=F32)
    tables = both_layers(modulation.reshape(2, 4, 3, feat_a))

    kinds = lax.dynamic_slice_in_dim(row_kind, section, 1, 0)[0]
    kinds_other = lax.dynamic_slice_in_dim(row_kind, 1 - section, 1, 0)[0]
    own_mask = key_mask(kinds, head_dim)
    other_mask = key_mask(kinds_other, head_dim)
    kinds_a = lax.dynamic_slice_in_dim(kinds, wide_idx * rows_a, rows_a)
    places = lax.dynamic_slice_in_dim(positions, section, 1, 1)[:, 0]
    places = lax.dynamic_slice_in_dim(places, narrow_idx * rows_b, rows_b, 1)
    kinds_q = lax.dynamic_slice_in_dim(kinds, narrow_idx * rows_b, rows_b)
    cosine, sine = rotary_tables(places, head_dim)

    stale = lax.all_gather(stale_cache[0, 1].transpose(1, 0, 2), "narrow", axis=1, tiled=True)

    def normalize(values):
        moments = lax.psum(
            jnp.stack([jnp.sum(values, axis=1), jnp.sum(values * values, axis=1)]), "narrow"
        )
        row_mean = moments[0] / model_width
        variance = moments[1] / model_width - row_mean * row_mean
        return (values - row_mean[:, None]) * lax.rsqrt(variance + EPS_ROW)[:, None]

    layer_in = lax.dynamic_slice_in_dim(hidden_in, section, 1, 0)[0]
    results = []
    caches = []
    for layer in range(2):
        table = tables[layer]
        x_in = layer_in.astype(F32)
        entry = modulate(normalize(x_in), table[0], kinds_a)
        qkv_terms = jnp.dot(
            lax.all_gather(entry, "wide", axis=0, tiled=True),
            qkv_weights[layer],
            preferred_element_type=F32,
        ).astype(BF)
        qkv = lax.psum_scatter(qkv_terms, "narrow", scatter_dimension=0, tiled=True)
        queries, fresh = prepare(
            qkv, cosine, sine, kinds_q, norm_pairs(norm_rows[layer]), heads, head_dim
        )
        caches.append(fresh.transpose(1, 0, 2))
        fresh = lax.all_gather(fresh, "narrow", axis=1, tiled=True)
        if layer == 0:
            other = jnp.where(lead, stale, swap(fresh))
        else:
            other = swap(jnp.where(lead, fresh, stale))
        attended = attend(queries, fresh, other, own_mask, other_mask, head_dim)
        attended = lax.all_gather(attended, "narrow", axis=0, tiled=True)
        proj_terms = jnp.dot(attended, out_weights[layer], preferred_element_type=F32).astype(BF)
        projected = lax.psum_scatter(proj_terms, "wide", scatter_dimension=0, tiled=True)
        after = x_in + pick(table[0], kinds_a, 2) * projected.astype(F32)
        entry = modulate(normalize(after), table[1], kinds_a)
        up_terms = jnp.dot(
            lax.all_gather(entry, "wide", axis=0, tiled=True),
            up_weights[layer],
            preferred_element_type=F32,
        ).astype(BF)
        up_sum = lax.psum_scatter(up_terms, "narrow", scatter_dimension=0, tiled=True)
        inner = jax.nn.gelu(up_sum.astype(F32), approximate=True).astype(BF)
        down_terms = jnp.dot(
            lax.all_gather(inner, "narrow", axis=0, tiled=True),
            down_weights[layer],
            preferred_element_type=F32,
        ).astype(BF)
        down_sum = lax.psum_scatter(down_terms, "wide", scatter_dimension=0, tiled=True)
        layer_in = (after + pick(table[1], kinds_a, 2) * down_sum.astype(F32)).astype(BF)
        results.append(layer_in)

    return (by_layer(results, lead), by_layer(caches, lead))


def solution(mesh):
    in_specs = (
        P(None, "wide", "narrow"),
        P(),
        P(),
        P(),
        P("section", None, "narrow", "wide", None),
        P("section", "narrow", "wide"),
        P("section", None, None),
        P("section", "wide", "narrow"),
        P("section", None, None, None, "narrow"),
        P("section", "narrow", "wide"),
        P("section", "wide", "narrow"),
    )
    out_specs = (P("section", None, "wide", "narrow"), P("section", None, "narrow", "wide", None))
    return jax.shard_map(
        per_device, mesh=mesh, in_specs=in_specs, out_specs=out_specs, check_vma=False
    )
```

```python
import functools

import jax
import jax.numpy as jnp
from jax import lax
from jax.experimental import pallas as pl
from jax.experimental.pallas import tpu as pltpu
from jax.sharding import PartitionSpec as P

EPS_ROW = 1e-05
EPS_HEAD = 1e-06
FAR = -1e30
LOG2E = 1.4426950408889634
BF = jnp.bfloat16
F32 = jnp.float32


def time_features(timesteps, feature_count):
    half_count = feature_count // 2
    frequency = jnp.exp(-jnp.log(10000.0) * jnp.arange(half_count, dtype=F32) / half_count)
    angle = timesteps.astype(F32)[:, None] * frequency[None, :]
    return jnp.concatenate([jnp.cos(angle), jnp.sin(angle)], axis=1)


def rotary_tables(row_positions, head_dim):
    dim_frame = head_dim // 4
    dim_plane = head_dim // 8 * 3
    pieces = []
    for axis_pos, span_dims in ((0, dim_frame), (1, dim_plane), (2, dim_plane)):
        frequency = 10000.0 ** (-jnp.arange(0, span_dims, 2, dtype=F32) / span_dims)
        pieces.append(row_positions[axis_pos].astype(F32)[:, None] * jnp.repeat(frequency, 2)[None, :])
    angles = jnp.concatenate(pieces, axis=1)
    sign = jnp.where(jnp.arange(head_dim) % 2 == 0, -1.0, 1.0).astype(F32)
    cosine = jnp.cos(angles)
    sine = jnp.sin(angles) * sign[None, :]
    return jnp.concatenate([cosine, cosine], axis=1), jnp.concatenate([sine, sine], axis=1)


def prepare_kernel(heads, head_dim, qkv_ref, cos_ref, sin_ref, kind_ref, norm_ref, q_ref, pair_ref):
    pair = 2 * head_dim
    rows = qkv_ref.shape[0]
    lane = lax.broadcasted_iota(jnp.int32, (rows, pair), 1)
    first = lane < head_dim
    even = lane % 2 == 0
    request = kind_ref[...] // 2
    mask_part = jnp.where(lane == head_dim + request, 1.0, 0.0)
    cosine = cos_ref[...]
    sine = sin_ref[...]
    gain = norm_ref[0:1, :]
    bias = norm_ref[1:2, :]
    for h in range(heads):
        base = 3 * head_dim * h
        both = qkv_ref[:, base : base + pair].astype(F32)
        key_value = qkv_ref[:, base + head_dim : base + head_dim + pair].astype(F32)
        mean_q = jnp.sum(jnp.where(first, both, 0.0), axis=1, keepdims=True) / head_dim
        mean_k = jnp.sum(jnp.where(first, 0.0, both), axis=1, keepdims=True) / head_dim
        center = both - jnp.where(first, mean_q, mean_k)
        square = center * center
        var_q = jnp.sum(jnp.where(first, square, 0.0), axis=1, keepdims=True) / head_dim
        var_k = jnp.sum(jnp.where(first, 0.0, square), axis=1, keepdims=True) / head_dim
        scale = jnp.where(first, lax.rsqrt(var_q + EPS_HEAD), lax.rsqrt(var_k + EPS_HEAD))
        normed = center * scale * gain + bias
        swapped = jnp.where(even, pltpu.roll(normed, pair - 1, 1), pltpu.roll(normed, 1, 1))
        turned = normed * cosine + swapped * sine
        q_ref[h] = jnp.where(first, turned, mask_part).astype(BF)
        pair_ref[h] = jnp.where(first, pltpu.roll(turned, head_dim, 1), key_value).astype(BF)


def prepare(qkv, cosine, sine, kinds, norm_rows, heads, head_dim):
    rows, width = qkv.shape
    block = min(256, rows)
    pair = 2 * head_dim
    return pl.pallas_call(
        functools.partial(prepare_kernel, heads, head_dim),
        grid=(rows // block,),
        in_specs=[
            pl.BlockSpec((block, width), lambda i: (i, 0)),
            pl.BlockSpec((block, pair), lambda i: (i, 0)),
            pl.BlockSpec((block, pair), lambda i: (i, 0)),
            pl.BlockSpec((block, 1), lambda i: (i, 0)),
            pl.BlockSpec((2, pair), lambda i: (0, 0)),
        ],
        out_specs=[
            pl.BlockSpec((heads, block, pair), lambda i: (0, i, 0)),
            pl.BlockSpec((heads, block, pair), lambda i: (0, i, 0)),
        ],
        out_shape=[
            jax.ShapeDtypeStruct((heads, rows, pair), BF),
            jax.ShapeDtypeStruct((heads, rows, pair), BF),
        ],
        compiler_params=pltpu.CompilerParams(vmem_limit_bytes=48 * 1024 * 1024),
        name="prepare",
    )(qkv, cosine, sine, kinds[:, None], norm_rows)


def attend_kernel(heads, head_dim, q_ref, own_ref, other_ref, own_mask_ref, other_mask_ref, out_ref):
    pair = 2 * head_dim
    keys_count = own_ref.shape[1]
    lane = lax.broadcasted_iota(jnp.int32, (keys_count, pair), 1)
    first = lane < head_dim
    one = jnp.where(lane == 0, 1.0, 0.0).astype(BF)
    factor = LOG2E * head_dim ** (-0.5)
    pieces = []
    for h in range(heads):
        queries = q_ref[h]
        own = own_ref[h]
        other = other_ref[h]
        contract = (((1,), (1,)), ((), ()))
        scores_a = lax.dot_general(
            queries, jnp.where(first, own, own_mask_ref[...]), contract, preferred_element_type=F32
        )
        scores_b = lax.dot_general(
            queries, jnp.where(first, other, other_mask_ref[...]), contract, preferred_element_type=F32
        )
        top = jnp.maximum(
            jnp.max(scores_a, axis=1, keepdims=True), jnp.max(scores_b, axis=1, keepdims=True)
        )
        weights_a = jnp.exp2((scores_a - top) * factor).astype(BF)
        weights_b = jnp.exp2((scores_b - top) * factor).astype(BF)
        mixed = jnp.dot(weights_a, jnp.where(first, one, own), preferred_element_type=F32)
        mixed += jnp.dot(weights_b, jnp.where(first, one, other), preferred_element_type=F32)
        pieces.append(mixed[:, head_dim:] / mixed[:, 0:1])
    out_ref[...] = jnp.concatenate(pieces, axis=1).astype(BF)


def attend(queries, own, other, own_mask, other_mask, head_dim):
    heads, rows, pair = queries.shape
    keys_count = own.shape[1]
    block = min(256, rows)
    whole = pl.BlockSpec((heads, keys_count, pair), lambda i: (0, 0, 0))
    mask = pl.BlockSpec((keys_count, pair), lambda i: (0, 0))
    return pl.pallas_call(
        functools.partial(attend_kernel, heads, head_dim),
        grid=(rows // block,),
        in_specs=[pl.BlockSpec((heads, block, pair), lambda i: (0, i, 0)), whole, whole, mask, mask],
        out_specs=pl.BlockSpec((block, heads * head_dim), lambda i: (i, 0)),
        out_shape=jax.ShapeDtypeStruct((rows, heads * head_dim), BF),
        compiler_params=pltpu.CompilerParams(vmem_limit_bytes=48 * 1024 * 1024),
        name="attend",
    )(queries, own, other, own_mask, other_mask)


def key_mask(kinds, head_dim):
    lane = jnp.arange(2 * head_dim)[None, :]
    foreign = (lane >= head_dim) & (lane < head_dim + 2) & (lane - head_dim != (kinds // 2)[:, None])
    return jnp.where(foreign, FAR, 0.0).astype(BF)


def pick(table, kinds, part):
    column = kinds[:, None]
    low = jnp.where(column == 0, table[0, part][None], table[1, part][None])
    high = jnp.where(column == 2, table[2, part][None], table[3, part][None])
    return jnp.where(column < 2, low, high)


def exchange(blocks, axis):
    n = lax.axis_size(axis)
    me = lax.axis_index(axis)
    got = jnp.zeros_like(blocks)
    got = lax.dynamic_update_slice_in_dim(
        got, lax.dynamic_slice_in_dim(blocks, me, 1, 0), me, 0
    )
    for step in range(1, n):
        there = (me + step) % n
        back = (me + n - step) % n
        block = lax.dynamic_slice_in_dim(blocks, there, 1, 0)
        block = lax.ppermute(block, axis, [(i, (i + step) % n) for i in range(n)])
        got = lax.dynamic_update_slice_in_dim(got, block, back, 0)
    return got


def per_device(
    hidden_in,
    row_kind,
    positions,
    timesteps,
    stale_cache,
    w_qkv,
    qk_norm,
    w_out,
    ada_weight,
    w_up,
    w_down,
):
    operands = (
        hidden_in,
        row_kind,
        positions,
        timesteps,
        stale_cache,
        w_qkv[0],
        qk_norm[0],
        w_out[0],
        ada_weight[0],
        w_up[0],
        w_down[0],
    )
    n_narrow = lax.axis_size("narrow")
    if n_narrow == 4 and lax.axis_size("wide") == 4 and stale_cache.shape[3] % n_narrow == 0:
        return in_pairs(*operands)
    return features_split(*operands)


def swap(value):
    return lax.ppermute(value, "section", [(0, 1), (1, 0)])


def by_layer(parts, lead):
    got = swap(jnp.where(lead, parts[1], parts[0]))
    kept = jnp.where(lead, parts[0], parts[1])
    return jnp.stack([jnp.where(lead, kept, got), jnp.where(lead, got, kept)])[None]


def norm_pairs(norms):
    return jnp.stack([jnp.concatenate([norms[0], norms[2]]), jnp.concatenate([norms[1], norms[3]])])


def modulate(values, table, kinds):
    return (values * (1.0 + pick(table, kinds, 1)) + pick(table, kinds, 0)).astype(BF)


def wide_pairs(step):
    return [(i, i ^ step) for i in range(lax.axis_size("wide"))]


def gather_wide(block):
    got = [lax.ppermute(block, "wide", wide_pairs(step)) for step in range(1, lax.axis_size("wide"))]
    return jnp.concatenate([block] + got, axis=0)


def scatter_wide(terms):
    total = terms[0].astype(F32)
    for step in range(1, len(terms)):
        total += lax.ppermute(terms[step], "wide", wide_pairs(step)).astype(F32)
    return total


def to_mate(value):
    return lax.ppermute(value, "narrow", [(i, i ^ 1) for i in range(lax.axis_size("narrow"))])


def to_partner(value):
    return lax.ppermute(value, "narrow", [(i, i ^ 2) for i in range(lax.axis_size("narrow"))])


def statistics(values):
    width = values.shape[1]
    mean = jnp.mean(values, axis=1)
    center = values - mean[:, None]
    own = jnp.stack([mean, jnp.sum(center * center, axis=1)])
    far = to_partner(own)
    whole_mean = 0.5 * (own[0] + far[0])
    spread = own[1] + far[1] + width * ((own[0] - whole_mean) ** 2 + (far[0] - whole_mean) ** 2)
    return whole_mean, lax.rsqrt(spread / (2 * width) + EPS_ROW)


def normed(values, moments, table, kinds):
    mean, scale = moments
    return modulate((values - mean[:, None]) * scale[:, None], table, kinds)


def ordered(*values):
    return lax.optimization_barrier(values)


def in_pairs(
    hidden_in,
    row_kind,
    positions,
    timesteps,
    stale_cache,
    w_qkv,
    qk_norm,
    w_out,
    ada_weight,
    w_up,
    w_down,
):
    n_wide = lax.axis_size("wide")
    n_narrow = lax.axis_size("narrow")
    wide_idx = lax.axis_index("wide")
    narrow_idx = lax.axis_index("narrow")
    section = lax.axis_index("section")
    lead = section == 0
    odd = narrow_idx % 2
    high = narrow_idx // 2
    lower = high == 0
    _, rows_a, feat_a = hidden_in.shape
    halves = 2
    part = rows_a // halves
    total_rows = rows_a * n_wide
    chunk = total_rows // halves
    rows_b = total_rows // n_narrow
    heads_local = stale_cache.shape[3]
    heads = heads_local // n_narrow
    pair = stale_cache.shape[4]
    head_dim = pair // 2
    head_group = [0, 2, 1, 3]

    def both_layers(own):
        other = swap(own)
        return (jnp.where(lead, own, other), jnp.where(lead, other, own))

    def relative(values):
        blocks = values.reshape(n_wide, halves, part)
        order = [lax.dynamic_index_in_dim(blocks, wide_idx ^ step, 0, False) for step in range(n_wide)]
        return jnp.stack(order, axis=1).reshape(total_rows)

    def mate_half(layer, sent):
        pairs = [(layer * n_narrow + i, layer * n_narrow + (i ^ 1)) for i in range(n_narrow)]
        return lax.ppermute(sent, ("section", "narrow"), pairs)

    def passed(layer, value):
        return lax.ppermute(value, "section", [(layer, 1 - layer)])

    def pass_on(layer, kept, got, axis):
        joined = jnp.concatenate([kept, got], axis=axis)
        return joined, passed(layer, joined)

    def weight_of(layer, parts, axis):
        return pass_on(layer, parts[0], mate_half(layer, parts[1]), axis)

    def select(layer, weight):
        return jnp.where(section == layer, weight[0], weight[1])

    def two_blocks(own, axis, size, first, second):
        starts = [first * size, second * size]
        return jnp.concatenate([lax.dynamic_slice_in_dim(own, at, size, axis) for at in starts], axis=axis)

    size = w_qkv.shape[1] // 4
    qkv_parts = [two_blocks(w_qkv, 1, size, 2 * p + 1 - high, 2 * p + high) for p in (odd, 1 - odd)]
    size = w_out.shape[0] // 4
    out_parts = [two_blocks(w_out, 0, size, 2 * p + high, 2 * p + 1 - high) for p in (odd, 1 - odd)]
    size = w_up.shape[1] // 2
    up_parts = [lax.dynamic_slice_in_dim(w_up, p * size, size, 1) for p in (odd, 1 - odd)]
    size = w_down.shape[0] // 2
    down_parts = [lax.dynamic_slice_in_dim(w_down, p * size, size, 0) for p in (odd, 1 - odd)]

    def ordered_parts(value, parts):
        value, sent = ordered(value, parts[1])
        return value, (parts[0], sent)

    layer_in = lax.dynamic_index_in_dim(hidden_in, section, 0, False)
    layer_in = jnp.concatenate([layer_in, to_mate(layer_in)], axis=1)
    layer_in, sent, timesteps, stale = ordered(layer_in, qkv_parts[1], timesteps, stale_cache[0, 1])
    got = mate_half(0, sent)
    kept = passed(0, qkv_parts[0])
    layer_in, kept = ordered(layer_in, kept)
    qkv_now = jnp.concatenate(
        [
            jnp.where(lead, qkv_parts[0], kept),
            jnp.where(lead, got, passed(0, got)),
        ],
        axis=0,
    )
    first_mean, first_scale = statistics(layer_in.astype(F32))
    layer_in = [layer_in[h * part : (h + 1) * part] for h in range(halves)]

    activated = jax.nn.silu(time_features(timesteps, ada_weight.shape[1])).astype(BF)
    modulation = jnp.einsum("re,kesd->krsd", activated, ada_weight, preferred_element_type=F32)
    modulation = modulation.reshape(2, 4, 3, feat_a)
    modulation = jnp.concatenate([modulation, to_mate(modulation)], axis=-1)
    shape = modulation.shape
    width = shape[-1]
    rows = modulation.reshape(-1, width)
    last = jnp.concatenate([qk_norm.reshape(-1), jnp.zeros((width - qk_norm.size,), F32)])
    both = both_layers(jnp.concatenate([rows, last[None]], axis=0))
    tables = [table[:-1].reshape(shape) for table in both]
    norm_rows = [table[-1, : qk_norm.size].reshape(qk_norm.shape) for table in both]
    kinds = lax.dynamic_index_in_dim(row_kind, section, 0, False)
    kinds_other = lax.dynamic_index_in_dim(row_kind, 1 - section, 0, False)
    kinds_r = relative(kinds)
    own_mask = key_mask(kinds_r, head_dim)
    other_mask = key_mask(jnp.where(lead, kinds_other, relative(kinds_other)), head_dim)
    kinds_a = lax.dynamic_slice_in_dim(kinds, wide_idx * rows_a, rows_a)
    kinds_h = [kinds_a[h * part : (h + 1) * part] for h in range(halves)]
    places = lax.dynamic_index_in_dim(positions, section, 1, False)
    places = jnp.stack([relative(places[i]) for i in range(3)])
    cosine, sine = rotary_tables(places, head_dim)

    def stale_heads(rows_part):
        blocks = rows_part.reshape(rows_b, n_narrow, heads, pair)
        blocks = jnp.stack([blocks[:, group] for group in head_group]).transpose(0, 2, 1, 3)
        got = exchange(blocks, "narrow")
        return got.transpose(1, 0, 2, 3).reshape(heads, total_rows, pair)

    def to_rows(fresh):
        blocks = [f.reshape(heads, n_wide, part, pair) for f in fresh]
        per_narrow = []
        for there in range(n_narrow):
            picked = [lax.dynamic_index_in_dim(b, wide_idx ^ there, 1, False) for b in blocks]
            per_narrow.append(jnp.concatenate(picked, axis=1))
        got = exchange(jnp.stack(per_narrow), "narrow")
        got = jnp.stack([got[sender] for sender in head_group])
        return got.transpose(2, 0, 1, 3).reshape(rows_b, heads_local, pair)

    def summed(terms):
        total = scatter_wide([terms[r * part : (r + 1) * part] for r in range(n_wide)]).astype(BF)
        far = to_mate(jnp.concatenate([total[:, feat_a:], total[:, :feat_a]], axis=1))
        return total.astype(F32) + far.astype(F32)

    results = []
    caches = []
    for layer in range(2):
        table = tables[layer]
        norm_pair = norm_pairs(norm_rows[layer])
        x_in = [block.astype(F32) for block in layer_in]
        queries = []
        fresh = []
        for h in range(halves):
            if layer == 0:
                rows = slice(h * part, (h + 1) * part)
                moments = (first_mean[rows], first_scale[rows])
            else:
                moments = statistics(x_in[h])
            entry = normed(x_in[h], moments, table[0], kinds_h[h])
            if layer == 0 and h == 0:
                entry, stale = ordered(entry, stale_heads(stale))
            terms = jnp.dot(gather_wide(entry), qkv_now, preferred_element_type=F32).astype(BF)
            if layer == 0 and h == 0:
                terms, out_sent, up_sent = ordered(terms, out_parts[1], up_parts[1])
                out_got, up_got = mate_half(0, out_sent), mate_half(0, up_sent)
            if layer == 0 and h == 1:
                terms, out_got, up_got = ordered(terms, out_got, up_got)
                out_weight = pass_on(0, out_parts[0], out_got, 1)
                up_weight = pass_on(0, up_parts[0], up_got, 0)
            width = terms.shape[1] // 2
            qkv = terms[:, width:].astype(F32) + to_partner(terms[:, :width]).astype(F32)
            rows = slice(h * chunk, (h + 1) * chunk)
            q, pairs = prepare(
                qkv, cosine[rows], sine[rows], kinds_r[rows], norm_pair, heads, head_dim
            )
            queries.append(q)
            fresh.append(pairs)
        own = jnp.concatenate(fresh, axis=1)
        own, *weights = ordered(own, *out_weight, *up_weight)
        out_weight, up_weight = weights[:2], weights[2:]
        if layer == 0:
            other = jnp.where(lead, stale, lax.ppermute(own, "section", [(0, 1)]))
        else:
            other = swap(jnp.where(lead, own, stale))
        after = []
        for h in range(halves):
            attended = attend(queries[h], own, other, own_mask, other_mask, head_dim)
            if h == 1:
                attended, first_terms = ordered(attended, first_terms)
            attended = jnp.concatenate([attended, to_partner(attended)], axis=1)
            terms = jnp.dot(attended, select(layer, out_weight), preferred_element_type=F32).astype(BF)
            if h == 0:
                first_terms = terms
            else:
                terms, *fresh = ordered(terms, *fresh)
                cache = to_rows(fresh)
            after.append(x_in[h] + pick(table[0], kinds_h[h], 2) * summed(terms))
        after[0], cache = ordered(after[0], cache)
        caches.append(cache)
        inner = []
        mean, scale = statistics(jnp.concatenate(after, axis=0))
        for h in range(halves):
            rows = slice(h * part, (h + 1) * part)
            entry = normed(after[h], (mean[rows], scale[rows]), table[1], kinds_h[h])
            if layer == 0 and h == 0:
                entry, parts = ordered_parts(entry, qkv_parts)
                qkv_weight = weight_of(1, parts, 0)
            if h == 0:
                entry, down_sent = ordered(entry, down_parts[1])
                down_got = mate_half(layer, down_sent)
            entry = gather_wide(entry)
            up = jnp.dot(entry, select(layer, up_weight), preferred_element_type=F32).astype(BF)
            if h == 1:
                up, down_got = ordered(up, down_got)
                down_weight = pass_on(layer, down_parts[0], down_got, 1)
            size = chunk // 2
            got = to_partner(lax.dynamic_slice_in_dim(up, (1 - high) * size, size, 0))
            up = lax.dynamic_slice_in_dim(up, high * size, size, 0).astype(F32) + got.astype(F32)
            inner.append(jax.nn.gelu(up, approximate=True).astype(BF))
        inner[0], *down_weight = ordered(inner[0], *down_weight)
        if layer == 0:
            inner[0], parts = ordered_parts(inner[0], out_parts)
            out_weight = weight_of(1, parts, 1)
            inner[0], parts = ordered_parts(inner[0], up_parts)
            up_weight = weight_of(1, parts, 0)
            qkv_now = select(1, qkv_weight)
        layer_in = []
        for h in range(halves):
            got = to_partner(inner[h])
            first = jnp.where(lower, inner[h], got)
            second = jnp.where(lower, got, inner[h])
            whole = jnp.concatenate([first, second], axis=0)
            terms = jnp.dot(whole, select(layer, down_weight), preferred_element_type=F32).astype(BF)
            layer_in.append((after[h] + pick(table[1], kinds_h[h], 2) * summed(terms)).astype(BF))
        results.append(jnp.concatenate([block[:, :feat_a] for block in layer_in], axis=0))
    return (by_layer(results, lead), by_layer(caches, lead))


def features_split(
    hidden_in,
    row_kind,
    positions,
    timesteps,
    stale_cache,
    w_qkv,
    qk_norm,
    w_out,
    ada_weight,
    w_up,
    w_down,
):
    n_wide = lax.axis_size("wide")
    n_narrow = lax.axis_size("narrow")
    wide_idx = lax.axis_index("wide")
    narrow_idx = lax.axis_index("narrow")
    section = lax.axis_index("section")
    patch_count, rows_a, feat_a = hidden_in.shape
    total_rows = rows_a * n_wide
    rows_b = total_rows // n_narrow
    heads_local = stale_cache.shape[3]
    pair = stale_cache.shape[4]
    head_dim = pair // 2
    model_width = feat_a * n_narrow
    heads = heads_local
    lead = section == 0

    def both_layers(own):
        other = swap(own)
        return (jnp.where(lead, own, other), jnp.where(lead, other, own))

    qkv_weights = both_layers(w_qkv)
    out_weights = both_layers(w_out)
    up_weights = both_layers(w_up)
    down_weights = both_layers(w_down)
    norm_rows = both_layers(qk_norm)

    activated = jax.nn.silu(time_features(timesteps, ada_weight.shape[1])).astype(BF)
    modulation = jnp.einsum("re,kesd->krsd", activated, ada_weight, preferred_element_type=F32)
    tables = both_layers(modulation.reshape(2, 4, 3, feat_a))

    kinds = lax.dynamic_slice_in_dim(row_kind, section, 1, 0)[0]
    kinds_other = lax.dynamic_slice_in_dim(row_kind, 1 - section, 1, 0)[0]
    own_mask = key_mask(kinds, head_dim)
    other_mask = key_mask(kinds_other, head_dim)
    kinds_a = lax.dynamic_slice_in_dim(kinds, wide_idx * rows_a, rows_a)
    places = lax.dynamic_slice_in_dim(positions, section, 1, 1)[:, 0]
    places = lax.dynamic_slice_in_dim(places, narrow_idx * rows_b, rows_b, 1)
    kinds_q = lax.dynamic_slice_in_dim(kinds, narrow_idx * rows_b, rows_b)
    cosine, sine = rotary_tables(places, head_dim)

    stale = lax.all_gather(stale_cache[0, 1].transpose(1, 0, 2), "narrow", axis=1, tiled=True)

    def normalize(values):
        moments = lax.psum(
            jnp.stack([jnp.sum(values, axis=1), jnp.sum(values * values, axis=1)]), "narrow"
        )
        row_mean = moments[0] / model_width
        variance = moments[1] / model_width - row_mean * row_mean
        return (values - row_mean[:, None]) * lax.rsqrt(variance + EPS_ROW)[:, None]

    layer_in = lax.dynamic_slice_in_dim(hidden_in, section, 1, 0)[0]
    results = []
    caches = []
    for layer in range(2):
        table = tables[layer]
        x_in = layer_in.astype(F32)
        entry = modulate(normalize(x_in), table[0], kinds_a)
        qkv_terms = jnp.dot(
            lax.all_gather(entry, "wide", axis=0, tiled=True),
            qkv_weights[layer],
            preferred_element_type=F32,
        ).astype(BF)
        qkv = lax.psum_scatter(qkv_terms, "narrow", scatter_dimension=0, tiled=True)
        queries, fresh = prepare(
            qkv, cosine, sine, kinds_q, norm_pairs(norm_rows[layer]), heads, head_dim
        )
        caches.append(fresh.transpose(1, 0, 2))
        fresh = lax.all_gather(fresh, "narrow", axis=1, tiled=True)
        if layer == 0:
            other = jnp.where(lead, stale, swap(fresh))
        else:
            other = swap(jnp.where(lead, fresh, stale))
        attended = attend(queries, fresh, other, own_mask, other_mask, head_dim)
        attended = lax.all_gather(attended, "narrow", axis=0, tiled=True)
        proj_terms = jnp.dot(attended, out_weights[layer], preferred_element_type=F32).astype(BF)
        projected = lax.psum_scatter(proj_terms, "wide", scatter_dimension=0, tiled=True)
        after = x_in + pick(table[0], kinds_a, 2) * projected.astype(F32)
        entry = modulate(normalize(after), table[1], kinds_a)
        up_terms = jnp.dot(
            lax.all_gather(entry, "wide", axis=0, tiled=True),
            up_weights[layer],
            preferred_element_type=F32,
        ).astype(BF)
        up_sum = lax.psum_scatter(up_terms, "narrow", scatter_dimension=0, tiled=True)
        inner = jax.nn.gelu(up_sum.astype(F32), approximate=True).astype(BF)
        down_terms = jnp.dot(
            lax.all_gather(inner, "narrow", axis=0, tiled=True),
            down_weights[layer],
            preferred_element_type=F32,
        ).astype(BF)
        down_sum = lax.psum_scatter(down_terms, "wide", scatter_dimension=0, tiled=True)
        layer_in = (after + pick(table[1], kinds_a, 2) * down_sum.astype(F32)).astype(BF)
        results.append(layer_in)

    return (by_layer(results, lead), by_layer(caches, lead))


def solution(mesh):
    in_specs = (
        P(None, "wide", "narrow"),
        P(),
        P(),
        P(),
        P("section", None, "narrow", "wide", None),
        P("section", "narrow", "wide"),
        P("section", None, None),
        P("section", "wide", "narrow"),
        P("section", None, None, None, "narrow"),
        P("section", "narrow", "wide"),
        P("section", "wide", "narrow"),
    )
    out_specs = (P("section", None, "wide", "narrow"), P("section", None, "narrow", "wide", None))
    return jax.shard_map(
        per_device, mesh=mesh, in_specs=in_specs, out_specs=out_specs, check_vma=False
    )
```

```python
import functools

import jax
import jax.numpy as jnp
from jax import lax
from jax.experimental import pallas as pl
from jax.experimental.pallas import tpu as pltpu
from jax.sharding import PartitionSpec as P

EPS_ROW = 1e-05
EPS_HEAD = 1e-06
FAR = -1e30
LOG2E = 1.4426950408889634
BF = jnp.bfloat16
F32 = jnp.float32


def time_features(timesteps, feature_count):
    half_count = feature_count // 2
    frequency = jnp.exp(-jnp.log(10000.0) * jnp.arange(half_count, dtype=F32) / half_count)
    angle = timesteps.astype(F32)[:, None] * frequency[None, :]
    return jnp.concatenate([jnp.cos(angle), jnp.sin(angle)], axis=1)


def rotary_tables(row_positions, head_dim):
    dim_frame = head_dim // 4
    dim_plane = head_dim // 8 * 3
    pieces = []
    for axis_pos, span_dims in ((0, dim_frame), (1, dim_plane), (2, dim_plane)):
        frequency = 10000.0 ** (-jnp.arange(0, span_dims, 2, dtype=F32) / span_dims)
        pieces.append(row_positions[axis_pos].astype(F32)[:, None] * jnp.repeat(frequency, 2)[None, :])
    angles = jnp.concatenate(pieces, axis=1)
    sign = jnp.where(jnp.arange(head_dim) % 2 == 0, -1.0, 1.0).astype(F32)
    cosine = jnp.cos(angles)
    sine = jnp.sin(angles) * sign[None, :]
    return jnp.concatenate([cosine, cosine], axis=1), jnp.concatenate([sine, sine], axis=1)


def prepare_kernel(heads, head_dim, qkv_ref, cos_ref, sin_ref, kind_ref, norm_ref, q_ref, pair_ref):
    pair = 2 * head_dim
    rows = qkv_ref.shape[0]
    lane = lax.broadcasted_iota(jnp.int32, (rows, pair), 1)
    first = lane < head_dim
    even = lane % 2 == 0
    request = kind_ref[...] // 2
    mask_part = jnp.where(lane == head_dim + request, 1.0, 0.0)
    cosine = cos_ref[...]
    sine = sin_ref[...]
    gain = norm_ref[0:1, :]
    bias = norm_ref[1:2, :]
    for h in range(heads):
        base = 3 * head_dim * h
        both = qkv_ref[:, base : base + pair].astype(F32)
        key_value = qkv_ref[:, base + head_dim : base + head_dim + pair].astype(F32)
        mean_q = jnp.sum(jnp.where(first, both, 0.0), axis=1, keepdims=True) / head_dim
        mean_k = jnp.sum(jnp.where(first, 0.0, both), axis=1, keepdims=True) / head_dim
        center = both - jnp.where(first, mean_q, mean_k)
        square = center * center
        var_q = jnp.sum(jnp.where(first, square, 0.0), axis=1, keepdims=True) / head_dim
        var_k = jnp.sum(jnp.where(first, 0.0, square), axis=1, keepdims=True) / head_dim
        scale = jnp.where(first, lax.rsqrt(var_q + EPS_HEAD), lax.rsqrt(var_k + EPS_HEAD))
        normed = center * scale * gain + bias
        swapped = jnp.where(even, pltpu.roll(normed, pair - 1, 1), pltpu.roll(normed, 1, 1))
        turned = normed * cosine + swapped * sine
        q_ref[h] = jnp.where(first, turned, mask_part).astype(BF)
        pair_ref[h] = jnp.where(first, pltpu.roll(turned, head_dim, 1), key_value).astype(BF)


def prepare(qkv, cosine, sine, kinds, norm_rows, heads, head_dim):
    rows, width = qkv.shape
    block = min(256, rows)
    pair = 2 * head_dim
    return pl.pallas_call(
        functools.partial(prepare_kernel, heads, head_dim),
        grid=(rows // block,),
        in_specs=[
            pl.BlockSpec((block, width), lambda i: (i, 0)),
            pl.BlockSpec((block, pair), lambda i: (i, 0)),
            pl.BlockSpec((block, pair), lambda i: (i, 0)),
            pl.BlockSpec((block, 1), lambda i: (i, 0)),
            pl.BlockSpec((2, pair), lambda i: (0, 0)),
        ],
        out_specs=[
            pl.BlockSpec((heads, block, pair), lambda i: (0, i, 0)),
            pl.BlockSpec((heads, block, pair), lambda i: (0, i, 0)),
        ],
        out_shape=[
            jax.ShapeDtypeStruct((heads, rows, pair), BF),
            jax.ShapeDtypeStruct((heads, rows, pair), BF),
        ],
        compiler_params=pltpu.CompilerParams(vmem_limit_bytes=48 * 1024 * 1024),
        name="prepare",
    )(qkv, cosine, sine, kinds[:, None], norm_rows)


def attend_kernel(heads, head_dim, q_ref, own_ref, other_ref, own_mask_ref, other_mask_ref, out_ref):
    pair = 2 * head_dim
    keys_count = own_ref.shape[1]
    lane = lax.broadcasted_iota(jnp.int32, (keys_count, pair), 1)
    first = lane < head_dim
    one = jnp.where(lane == 0, 1.0, 0.0).astype(BF)
    factor = LOG2E * head_dim ** (-0.5)
    pieces = []
    for h in range(heads):
        queries = q_ref[h]
        own = own_ref[h]
        other = other_ref[h]
        contract = (((1,), (1,)), ((), ()))
        scores_a = lax.dot_general(
            queries, jnp.where(first, own, own_mask_ref[...]), contract, preferred_element_type=F32
        )
        scores_b = lax.dot_general(
            queries, jnp.where(first, other, other_mask_ref[...]), contract, preferred_element_type=F32
        )
        top = jnp.maximum(
            jnp.max(scores_a, axis=1, keepdims=True), jnp.max(scores_b, axis=1, keepdims=True)
        )
        weights_a = jnp.exp2((scores_a - top) * factor).astype(BF)
        weights_b = jnp.exp2((scores_b - top) * factor).astype(BF)
        mixed = jnp.dot(weights_a, jnp.where(first, one, own), preferred_element_type=F32)
        mixed += jnp.dot(weights_b, jnp.where(first, one, other), preferred_element_type=F32)
        pieces.append(mixed[:, head_dim:] / mixed[:, 0:1])
    out_ref[...] = jnp.concatenate(pieces, axis=1).astype(BF)


def attend(queries, own, other, own_mask, other_mask, head_dim):
    heads, rows, pair = queries.shape
    keys_count = own.shape[1]
    block = min(256, rows)
    whole = pl.BlockSpec((heads, keys_count, pair), lambda i: (0, 0, 0))
    mask = pl.BlockSpec((keys_count, pair), lambda i: (0, 0))
    return pl.pallas_call(
        functools.partial(attend_kernel, heads, head_dim),
        grid=(rows // block,),
        in_specs=[pl.BlockSpec((heads, block, pair), lambda i: (0, i, 0)), whole, whole, mask, mask],
        out_specs=pl.BlockSpec((block, heads * head_dim), lambda i: (i, 0)),
        out_shape=jax.ShapeDtypeStruct((rows, heads * head_dim), BF),
        compiler_params=pltpu.CompilerParams(vmem_limit_bytes=48 * 1024 * 1024),
        name="attend",
    )(queries, own, other, own_mask, other_mask)


def key_mask(kinds, head_dim):
    lane = jnp.arange(2 * head_dim)[None, :]
    foreign = (lane >= head_dim) & (lane < head_dim + 2) & (lane - head_dim != (kinds // 2)[:, None])
    return jnp.where(foreign, FAR, 0.0).astype(BF)


def pick(table, kinds, part):
    column = kinds[:, None]
    low = jnp.where(column == 0, table[0, part][None], table[1, part][None])
    high = jnp.where(column == 2, table[2, part][None], table[3, part][None])
    return jnp.where(column < 2, low, high)


def exchange(blocks, axis):
    n = lax.axis_size(axis)
    me = lax.axis_index(axis)
    got = jnp.zeros_like(blocks)
    got = lax.dynamic_update_slice_in_dim(
        got, lax.dynamic_slice_in_dim(blocks, me, 1, 0), me, 0
    )
    for step in range(1, n):
        there = (me + step) % n
        back = (me + n - step) % n
        block = lax.dynamic_slice_in_dim(blocks, there, 1, 0)
        block = lax.ppermute(block, axis, [(i, (i + step) % n) for i in range(n)])
        got = lax.dynamic_update_slice_in_dim(got, block, back, 0)
    return got


def per_device(
    hidden_in,
    row_kind,
    positions,
    timesteps,
    stale_cache,
    w_qkv,
    qk_norm,
    w_out,
    ada_weight,
    w_up,
    w_down,
):
    operands = (
        hidden_in,
        row_kind,
        positions,
        timesteps,
        stale_cache,
        w_qkv[0],
        qk_norm[0],
        w_out[0],
        ada_weight[0],
        w_up[0],
        w_down[0],
    )
    n_narrow = lax.axis_size("narrow")
    if n_narrow == 4 and lax.axis_size("wide") == 4 and stale_cache.shape[3] % n_narrow == 0:
        return in_pairs(*operands)
    return features_split(*operands)


def swap(value):
    return lax.ppermute(value, "section", [(0, 1), (1, 0)])


def by_layer(parts, lead):
    got = swap(jnp.where(lead, parts[1], parts[0]))
    kept = jnp.where(lead, parts[0], parts[1])
    return jnp.stack([jnp.where(lead, kept, got), jnp.where(lead, got, kept)])[None]


def norm_pairs(norms):
    return jnp.stack([jnp.concatenate([norms[0], norms[2]]), jnp.concatenate([norms[1], norms[3]])])


def modulate(values, table, kinds):
    return (values * (1.0 + pick(table, kinds, 1)) + pick(table, kinds, 0)).astype(BF)


def wide_pairs(step):
    return [(i, i ^ step) for i in range(lax.axis_size("wide"))]


def gather_wide(block):
    got = [lax.ppermute(block, "wide", wide_pairs(step)) for step in range(1, lax.axis_size("wide"))]
    return jnp.concatenate([block] + got, axis=0)


def scatter_wide(terms):
    total = terms[0].astype(F32)
    for step in range(1, len(terms)):
        total += lax.ppermute(terms[step], "wide", wide_pairs(step)).astype(F32)
    return total


def to_mate(value):
    return lax.ppermute(value, "narrow", [(i, i ^ 1) for i in range(lax.axis_size("narrow"))])


def to_partner(value):
    return lax.ppermute(value, "narrow", [(i, i ^ 2) for i in range(lax.axis_size("narrow"))])


def statistics(values):
    width = values.shape[1]
    mean = jnp.mean(values, axis=1)
    center = values - mean[:, None]
    own = jnp.stack([mean, jnp.sum(center * center, axis=1)])
    far = to_partner(own)
    whole_mean = 0.5 * (own[0] + far[0])
    spread = own[1] + far[1] + width * ((own[0] - whole_mean) ** 2 + (far[0] - whole_mean) ** 2)
    return whole_mean, lax.rsqrt(spread / (2 * width) + EPS_ROW)


def normed(values, moments, table, kinds):
    mean, scale = moments
    return modulate((values - mean[:, None]) * scale[:, None], table, kinds)


def ordered(*values):
    return lax.optimization_barrier(values)


def in_pairs(
    hidden_in,
    row_kind,
    positions,
    timesteps,
    stale_cache,
    w_qkv,
    qk_norm,
    w_out,
    ada_weight,
    w_up,
    w_down,
):
    n_wide = lax.axis_size("wide")
    n_narrow = lax.axis_size("narrow")
    wide_idx = lax.axis_index("wide")
    narrow_idx = lax.axis_index("narrow")
    section = lax.axis_index("section")
    lead = section == 0
    odd = narrow_idx % 2
    high = narrow_idx // 2
    lower = high == 0
    _, rows_a, feat_a = hidden_in.shape
    halves = 2
    part = rows_a // halves
    total_rows = rows_a * n_wide
    chunk = total_rows // halves
    rows_b = total_rows // n_narrow
    heads_local = stale_cache.shape[3]
    heads = heads_local // n_narrow
    pair = stale_cache.shape[4]
    head_dim = pair // 2
    head_group = [0, 2, 1, 3]

    def both_layers(own):
        other = swap(own)
        return (jnp.where(lead, own, other), jnp.where(lead, other, own))

    def relative(values):
        blocks = values.reshape(n_wide, halves, part)
        order = [lax.dynamic_index_in_dim(blocks, wide_idx ^ step, 0, False) for step in range(n_wide)]
        return jnp.stack(order, axis=1).reshape(total_rows)

    def mate_half(layer, sent):
        pairs = [(layer * n_narrow + i, layer * n_narrow + (i ^ 1)) for i in range(n_narrow)]
        return lax.ppermute(sent, ("section", "narrow"), pairs)

    def passed(layer, value):
        return lax.ppermute(value, "section", [(layer, 1 - layer)])

    def pass_on(layer, kept, got, axis):
        joined = jnp.concatenate([kept, got], axis=axis)
        return joined, passed(layer, joined)

    def weight_of(layer, parts, axis):
        return pass_on(layer, parts[0], mate_half(layer, parts[1]), axis)

    def select(layer, weight):
        return jnp.where(section == layer, weight[0], weight[1])

    def two_blocks(own, axis, size, first, second):
        starts = [first * size, second * size]
        return jnp.concatenate([lax.dynamic_slice_in_dim(own, at, size, axis) for at in starts], axis=axis)

    size = w_qkv.shape[1] // 4
    qkv_parts = [two_blocks(w_qkv, 1, size, 2 * p + 1 - high, 2 * p + high) for p in (odd, 1 - odd)]
    size = w_out.shape[0] // 4
    out_parts = [two_blocks(w_out, 0, size, 2 * p + high, 2 * p + 1 - high) for p in (odd, 1 - odd)]
    size = w_up.shape[1] // 2
    up_parts = [lax.dynamic_slice_in_dim(w_up, p * size, size, 1) for p in (odd, 1 - odd)]
    size = w_down.shape[0] // 2
    down_parts = [lax.dynamic_slice_in_dim(w_down, p * size, size, 0) for p in (odd, 1 - odd)]

    def ordered_parts(value, parts):
        value, sent = ordered(value, parts[1])
        return value, (parts[0], sent)

    layer_in = lax.dynamic_index_in_dim(hidden_in, section, 0, False)
    layer_in = jnp.concatenate([layer_in, to_mate(layer_in)], axis=1)
    layer_in, timesteps = ordered(layer_in, timesteps)
    first_mean, first_scale = statistics(layer_in.astype(F32))
    layer_in = [layer_in[h * part : (h + 1) * part] for h in range(halves)]
    activated = jax.nn.silu(time_features(timesteps, ada_weight.shape[1])).astype(BF)
    modulation = jnp.einsum("re,kesd->krsd", activated, ada_weight, preferred_element_type=F32)
    modulation = modulation.reshape(2, 4, 3, feat_a)
    modulation = jnp.concatenate([modulation, to_mate(modulation)], axis=-1)
    kept = passed(0, qkv_parts[0])
    modulation, first_mean, sent, kept = ordered(modulation, first_mean, qkv_parts[1], kept)
    got = mate_half(0, sent)
    qkv_now = jnp.concatenate(
        [jnp.where(lead, qkv_parts[0], kept), jnp.where(lead, got, passed(0, got))], axis=0
    )
    shape = modulation.shape
    width = shape[-1]
    rows = modulation.reshape(-1, width)
    last = jnp.concatenate([qk_norm.reshape(-1), jnp.zeros((width - qk_norm.size,), F32)])
    both = both_layers(jnp.concatenate([rows, last[None]], axis=0))
    tables = [table[:-1].reshape(shape) for table in both]
    norm_rows = [table[-1, : qk_norm.size].reshape(qk_norm.shape) for table in both]

    kinds = lax.dynamic_index_in_dim(row_kind, section, 0, False)
    kinds_other = lax.dynamic_index_in_dim(row_kind, 1 - section, 0, False)
    kinds_r = relative(kinds)
    own_mask = key_mask(kinds_r, head_dim)
    other_mask = key_mask(jnp.where(lead, kinds_other, relative(kinds_other)), head_dim)
    kinds_a = lax.dynamic_slice_in_dim(kinds, wide_idx * rows_a, rows_a)
    kinds_h = [kinds_a[h * part : (h + 1) * part] for h in range(halves)]
    places = lax.dynamic_index_in_dim(positions, section, 1, False)
    places = jnp.stack([relative(places[i]) for i in range(3)])
    cosine, sine = rotary_tables(places, head_dim)

    def stale_heads(rows_part):
        blocks = rows_part.reshape(rows_b, n_narrow, heads, pair)
        blocks = jnp.stack([blocks[:, group] for group in head_group]).transpose(0, 2, 1, 3)
        got = exchange(blocks, "narrow")
        return got.transpose(1, 0, 2, 3).reshape(heads, total_rows, pair)

    def to_rows(fresh):
        blocks = [f.reshape(heads, n_wide, part, pair) for f in fresh]
        per_narrow = []
        for there in range(n_narrow):
            picked = [lax.dynamic_index_in_dim(b, wide_idx ^ there, 1, False) for b in blocks]
            per_narrow.append(jnp.concatenate(picked, axis=1))
        got = exchange(jnp.stack(per_narrow), "narrow")
        got = jnp.stack([got[sender] for sender in head_group])
        return got.transpose(2, 0, 1, 3).reshape(rows_b, heads_local, pair)

    def summed(terms):
        total = scatter_wide([terms[r * part : (r + 1) * part] for r in range(n_wide)]).astype(BF)
        far = to_mate(jnp.concatenate([total[:, feat_a:], total[:, :feat_a]], axis=1))
        return total.astype(F32) + far.astype(F32)

    results = []
    caches = []
    for layer in range(2):
        table = tables[layer]
        norm_pair = norm_pairs(norm_rows[layer])
        x_in = [block.astype(F32) for block in layer_in]
        queries = []
        fresh = []
        for h in range(halves):
            if layer == 0:
                rows = slice(h * part, (h + 1) * part)
                moments = (first_mean[rows], first_scale[rows])
            else:
                moments = statistics(x_in[h])
            entry = normed(x_in[h], moments, table[0], kinds_h[h])
            if layer == 0 and h == 0:
                entry, stale = ordered(entry, stale_cache[0, 1])
                stale = stale_heads(stale)
                entry, out_sent = ordered(entry, out_parts[1])
                out_got = mate_half(0, out_sent)
            terms = jnp.dot(gather_wide(entry), qkv_now, preferred_element_type=F32).astype(BF)
            if layer == 0 and h == 1:
                terms, stale, out_got, up_sent = ordered(terms, stale, out_got, up_parts[1])
                out_weight = pass_on(0, out_parts[0], out_got, 1)
                up_got = mate_half(0, up_sent)
            width = terms.shape[1] // 2
            qkv = terms[:, width:].astype(F32) + to_partner(terms[:, :width]).astype(F32)
            rows = slice(h * chunk, (h + 1) * chunk)
            q, pairs = prepare(
                qkv, cosine[rows], sine[rows], kinds_r[rows], norm_pair, heads, head_dim
            )
            queries.append(q)
            fresh.append(pairs)
        own = jnp.concatenate(fresh, axis=1)
        own, *out_weight = ordered(own, *out_weight)
        if layer == 0:
            other = jnp.where(lead, stale, lax.ppermute(own, "section", [(0, 1)]))
        else:
            other = swap(jnp.where(lead, own, stale))
        after = []
        for h in range(halves):
            attended = attend(queries[h], own, other, own_mask, other_mask, head_dim)
            attended = jnp.concatenate([attended, to_partner(attended)], axis=1)
            terms = jnp.dot(attended, select(layer, out_weight), preferred_element_type=F32).astype(BF)
            if layer == 0 and h == 0:
                terms, up_got = ordered(terms, up_got)
                up_weight = pass_on(0, up_parts[0], up_got, 0)
            if h == 1:
                terms, down_sent, *fresh = ordered(terms, down_parts[1], *fresh)
                cache = to_rows(fresh)
                down_weight = weight_of(layer, (down_parts[0], down_sent), 1)
            after.append(x_in[h] + pick(table[0], kinds_h[h], 2) * summed(terms))
        inner = []
        for h in range(halves):
            entry = normed(after[h], statistics(after[h]), table[1], kinds_h[h])
            if layer == 0 and h == 0:
                entry, parts = ordered_parts(entry, qkv_parts)
                qkv_weight = weight_of(1, parts, 0)
            entry = gather_wide(entry)
            up = jnp.dot(entry, select(layer, up_weight), preferred_element_type=F32).astype(BF)
            size = chunk // 2
            got = to_partner(lax.dynamic_slice_in_dim(up, (1 - high) * size, size, 0))
            up = lax.dynamic_slice_in_dim(up, high * size, size, 0).astype(F32) + got.astype(F32)
            inner.append(jax.nn.gelu(up, approximate=True).astype(BF))
        layer_in = []
        for h in range(halves):
            got = to_partner(inner[h])
            if h == 1:
                got, cache = ordered(got, cache)
                caches.append(cache)
            first = jnp.where(lower, inner[h], got)
            second = jnp.where(lower, got, inner[h])
            whole = jnp.concatenate([first, second], axis=0)
            terms = jnp.dot(whole, select(layer, down_weight), preferred_element_type=F32).astype(BF)
            if layer == 0 and h == 0:
                terms, parts = ordered_parts(terms, out_parts)
                out_weight = weight_of(1, parts, 1)
                terms, parts = ordered_parts(terms, up_parts)
                up_weight = weight_of(1, parts, 0)
                qkv_now = select(1, qkv_weight)
            layer_in.append((after[h] + pick(table[1], kinds_h[h], 2) * summed(terms)).astype(BF))
        results.append(jnp.concatenate([block[:, :feat_a] for block in layer_in], axis=0))
    return (by_layer(results, lead), by_layer(caches, lead))


def features_split(
    hidden_in,
    row_kind,
    positions,
    timesteps,
    stale_cache,
    w_qkv,
    qk_norm,
    w_out,
    ada_weight,
    w_up,
    w_down,
):
    n_wide = lax.axis_size("wide")
    n_narrow = lax.axis_size("narrow")
    wide_idx = lax.axis_index("wide")
    narrow_idx = lax.axis_index("narrow")
    section = lax.axis_index("section")
    patch_count, rows_a, feat_a = hidden_in.shape
    total_rows = rows_a * n_wide
    rows_b = total_rows // n_narrow
    heads_local = stale_cache.shape[3]
    pair = stale_cache.shape[4]
    head_dim = pair // 2
    model_width = feat_a * n_narrow
    heads = heads_local
    lead = section == 0

    def both_layers(own):
        other = swap(own)
        return (jnp.where(lead, own, other), jnp.where(lead, other, own))

    qkv_weights = both_layers(w_qkv)
    out_weights = both_layers(w_out)
    up_weights = both_layers(w_up)
    down_weights = both_layers(w_down)
    norm_rows = both_layers(qk_norm)

    activated = jax.nn.silu(time_features(timesteps, ada_weight.shape[1])).astype(BF)
    modulation = jnp.einsum("re,kesd->krsd", activated, ada_weight, preferred_element_type=F32)
    tables = both_layers(modulation.reshape(2, 4, 3, feat_a))

    kinds = lax.dynamic_slice_in_dim(row_kind, section, 1, 0)[0]
    kinds_other = lax.dynamic_slice_in_dim(row_kind, 1 - section, 1, 0)[0]
    own_mask = key_mask(kinds, head_dim)
    other_mask = key_mask(kinds_other, head_dim)
    kinds_a = lax.dynamic_slice_in_dim(kinds, wide_idx * rows_a, rows_a)
    places = lax.dynamic_slice_in_dim(positions, section, 1, 1)[:, 0]
    places = lax.dynamic_slice_in_dim(places, narrow_idx * rows_b, rows_b, 1)
    kinds_q = lax.dynamic_slice_in_dim(kinds, narrow_idx * rows_b, rows_b)
    cosine, sine = rotary_tables(places, head_dim)

    stale = lax.all_gather(stale_cache[0, 1].transpose(1, 0, 2), "narrow", axis=1, tiled=True)

    def normalize(values):
        moments = lax.psum(
            jnp.stack([jnp.sum(values, axis=1), jnp.sum(values * values, axis=1)]), "narrow"
        )
        row_mean = moments[0] / model_width
        variance = moments[1] / model_width - row_mean * row_mean
        return (values - row_mean[:, None]) * lax.rsqrt(variance + EPS_ROW)[:, None]

    layer_in = lax.dynamic_slice_in_dim(hidden_in, section, 1, 0)[0]
    results = []
    caches = []
    for layer in range(2):
        table = tables[layer]
        x_in = layer_in.astype(F32)
        entry = modulate(normalize(x_in), table[0], kinds_a)
        qkv_terms = jnp.dot(
            lax.all_gather(entry, "wide", axis=0, tiled=True),
            qkv_weights[layer],
            preferred_element_type=F32,
        ).astype(BF)
        qkv = lax.psum_scatter(qkv_terms, "narrow", scatter_dimension=0, tiled=True)
        queries, fresh = prepare(
            qkv, cosine, sine, kinds_q, norm_pairs(norm_rows[layer]), heads, head_dim
        )
        caches.append(fresh.transpose(1, 0, 2))
        fresh = lax.all_gather(fresh, "narrow", axis=1, tiled=True)
        if layer == 0:
            other = jnp.where(lead, stale, swap(fresh))
        else:
            other = swap(jnp.where(lead, fresh, stale))
        attended = attend(queries, fresh, other, own_mask, other_mask, head_dim)
        attended = lax.all_gather(attended, "narrow", axis=0, tiled=True)
        proj_terms = jnp.dot(attended, out_weights[layer], preferred_element_type=F32).astype(BF)
        projected = lax.psum_scatter(proj_terms, "wide", scatter_dimension=0, tiled=True)
        after = x_in + pick(table[0], kinds_a, 2) * projected.astype(F32)
        entry = modulate(normalize(after), table[1], kinds_a)
        up_terms = jnp.dot(
            lax.all_gather(entry, "wide", axis=0, tiled=True),
            up_weights[layer],
            preferred_element_type=F32,
        ).astype(BF)
        up_sum = lax.psum_scatter(up_terms, "narrow", scatter_dimension=0, tiled=True)
        inner = jax.nn.gelu(up_sum.astype(F32), approximate=True).astype(BF)
        down_terms = jnp.dot(
            lax.all_gather(inner, "narrow", axis=0, tiled=True),
            down_weights[layer],
            preferred_element_type=F32,
        ).astype(BF)
        down_sum = lax.psum_scatter(down_terms, "wide", scatter_dimension=0, tiled=True)
        layer_in = (after + pick(table[1], kinds_a, 2) * down_sum.astype(F32)).astype(BF)
        results.append(layer_in)

    return (by_layer(results, lead), by_layer(caches, lead))


def solution(mesh):
    in_specs = (
        P(None, "wide", "narrow"),
        P(),
        P(),
        P(),
        P("section", None, "narrow", "wide", None),
        P("section", "narrow", "wide"),
        P("section", None, None),
        P("section", "wide", "narrow"),
        P("section", None, None, None, "narrow"),
        P("section", "narrow", "wide"),
        P("section", "wide", "narrow"),
    )
    out_specs = (P("section", None, "wide", "narrow"), P("section", None, "narrow", "wide", None))
    return jax.shard_map(
        per_device, mesh=mesh, in_specs=in_specs, out_specs=out_specs, check_vma=False
    )
```

```python
import functools

import jax
import jax.numpy as jnp
from jax import lax
from jax.experimental import pallas as pl
from jax.experimental.pallas import tpu as pltpu
from jax.sharding import PartitionSpec as P

EPS_ROW = 1e-05
EPS_HEAD = 1e-06
FAR = -1e30
LOG2E = 1.4426950408889634
BF = jnp.bfloat16
F32 = jnp.float32


def time_features(timesteps, feature_count):
    half_count = feature_count // 2
    frequency = jnp.exp(-jnp.log(10000.0) * jnp.arange(half_count, dtype=F32) / half_count)
    angle = timesteps.astype(F32)[:, None] * frequency[None, :]
    return jnp.concatenate([jnp.cos(angle), jnp.sin(angle)], axis=1)


def rotary_tables(row_positions, head_dim):
    dim_frame = head_dim // 4
    dim_plane = head_dim // 8 * 3
    pieces = []
    for axis_pos, span_dims in ((0, dim_frame), (1, dim_plane), (2, dim_plane)):
        frequency = 10000.0 ** (-jnp.arange(0, span_dims, 2, dtype=F32) / span_dims)
        pieces.append(row_positions[axis_pos].astype(F32)[:, None] * jnp.repeat(frequency, 2)[None, :])
    angles = jnp.concatenate(pieces, axis=1)
    sign = jnp.where(jnp.arange(head_dim) % 2 == 0, -1.0, 1.0).astype(F32)
    cosine = jnp.cos(angles)
    sine = jnp.sin(angles) * sign[None, :]
    return jnp.concatenate([cosine, cosine], axis=1), jnp.concatenate([sine, sine], axis=1)


def prepare_kernel(heads, head_dim, qkv_ref, cos_ref, sin_ref, kind_ref, norm_ref, q_ref, pair_ref):
    pair = 2 * head_dim
    rows = qkv_ref.shape[0]
    lane = lax.broadcasted_iota(jnp.int32, (rows, pair), 1)
    first = lane < head_dim
    even = lane % 2 == 0
    request = kind_ref[...] // 2
    mask_part = jnp.where(lane == head_dim + request, 1.0, 0.0)
    cosine = cos_ref[...]
    sine = sin_ref[...]
    gain = norm_ref[0:1, :]
    bias = norm_ref[1:2, :]
    for h in range(heads):
        base = 3 * head_dim * h
        both = qkv_ref[:, base : base + pair].astype(F32)
        key_value = qkv_ref[:, base + head_dim : base + head_dim + pair].astype(F32)
        mean_q = jnp.sum(jnp.where(first, both, 0.0), axis=1, keepdims=True) / head_dim
        mean_k = jnp.sum(jnp.where(first, 0.0, both), axis=1, keepdims=True) / head_dim
        center = both - jnp.where(first, mean_q, mean_k)
        square = center * center
        var_q = jnp.sum(jnp.where(first, square, 0.0), axis=1, keepdims=True) / head_dim
        var_k = jnp.sum(jnp.where(first, 0.0, square), axis=1, keepdims=True) / head_dim
        scale = jnp.where(first, lax.rsqrt(var_q + EPS_HEAD), lax.rsqrt(var_k + EPS_HEAD))
        normed = center * scale * gain + bias
        swapped = jnp.where(even, pltpu.roll(normed, pair - 1, 1), pltpu.roll(normed, 1, 1))
        turned = normed * cosine + swapped * sine
        q_ref[h] = jnp.where(first, turned, mask_part).astype(BF)
        pair_ref[h] = jnp.where(first, pltpu.roll(turned, head_dim, 1), key_value).astype(BF)


def prepare(qkv, cosine, sine, kinds, norm_rows, heads, head_dim):
    rows, width = qkv.shape
    block = min(256, rows)
    pair = 2 * head_dim
    return pl.pallas_call(
        functools.partial(prepare_kernel, heads, head_dim),
        grid=(rows // block,),
        in_specs=[
            pl.BlockSpec((block, width), lambda i: (i, 0)),
            pl.BlockSpec((block, pair), lambda i: (i, 0)),
            pl.BlockSpec((block, pair), lambda i: (i, 0)),
            pl.BlockSpec((block, 1), lambda i: (i, 0)),
            pl.BlockSpec((2, pair), lambda i: (0, 0)),
        ],
        out_specs=[
            pl.BlockSpec((heads, block, pair), lambda i: (0, i, 0)),
            pl.BlockSpec((heads, block, pair), lambda i: (0, i, 0)),
        ],
        out_shape=[
            jax.ShapeDtypeStruct((heads, rows, pair), BF),
            jax.ShapeDtypeStruct((heads, rows, pair), BF),
        ],
        compiler_params=pltpu.CompilerParams(vmem_limit_bytes=48 * 1024 * 1024),
        name="prepare",
    )(qkv, cosine, sine, kinds[:, None], norm_rows)


def attend_kernel(heads, head_dim, q_ref, own_ref, other_ref, own_mask_ref, other_mask_ref, out_ref):
    pair = 2 * head_dim
    keys_count = own_ref.shape[1]
    lane = lax.broadcasted_iota(jnp.int32, (keys_count, pair), 1)
    first = lane < head_dim
    one = jnp.where(lane == 0, 1.0, 0.0).astype(BF)
    factor = LOG2E * head_dim ** (-0.5)
    pieces = []
    for h in range(heads):
        queries = q_ref[h]
        own = own_ref[h]
        other = other_ref[h]
        contract = (((1,), (1,)), ((), ()))
        scores_a = lax.dot_general(
            queries, jnp.where(first, own, own_mask_ref[...]), contract, preferred_element_type=F32
        )
        scores_b = lax.dot_general(
            queries, jnp.where(first, other, other_mask_ref[...]), contract, preferred_element_type=F32
        )
        top = jnp.maximum(
            jnp.max(scores_a, axis=1, keepdims=True), jnp.max(scores_b, axis=1, keepdims=True)
        )
        weights_a = jnp.exp2((scores_a - top) * factor).astype(BF)
        weights_b = jnp.exp2((scores_b - top) * factor).astype(BF)
        mixed = jnp.dot(weights_a, jnp.where(first, one, own), preferred_element_type=F32)
        mixed += jnp.dot(weights_b, jnp.where(first, one, other), preferred_element_type=F32)
        pieces.append(mixed[:, head_dim:] / mixed[:, 0:1])
    out_ref[...] = jnp.concatenate(pieces, axis=1).astype(BF)


def attend(queries, own, other, own_mask, other_mask, head_dim):
    heads, rows, pair = queries.shape
    keys_count = own.shape[1]
    block = min(256, rows)
    whole = pl.BlockSpec((heads, keys_count, pair), lambda i: (0, 0, 0))
    mask = pl.BlockSpec((keys_count, pair), lambda i: (0, 0))
    return pl.pallas_call(
        functools.partial(attend_kernel, heads, head_dim),
        grid=(rows // block,),
        in_specs=[pl.BlockSpec((heads, block, pair), lambda i: (0, i, 0)), whole, whole, mask, mask],
        out_specs=pl.BlockSpec((block, heads * head_dim), lambda i: (i, 0)),
        out_shape=jax.ShapeDtypeStruct((rows, heads * head_dim), BF),
        compiler_params=pltpu.CompilerParams(vmem_limit_bytes=48 * 1024 * 1024),
        name="attend",
    )(queries, own, other, own_mask, other_mask)


def key_mask(kinds, head_dim):
    lane = jnp.arange(2 * head_dim)[None, :]
    foreign = (lane >= head_dim) & (lane < head_dim + 2) & (lane - head_dim != (kinds // 2)[:, None])
    return jnp.where(foreign, FAR, 0.0).astype(BF)


def pick(table, kinds, part):
    column = kinds[:, None]
    low = jnp.where(column == 0, table[0, part][None], table[1, part][None])
    high = jnp.where(column == 2, table[2, part][None], table[3, part][None])
    return jnp.where(column < 2, low, high)


def exchange(blocks, axis):
    n = lax.axis_size(axis)
    me = lax.axis_index(axis)
    got = jnp.zeros_like(blocks)
    got = lax.dynamic_update_slice_in_dim(
        got, lax.dynamic_slice_in_dim(blocks, me, 1, 0), me, 0
    )
    for step in range(1, n):
        there = (me + step) % n
        back = (me + n - step) % n
        block = lax.dynamic_slice_in_dim(blocks, there, 1, 0)
        block = lax.ppermute(block, axis, [(i, (i + step) % n) for i in range(n)])
        got = lax.dynamic_update_slice_in_dim(got, block, back, 0)
    return got


def per_device(
    hidden_in,
    row_kind,
    positions,
    timesteps,
    stale_cache,
    w_qkv,
    qk_norm,
    w_out,
    ada_weight,
    w_up,
    w_down,
):
    operands = (
        hidden_in,
        row_kind,
        positions,
        timesteps,
        stale_cache,
        w_qkv[0],
        qk_norm[0],
        w_out[0],
        ada_weight[0],
        w_up[0],
        w_down[0],
    )
    n_narrow = lax.axis_size("narrow")
    if n_narrow == 4 and lax.axis_size("wide") == 4 and stale_cache.shape[3] % n_narrow == 0:
        return in_pairs(*operands)
    return features_split(*operands)


def swap(value):
    return lax.ppermute(value, "section", [(0, 1), (1, 0)])


def by_layer(parts, lead):
    got = swap(jnp.where(lead, parts[1], parts[0]))
    kept = jnp.where(lead, parts[0], parts[1])
    return jnp.stack([jnp.where(lead, kept, got), jnp.where(lead, got, kept)])[None]


def norm_pairs(norms):
    return jnp.stack([jnp.concatenate([norms[0], norms[2]]), jnp.concatenate([norms[1], norms[3]])])


def modulate(values, table, kinds):
    return (values * (1.0 + pick(table, kinds, 1)) + pick(table, kinds, 0)).astype(BF)


def wide_pairs(step):
    return [(i, i ^ step) for i in range(lax.axis_size("wide"))]


def gather_wide(block):
    got = [lax.ppermute(block, "wide", wide_pairs(step)) for step in range(1, lax.axis_size("wide"))]
    return jnp.concatenate([block] + got, axis=0)


def scatter_wide(terms):
    total = terms[0].astype(F32)
    for step in range(1, len(terms)):
        total += lax.ppermute(terms[step], "wide", wide_pairs(step)).astype(F32)
    return total


def to_mate(value):
    return lax.ppermute(value, "narrow", [(i, i ^ 1) for i in range(lax.axis_size("narrow"))])


def to_partner(value):
    return lax.ppermute(value, "narrow", [(i, i ^ 2) for i in range(lax.axis_size("narrow"))])


def statistics(values):
    width = values.shape[1]
    mean = jnp.mean(values, axis=1)
    center = values - mean[:, None]
    own = jnp.stack([mean, jnp.sum(center * center, axis=1)])
    far = to_partner(own)
    whole_mean = 0.5 * (own[0] + far[0])
    spread = own[1] + far[1] + width * ((own[0] - whole_mean) ** 2 + (far[0] - whole_mean) ** 2)
    return whole_mean, lax.rsqrt(spread / (2 * width) + EPS_ROW)


def normed(values, moments, table, kinds):
    mean, scale = moments
    return modulate((values - mean[:, None]) * scale[:, None], table, kinds)


def ordered(*values):
    return lax.optimization_barrier(values)


def in_pairs(
    hidden_in,
    row_kind,
    positions,
    timesteps,
    stale_cache,
    w_qkv,
    qk_norm,
    w_out,
    ada_weight,
    w_up,
    w_down,
):
    n_wide = lax.axis_size("wide")
    n_narrow = lax.axis_size("narrow")
    wide_idx = lax.axis_index("wide")
    narrow_idx = lax.axis_index("narrow")
    section = lax.axis_index("section")
    lead = section == 0
    odd = narrow_idx % 2
    high = narrow_idx // 2
    lower = high == 0
    _, rows_a, feat_a = hidden_in.shape
    halves = 2
    part = rows_a // halves
    total_rows = rows_a * n_wide
    chunk = total_rows // halves
    rows_b = total_rows // n_narrow
    heads_local = stale_cache.shape[3]
    heads = heads_local // n_narrow
    pair = stale_cache.shape[4]
    head_dim = pair // 2
    head_group = [0, 2, 1, 3]

    def both_layers(own):
        other = swap(own)
        return (jnp.where(lead, own, other), jnp.where(lead, other, own))

    def relative(values):
        blocks = values.reshape(n_wide, halves, part)
        order = [lax.dynamic_index_in_dim(blocks, wide_idx ^ step, 0, False) for step in range(n_wide)]
        return jnp.stack(order, axis=1).reshape(total_rows)

    def mate_half(layer, sent):
        pairs = [(layer * n_narrow + i, layer * n_narrow + (i ^ 1)) for i in range(n_narrow)]
        return lax.ppermute(sent, ("section", "narrow"), pairs)

    def passed(layer, value):
        return lax.ppermute(value, "section", [(layer, 1 - layer)])

    def pass_on(layer, kept, got, axis):
        joined = jnp.concatenate([kept, got], axis=axis)
        return joined, passed(layer, joined)

    def weight_of(layer, parts, axis):
        return pass_on(layer, parts[0], mate_half(layer, parts[1]), axis)

    def select(layer, weight):
        return jnp.where(section == layer, weight[0], weight[1])

    def two_blocks(own, axis, size, first, second):
        starts = [first * size, second * size]
        return jnp.concatenate([lax.dynamic_slice_in_dim(own, at, size, axis) for at in starts], axis=axis)

    size = w_qkv.shape[1] // 4
    qkv_parts = [two_blocks(w_qkv, 1, size, 2 * p + 1 - high, 2 * p + high) for p in (odd, 1 - odd)]
    def ordered_parts(value, parts):
        value, sent = ordered(value, parts[1])
        return value, (parts[0], sent)

    def stale_heads(rows_part):
        blocks = rows_part.reshape(rows_b, n_narrow, heads, pair)
        blocks = jnp.stack([blocks[:, group] for group in head_group]).transpose(0, 2, 1, 3)
        got = exchange(blocks, "narrow")
        return got.transpose(1, 0, 2, 3).reshape(heads, total_rows, pair)

    stale = stale_heads(stale_cache[0, 1])
    layer_in = lax.dynamic_index_in_dim(hidden_in, section, 0, False)
    layer_in = jnp.concatenate([layer_in, to_mate(layer_in)], axis=1)
    layer_in, timesteps = ordered(layer_in, timesteps)
    first_mean, first_scale = statistics(layer_in.astype(F32))
    layer_in = [layer_in[h * part : (h + 1) * part] for h in range(halves)]
    activated = jax.nn.silu(time_features(timesteps, ada_weight.shape[1])).astype(BF)
    modulation = jnp.einsum("re,kesd->krsd", activated, ada_weight, preferred_element_type=F32)
    modulation = modulation.reshape(2, 4, 3, feat_a)
    modulation = jnp.concatenate([modulation, to_mate(modulation)], axis=-1)
    kept = passed(0, qkv_parts[0])
    modulation, first_mean, sent, kept, stale = ordered(
        modulation, first_mean, qkv_parts[1], kept, stale
    )
    got = mate_half(0, sent)
    qkv_now = jnp.concatenate(
        [jnp.where(lead, qkv_parts[0], kept), jnp.where(lead, got, passed(0, got))], axis=0
    )
    shape = modulation.shape
    width = shape[-1]
    rows = modulation.reshape(-1, width)
    last = jnp.concatenate([qk_norm.reshape(-1), jnp.zeros((width - qk_norm.size,), F32)])
    both = both_layers(jnp.concatenate([rows, last[None]], axis=0))
    tables = [table[:-1].reshape(shape) for table in both]
    norm_rows = [table[-1, : qk_norm.size].reshape(qk_norm.shape) for table in both]

    kinds = lax.dynamic_index_in_dim(row_kind, section, 0, False)
    kinds_other = lax.dynamic_index_in_dim(row_kind, 1 - section, 0, False)
    kinds_r = relative(kinds)
    own_mask = key_mask(kinds_r, head_dim)
    other_mask = key_mask(jnp.where(lead, kinds_other, relative(kinds_other)), head_dim)
    kinds_a = lax.dynamic_slice_in_dim(kinds, wide_idx * rows_a, rows_a)
    kinds_h = [kinds_a[h * part : (h + 1) * part] for h in range(halves)]
    places = lax.dynamic_index_in_dim(positions, section, 1, False)
    places = jnp.stack([relative(places[i]) for i in range(3)])
    cosine, sine = rotary_tables(places, head_dim)

    def to_rows(fresh):
        blocks = [f.reshape(heads, n_wide, part, pair) for f in fresh]
        per_narrow = []
        for there in range(n_narrow):
            picked = [lax.dynamic_index_in_dim(b, wide_idx ^ there, 1, False) for b in blocks]
            per_narrow.append(jnp.concatenate(picked, axis=1))
        got = exchange(jnp.stack(per_narrow), "narrow")
        got = jnp.stack([got[sender] for sender in head_group])
        return got.transpose(2, 0, 1, 3).reshape(rows_b, heads_local, pair)

    def summed(terms):
        total = scatter_wide([terms[r * part : (r + 1) * part] for r in range(n_wide)]).astype(BF)
        far = to_mate(jnp.concatenate([total[:, feat_a:], total[:, :feat_a]], axis=1))
        return total.astype(F32) + far.astype(F32)

    results = []
    caches = []
    for layer in range(2):
        table = tables[layer]
        norm_pair = norm_pairs(norm_rows[layer])
        x_in = [block.astype(F32) for block in layer_in]
        queries = []
        fresh = []
        for h in range(halves):
            if layer == 0:
                rows = slice(h * part, (h + 1) * part)
                moments = (first_mean[rows], first_scale[rows])
            else:
                moments = statistics(x_in[h])
            entry = normed(x_in[h], moments, table[0], kinds_h[h])
            if layer == 0 and h == 0:
                entry, w_out, w_up = ordered(entry, w_out, w_up)
                size = w_out.shape[0] // 4
                out_parts = [
                    two_blocks(w_out, 0, size, 2 * p + high, 2 * p + 1 - high) for p in (odd, 1 - odd)
                ]
                size = w_up.shape[1] // 2
                up_parts = [lax.dynamic_slice_in_dim(w_up, p * size, size, 1) for p in (odd, 1 - odd)]
                out_got = mate_half(0, out_parts[1])
            terms = jnp.dot(gather_wide(entry), qkv_now, preferred_element_type=F32).astype(BF)
            if layer == 0 and h == 1:
                terms, out_got, up_sent = ordered(terms, out_got, up_parts[1])
                out_weight = pass_on(0, out_parts[0], out_got, 1)
                up_got = mate_half(0, up_sent)
            width = terms.shape[1] // 2
            qkv = terms[:, width:].astype(F32) + to_partner(terms[:, :width]).astype(F32)
            rows = slice(h * chunk, (h + 1) * chunk)
            q, pairs = prepare(
                qkv, cosine[rows], sine[rows], kinds_r[rows], norm_pair, heads, head_dim
            )
            queries.append(q)
            fresh.append(pairs)
        own = jnp.concatenate(fresh, axis=1)
        own, *out_weight = ordered(own, *out_weight)
        if layer == 0:
            own, w_down = ordered(own, w_down)
            size = w_down.shape[0] // 2
            down_parts = [lax.dynamic_slice_in_dim(w_down, p * size, size, 0) for p in (odd, 1 - odd)]
        if layer == 0:
            other = jnp.where(lead, stale, lax.ppermute(own, "section", [(0, 1)]))
        else:
            other = swap(jnp.where(lead, own, stale))
        after = []
        for h in range(halves):
            attended = attend(queries[h], own, other, own_mask, other_mask, head_dim)
            attended = jnp.concatenate([attended, to_partner(attended)], axis=1)
            terms = jnp.dot(attended, select(layer, out_weight), preferred_element_type=F32).astype(BF)
            if layer == 0 and h == 0:
                terms, up_got = ordered(terms, up_got)
                up_weight = pass_on(0, up_parts[0], up_got, 0)
            if h == 1:
                terms, *fresh = ordered(terms, *fresh)
                cache = to_rows(fresh)
            after.append(x_in[h] + pick(table[0], kinds_h[h], 2) * summed(terms))
        after[0], after[1], cache = ordered(after[0], after[1], cache)
        caches.append(cache)
        ups = []
        for h in range(halves):
            entry = normed(after[h], statistics(after[h]), table[1], kinds_h[h])
            if layer == 0 and h == 0:
                entry, parts = ordered_parts(entry, qkv_parts)
                qkv_weight = weight_of(1, parts, 0)
            entry = gather_wide(entry)
            ups.append(
                jnp.dot(entry, select(layer, up_weight), preferred_element_type=F32).astype(BF)
            )
        ups[0], ups[1], down_sent = ordered(ups[0], ups[1], down_parts[1])
        down_got = mate_half(layer, down_sent)
        inner = []
        for h in range(halves):
            size = chunk // 2
            got = to_partner(lax.dynamic_slice_in_dim(ups[h], (1 - high) * size, size, 0))
            up = lax.dynamic_slice_in_dim(ups[h], high * size, size, 0).astype(F32) + got.astype(F32)
            inner.append(jax.nn.gelu(up, approximate=True).astype(BF))
        inner[0], inner[1], down_got = ordered(inner[0], inner[1], down_got)
        down_weight = pass_on(layer, down_parts[0], down_got, 1)
        layer_in = []
        for h in range(halves):
            got = to_partner(inner[h])
            first = jnp.where(lower, inner[h], got)
            second = jnp.where(lower, got, inner[h])
            whole = jnp.concatenate([first, second], axis=0)
            terms = jnp.dot(whole, select(layer, down_weight), preferred_element_type=F32).astype(BF)
            if layer == 0 and h == 0:
                terms, parts = ordered_parts(terms, out_parts)
                out_weight = weight_of(1, parts, 1)
                terms, parts = ordered_parts(terms, up_parts)
                up_weight = weight_of(1, parts, 0)
                qkv_now = select(1, qkv_weight)
            layer_in.append((after[h] + pick(table[1], kinds_h[h], 2) * summed(terms)).astype(BF))
        results.append(jnp.concatenate([block[:, :feat_a] for block in layer_in], axis=0))
    return (by_layer(results, lead), by_layer(caches, lead))


def features_split(
    hidden_in,
    row_kind,
    positions,
    timesteps,
    stale_cache,
    w_qkv,
    qk_norm,
    w_out,
    ada_weight,
    w_up,
    w_down,
):
    n_wide = lax.axis_size("wide")
    n_narrow = lax.axis_size("narrow")
    wide_idx = lax.axis_index("wide")
    narrow_idx = lax.axis_index("narrow")
    section = lax.axis_index("section")
    patch_count, rows_a, feat_a = hidden_in.shape
    total_rows = rows_a * n_wide
    rows_b = total_rows // n_narrow
    heads_local = stale_cache.shape[3]
    pair = stale_cache.shape[4]
    head_dim = pair // 2
    model_width = feat_a * n_narrow
    heads = heads_local
    lead = section == 0

    def both_layers(own):
        other = swap(own)
        return (jnp.where(lead, own, other), jnp.where(lead, other, own))

    qkv_weights = both_layers(w_qkv)
    out_weights = both_layers(w_out)
    up_weights = both_layers(w_up)
    down_weights = both_layers(w_down)
    norm_rows = both_layers(qk_norm)

    activated = jax.nn.silu(time_features(timesteps, ada_weight.shape[1])).astype(BF)
    modulation = jnp.einsum("re,kesd->krsd", activated, ada_weight, preferred_element_type=F32)
    tables = both_layers(modulation.reshape(2, 4, 3, feat_a))

    kinds = lax.dynamic_slice_in_dim(row_kind, section, 1, 0)[0]
    kinds_other = lax.dynamic_slice_in_dim(row_kind, 1 - section, 1, 0)[0]
    own_mask = key_mask(kinds, head_dim)
    other_mask = key_mask(kinds_other, head_dim)
    kinds_a = lax.dynamic_slice_in_dim(kinds, wide_idx * rows_a, rows_a)
    places = lax.dynamic_slice_in_dim(positions, section, 1, 1)[:, 0]
    places = lax.dynamic_slice_in_dim(places, narrow_idx * rows_b, rows_b, 1)
    kinds_q = lax.dynamic_slice_in_dim(kinds, narrow_idx * rows_b, rows_b)
    cosine, sine = rotary_tables(places, head_dim)

    stale = lax.all_gather(stale_cache[0, 1].transpose(1, 0, 2), "narrow", axis=1, tiled=True)

    def normalize(values):
        moments = lax.psum(
            jnp.stack([jnp.sum(values, axis=1), jnp.sum(values * values, axis=1)]), "narrow"
        )
        row_mean = moments[0] / model_width
        variance = moments[1] / model_width - row_mean * row_mean
        return (values - row_mean[:, None]) * lax.rsqrt(variance + EPS_ROW)[:, None]

    layer_in = lax.dynamic_slice_in_dim(hidden_in, section, 1, 0)[0]
    results = []
    caches = []
    for layer in range(2):
        table = tables[layer]
        x_in = layer_in.astype(F32)
        entry = modulate(normalize(x_in), table[0], kinds_a)
        qkv_terms = jnp.dot(
            lax.all_gather(entry, "wide", axis=0, tiled=True),
            qkv_weights[layer],
            preferred_element_type=F32,
        ).astype(BF)
        qkv = lax.psum_scatter(qkv_terms, "narrow", scatter_dimension=0, tiled=True)
        queries, fresh = prepare(
            qkv, cosine, sine, kinds_q, norm_pairs(norm_rows[layer]), heads, head_dim
        )
        caches.append(fresh.transpose(1, 0, 2))
        fresh = lax.all_gather(fresh, "narrow", axis=1, tiled=True)
        if layer == 0:
            other = jnp.where(lead, stale, swap(fresh))
        else:
            other = swap(jnp.where(lead, fresh, stale))
        attended = attend(queries, fresh, other, own_mask, other_mask, head_dim)
        attended = lax.all_gather(attended, "narrow", axis=0, tiled=True)
        proj_terms = jnp.dot(attended, out_weights[layer], preferred_element_type=F32).astype(BF)
        projected = lax.psum_scatter(proj_terms, "wide", scatter_dimension=0, tiled=True)
        after = x_in + pick(table[0], kinds_a, 2) * projected.astype(F32)
        entry = modulate(normalize(after), table[1], kinds_a)
        up_terms = jnp.dot(
            lax.all_gather(entry, "wide", axis=0, tiled=True),
            up_weights[layer],
            preferred_element_type=F32,
        ).astype(BF)
        up_sum = lax.psum_scatter(up_terms, "narrow", scatter_dimension=0, tiled=True)
        inner = jax.nn.gelu(up_sum.astype(F32), approximate=True).astype(BF)
        down_terms = jnp.dot(
            lax.all_gather(inner, "narrow", axis=0, tiled=True),
            down_weights[layer],
            preferred_element_type=F32,
        ).astype(BF)
        down_sum = lax.psum_scatter(down_terms, "wide", scatter_dimension=0, tiled=True)
        layer_in = (after + pick(table[1], kinds_a, 2) * down_sum.astype(F32)).astype(BF)
        results.append(layer_in)

    return (by_layer(results, lead), by_layer(caches, lead))


def solution(mesh):
    in_specs = (
        P(None, "wide", "narrow"),
        P(),
        P(),
        P(),
        P("section", None, "narrow", "wide", None),
        P("section", "narrow", "wide"),
        P("section", None, None),
        P("section", "wide", "narrow"),
        P("section", None, None, None, "narrow"),
        P("section", "narrow", "wide"),
        P("section", "wide", "narrow"),
    )
    out_specs = (P("section", None, "wide", "narrow"), P("section", None, "narrow", "wide", None))
    return jax.shard_map(
        per_device, mesh=mesh, in_specs=in_specs, out_specs=out_specs, check_vma=False
    )
```

```python
import functools

import jax
import jax.numpy as jnp
from jax import lax
from jax.experimental import pallas as pl
from jax.experimental.pallas import tpu as pltpu
from jax.sharding import PartitionSpec as P

EPS_ROW = 1e-05
EPS_HEAD = 1e-06
FAR = -1e30
LOG2E = 1.4426950408889634
BF = jnp.bfloat16
F32 = jnp.float32


def time_features(timesteps, feature_count):
    half_count = feature_count // 2
    frequency = jnp.exp(-jnp.log(10000.0) * jnp.arange(half_count, dtype=F32) / half_count)
    angle = timesteps.astype(F32)[:, None] * frequency[None, :]
    return jnp.concatenate([jnp.cos(angle), jnp.sin(angle)], axis=1)


def rotary_tables(row_positions, head_dim):
    dim_frame = head_dim // 4
    dim_plane = head_dim // 8 * 3
    pieces = []
    for axis_pos, span_dims in ((0, dim_frame), (1, dim_plane), (2, dim_plane)):
        frequency = 10000.0 ** (-jnp.arange(0, span_dims, 2, dtype=F32) / span_dims)
        pieces.append(row_positions[axis_pos].astype(F32)[:, None] * jnp.repeat(frequency, 2)[None, :])
    angles = jnp.concatenate(pieces, axis=1)
    sign = jnp.where(jnp.arange(head_dim) % 2 == 0, -1.0, 1.0).astype(F32)
    cosine = jnp.cos(angles)
    sine = jnp.sin(angles) * sign[None, :]
    return jnp.concatenate([cosine, cosine], axis=1), jnp.concatenate([sine, sine], axis=1)


def prepare_kernel(heads, head_dim, qkv_ref, cos_ref, sin_ref, kind_ref, norm_ref, q_ref, pair_ref):
    pair = 2 * head_dim
    rows = qkv_ref.shape[0]
    lane = lax.broadcasted_iota(jnp.int32, (rows, pair), 1)
    first = lane < head_dim
    even = lane % 2 == 0
    request = kind_ref[...] // 2
    mask_part = jnp.where(lane == head_dim + request, 1.0, 0.0)
    cosine = cos_ref[...]
    sine = sin_ref[...]
    gain = norm_ref[0:1, :]
    bias = norm_ref[1:2, :]
    for h in range(heads):
        base = 3 * head_dim * h
        both = qkv_ref[:, base : base + pair].astype(F32)
        key_value = qkv_ref[:, base + head_dim : base + head_dim + pair].astype(F32)
        mean_q = jnp.sum(jnp.where(first, both, 0.0), axis=1, keepdims=True) / head_dim
        mean_k = jnp.sum(jnp.where(first, 0.0, both), axis=1, keepdims=True) / head_dim
        center = both - jnp.where(first, mean_q, mean_k)
        square = center * center
        var_q = jnp.sum(jnp.where(first, square, 0.0), axis=1, keepdims=True) / head_dim
        var_k = jnp.sum(jnp.where(first, 0.0, square), axis=1, keepdims=True) / head_dim
        scale = jnp.where(first, lax.rsqrt(var_q + EPS_HEAD), lax.rsqrt(var_k + EPS_HEAD))
        normed = center * scale * gain + bias
        swapped = jnp.where(even, pltpu.roll(normed, pair - 1, 1), pltpu.roll(normed, 1, 1))
        turned = normed * cosine + swapped * sine
        q_ref[h] = jnp.where(first, turned, mask_part).astype(BF)
        pair_ref[h] = jnp.where(first, pltpu.roll(turned, head_dim, 1), key_value).astype(BF)


def prepare(qkv, cosine, sine, kinds, norm_rows, heads, head_dim):
    rows, width = qkv.shape
    block = min(256, rows)
    pair = 2 * head_dim
    return pl.pallas_call(
        functools.partial(prepare_kernel, heads, head_dim),
        grid=(rows // block,),
        in_specs=[
            pl.BlockSpec((block, width), lambda i: (i, 0)),
            pl.BlockSpec((block, pair), lambda i: (i, 0)),
            pl.BlockSpec((block, pair), lambda i: (i, 0)),
            pl.BlockSpec((block, 1), lambda i: (i, 0)),
            pl.BlockSpec((2, pair), lambda i: (0, 0)),
        ],
        out_specs=[
            pl.BlockSpec((heads, block, pair), lambda i: (0, i, 0)),
            pl.BlockSpec((heads, block, pair), lambda i: (0, i, 0)),
        ],
        out_shape=[
            jax.ShapeDtypeStruct((heads, rows, pair), BF),
            jax.ShapeDtypeStruct((heads, rows, pair), BF),
        ],
        compiler_params=pltpu.CompilerParams(vmem_limit_bytes=48 * 1024 * 1024),
        name="prepare",
    )(qkv, cosine, sine, kinds[:, None], norm_rows)


def attend_kernel(heads, head_dim, q_ref, own_ref, other_ref, own_mask_ref, other_mask_ref, out_ref):
    pair = 2 * head_dim
    keys_count = own_ref.shape[1]
    lane = lax.broadcasted_iota(jnp.int32, (keys_count, pair), 1)
    first = lane < head_dim
    one = jnp.where(lane == 0, 1.0, 0.0).astype(BF)
    factor = LOG2E * head_dim ** (-0.5)
    pieces = []
    for h in range(heads):
        queries = q_ref[h]
        own = own_ref[h]
        other = other_ref[h]
        contract = (((1,), (1,)), ((), ()))
        scores_a = lax.dot_general(
            queries, jnp.where(first, own, own_mask_ref[...]), contract, preferred_element_type=F32
        )
        scores_b = lax.dot_general(
            queries, jnp.where(first, other, other_mask_ref[...]), contract, preferred_element_type=F32
        )
        top = jnp.maximum(
            jnp.max(scores_a, axis=1, keepdims=True), jnp.max(scores_b, axis=1, keepdims=True)
        )
        weights_a = jnp.exp2((scores_a - top) * factor).astype(BF)
        weights_b = jnp.exp2((scores_b - top) * factor).astype(BF)
        mixed = jnp.dot(weights_a, jnp.where(first, one, own), preferred_element_type=F32)
        mixed += jnp.dot(weights_b, jnp.where(first, one, other), preferred_element_type=F32)
        pieces.append(mixed[:, head_dim:] / mixed[:, 0:1])
    out_ref[...] = jnp.concatenate(pieces, axis=1).astype(BF)


def attend(queries, own, other, own_mask, other_mask, head_dim):
    heads, rows, pair = queries.shape
    keys_count = own.shape[1]
    block = min(256, rows)
    whole = pl.BlockSpec((heads, keys_count, pair), lambda i: (0, 0, 0))
    mask = pl.BlockSpec((keys_count, pair), lambda i: (0, 0))
    return pl.pallas_call(
        functools.partial(attend_kernel, heads, head_dim),
        grid=(rows // block,),
        in_specs=[pl.BlockSpec((heads, block, pair), lambda i: (0, i, 0)), whole, whole, mask, mask],
        out_specs=pl.BlockSpec((block, heads * head_dim), lambda i: (i, 0)),
        out_shape=jax.ShapeDtypeStruct((rows, heads * head_dim), BF),
        compiler_params=pltpu.CompilerParams(vmem_limit_bytes=48 * 1024 * 1024),
        name="attend",
    )(queries, own, other, own_mask, other_mask)


def key_mask(kinds, head_dim):
    lane = jnp.arange(2 * head_dim)[None, :]
    foreign = (lane >= head_dim) & (lane < head_dim + 2) & (lane - head_dim != (kinds // 2)[:, None])
    return jnp.where(foreign, FAR, 0.0).astype(BF)


def pick(table, kinds, part):
    column = kinds[:, None]
    low = jnp.where(column == 0, table[0, part][None], table[1, part][None])
    high = jnp.where(column == 2, table[2, part][None], table[3, part][None])
    return jnp.where(column < 2, low, high)


def exchange(blocks, axis):
    n = lax.axis_size(axis)
    me = lax.axis_index(axis)
    got = jnp.zeros_like(blocks)
    got = lax.dynamic_update_slice_in_dim(
        got, lax.dynamic_slice_in_dim(blocks, me, 1, 0), me, 0
    )
    for step in range(1, n):
        there = (me + step) % n
        back = (me + n - step) % n
        block = lax.dynamic_slice_in_dim(blocks, there, 1, 0)
        block = lax.ppermute(block, axis, [(i, (i + step) % n) for i in range(n)])
        got = lax.dynamic_update_slice_in_dim(got, block, back, 0)
    return got


def per_device(
    hidden_in,
    row_kind,
    positions,
    timesteps,
    stale_cache,
    w_qkv,
    qk_norm,
    w_out,
    ada_weight,
    w_up,
    w_down,
):
    operands = (
        hidden_in,
        row_kind,
        positions,
        timesteps,
        stale_cache,
        w_qkv[0],
        qk_norm[0],
        w_out[0],
        ada_weight[0],
        w_up[0],
        w_down[0],
    )
    n_narrow = lax.axis_size("narrow")
    if n_narrow == 4 and lax.axis_size("wide") == 4 and stale_cache.shape[3] % n_narrow == 0:
        return in_pairs(*operands)
    return features_split(*operands)


def swap(value):
    return lax.ppermute(value, "section", [(0, 1), (1, 0)])


def by_layer(parts, lead):
    got = swap(jnp.where(lead, parts[1], parts[0]))
    kept = jnp.where(lead, parts[0], parts[1])
    return jnp.stack([jnp.where(lead, kept, got), jnp.where(lead, got, kept)])[None]


def norm_pairs(norms):
    return jnp.stack([jnp.concatenate([norms[0], norms[2]]), jnp.concatenate([norms[1], norms[3]])])


def modulate(values, table, kinds):
    return (values * (1.0 + pick(table, kinds, 1)) + pick(table, kinds, 0)).astype(BF)


def wide_pairs(step):
    return [(i, i ^ step) for i in range(lax.axis_size("wide"))]


def gather_wide(block):
    got = [lax.ppermute(block, "wide", wide_pairs(step)) for step in range(1, lax.axis_size("wide"))]
    return jnp.concatenate([block] + got, axis=0)


def scatter_wide(terms):
    total = terms[0].astype(F32)
    for step in range(1, len(terms)):
        total += lax.ppermute(terms[step], "wide", wide_pairs(step)).astype(F32)
    return total


def to_mate(value):
    return lax.ppermute(value, "narrow", [(i, i ^ 1) for i in range(lax.axis_size("narrow"))])


def to_partner(value):
    return lax.ppermute(value, "narrow", [(i, i ^ 2) for i in range(lax.axis_size("narrow"))])


def statistics(values):
    width = values.shape[1]
    mean = jnp.mean(values, axis=1)
    center = values - mean[:, None]
    own = jnp.stack([mean, jnp.sum(center * center, axis=1)])
    far = to_partner(own)
    whole_mean = 0.5 * (own[0] + far[0])
    spread = own[1] + far[1] + width * ((own[0] - whole_mean) ** 2 + (far[0] - whole_mean) ** 2)
    return whole_mean, lax.rsqrt(spread / (2 * width) + EPS_ROW)


def normed(values, moments, table, kinds):
    mean, scale = moments
    return modulate((values - mean[:, None]) * scale[:, None], table, kinds)


def ordered(*values):
    return lax.optimization_barrier(values)


def in_pairs(
    hidden_in,
    row_kind,
    positions,
    timesteps,
    stale_cache,
    w_qkv,
    qk_norm,
    w_out,
    ada_weight,
    w_up,
    w_down,
):
    n_wide = lax.axis_size("wide")
    n_narrow = lax.axis_size("narrow")
    wide_idx = lax.axis_index("wide")
    narrow_idx = lax.axis_index("narrow")
    section = lax.axis_index("section")
    lead = section == 0
    odd = narrow_idx % 2
    high = narrow_idx // 2
    lower = high == 0
    _, rows_a, feat_a = hidden_in.shape
    halves = 2
    part = rows_a // halves
    total_rows = rows_a * n_wide
    chunk = total_rows // halves
    rows_b = total_rows // n_narrow
    heads_local = stale_cache.shape[3]
    heads = heads_local // n_narrow
    pair = stale_cache.shape[4]
    head_dim = pair // 2
    head_group = [0, 2, 1, 3]

    def both_layers(own):
        other = swap(own)
        return (jnp.where(lead, own, other), jnp.where(lead, other, own))

    def relative(values):
        blocks = values.reshape(n_wide, halves, part)
        order = [lax.dynamic_index_in_dim(blocks, wide_idx ^ step, 0, False) for step in range(n_wide)]
        return jnp.stack(order, axis=1).reshape(total_rows)

    def mate_half(layer, sent):
        pairs = [(layer * n_narrow + i, layer * n_narrow + (i ^ 1)) for i in range(n_narrow)]
        return lax.ppermute(sent, ("section", "narrow"), pairs)

    def passed(layer, value):
        return lax.ppermute(value, "section", [(layer, 1 - layer)])

    def pass_on(layer, kept, got, axis):
        joined = jnp.concatenate([kept, got], axis=axis)
        return joined, passed(layer, joined)

    def weight_of(layer, parts, axis):
        return pass_on(layer, parts[0], mate_half(layer, parts[1]), axis)

    def select(layer, weight):
        return jnp.where(section == layer, weight[0], weight[1])

    def two_blocks(own, axis, size, first, second):
        starts = [first * size, second * size]
        return jnp.concatenate([lax.dynamic_slice_in_dim(own, at, size, axis) for at in starts], axis=axis)

    size = w_qkv.shape[1] // 4
    qkv_parts = [two_blocks(w_qkv, 1, size, 2 * p + 1 - high, 2 * p + high) for p in (odd, 1 - odd)]
    size = w_out.shape[0] // 4
    out_parts = [two_blocks(w_out, 0, size, 2 * p + high, 2 * p + 1 - high) for p in (odd, 1 - odd)]
    size = w_up.shape[1] // 2
    up_parts = [lax.dynamic_slice_in_dim(w_up, p * size, size, 1) for p in (odd, 1 - odd)]
    size = w_down.shape[0] // 2
    down_parts = [lax.dynamic_slice_in_dim(w_down, p * size, size, 0) for p in (odd, 1 - odd)]

    def ordered_parts(value, parts):
        value, sent = ordered(value, parts[1])
        return value, (parts[0], sent)

    layer_in = lax.dynamic_index_in_dim(hidden_in, section, 0, False)
    layer_in = jnp.concatenate([layer_in, to_mate(layer_in)], axis=1)
    layer_in, timesteps = ordered(layer_in, timesteps)
    first_mean, first_scale = statistics(layer_in.astype(F32))
    layer_in = [layer_in[h * part : (h + 1) * part] for h in range(halves)]
    activated = jax.nn.silu(time_features(timesteps, ada_weight.shape[1])).astype(BF)
    modulation = jnp.einsum("re,kesd->krsd", activated, ada_weight, preferred_element_type=F32)
    modulation = modulation.reshape(2, 4, 3, feat_a)
    modulation = jnp.concatenate([modulation, to_mate(modulation)], axis=-1)
    kept = passed(0, qkv_parts[0])
    modulation, first_mean, sent, kept = ordered(modulation, first_mean, qkv_parts[1], kept)
    got = mate_half(0, sent)
    qkv_now = jnp.concatenate(
        [jnp.where(lead, qkv_parts[0], kept), jnp.where(lead, got, passed(0, got))], axis=0
    )
    shape = modulation.shape
    width = shape[-1]
    rows = modulation.reshape(-1, width)
    last = jnp.concatenate([qk_norm.reshape(-1), jnp.zeros((width - qk_norm.size,), F32)])
    both = both_layers(jnp.concatenate([rows, last[None]], axis=0))
    tables = [table[:-1].reshape(shape) for table in both]
    norm_rows = [table[-1, : qk_norm.size].reshape(qk_norm.shape) for table in both]

    kinds = lax.dynamic_index_in_dim(row_kind, section, 0, False)
    kinds_other = lax.dynamic_index_in_dim(row_kind, 1 - section, 0, False)
    kinds_r = relative(kinds)
    own_mask = key_mask(kinds_r, head_dim)
    other_mask = key_mask(jnp.where(lead, kinds_other, relative(kinds_other)), head_dim)
    kinds_a = lax.dynamic_slice_in_dim(kinds, wide_idx * rows_a, rows_a)
    kinds_h = [kinds_a[h * part : (h + 1) * part] for h in range(halves)]
    places = lax.dynamic_index_in_dim(positions, section, 1, False)
    places = jnp.stack([relative(places[i]) for i in range(3)])
    cosine, sine = rotary_tables(places, head_dim)

    def stale_heads(rows_part):
        blocks = rows_part.reshape(rows_b, n_narrow, heads, pair)
        blocks = jnp.stack([blocks[:, group] for group in head_group]).transpose(0, 2, 1, 3)
        got = exchange(blocks, "narrow")
        return got.transpose(1, 0, 2, 3).reshape(heads, total_rows, pair)

    def to_rows(fresh):
        blocks = [f.reshape(heads, n_wide, part, pair) for f in fresh]
        per_narrow = []
        for there in range(n_narrow):
            picked = [lax.dynamic_index_in_dim(b, wide_idx ^ there, 1, False) for b in blocks]
            per_narrow.append(jnp.concatenate(picked, axis=1))
        got = exchange(jnp.stack(per_narrow), "narrow")
        got = jnp.stack([got[sender] for sender in head_group])
        return got.transpose(2, 0, 1, 3).reshape(rows_b, heads_local, pair)

    def summed(terms):
        total = scatter_wide([terms[r * part : (r + 1) * part] for r in range(n_wide)]).astype(BF)
        far = to_mate(jnp.concatenate([total[:, feat_a:], total[:, :feat_a]], axis=1))
        return total.astype(F32) + far.astype(F32)

    def summed_mine(terms):
        total = scatter_wide([terms[r * part : (r + 1) * part] for r in range(n_wide)]).astype(BF)
        return total[:, :feat_a].astype(F32) + to_mate(total[:, feat_a:]).astype(F32)

    results = []
    caches = []
    for layer in range(2):
        table = tables[layer]
        norm_pair = norm_pairs(norm_rows[layer])
        x_in = [block.astype(F32) for block in layer_in]
        queries = []
        fresh = []
        for h in range(halves):
            if layer == 0:
                rows = slice(h * part, (h + 1) * part)
                moments = (first_mean[rows], first_scale[rows])
            else:
                moments = statistics(x_in[h])
            entry = normed(x_in[h], moments, table[0], kinds_h[h])
            if layer == 0 and h == 0:
                entry, stale = ordered(entry, stale_cache[0, 1])
                stale = stale_heads(stale)
                entry, out_sent = ordered(entry, out_parts[1])
                out_got = mate_half(0, out_sent)
            terms = jnp.dot(gather_wide(entry), qkv_now, preferred_element_type=F32).astype(BF)
            if layer == 0 and h == 1:
                terms, stale, out_got, up_sent = ordered(terms, stale, out_got, up_parts[1])
                out_weight = pass_on(0, out_parts[0], out_got, 1)
                up_got = mate_half(0, up_sent)
            width = terms.shape[1] // 2
            qkv = terms[:, width:].astype(F32) + to_partner(terms[:, :width]).astype(F32)
            rows = slice(h * chunk, (h + 1) * chunk)
            q, pairs = prepare(
                qkv, cosine[rows], sine[rows], kinds_r[rows], norm_pair, heads, head_dim
            )
            queries.append(q)
            fresh.append(pairs)
        own = jnp.concatenate(fresh, axis=1)
        own, *out_weight = ordered(own, *out_weight)
        if layer == 0:
            other = jnp.where(lead, stale, lax.ppermute(own, "section", [(0, 1)]))
        else:
            other = swap(jnp.where(lead, own, stale))
        after = []
        for h in range(halves):
            attended = attend(queries[h], own, other, own_mask, other_mask, head_dim)
            attended = jnp.concatenate([attended, to_partner(attended)], axis=1)
            terms = jnp.dot(attended, select(layer, out_weight), preferred_element_type=F32).astype(BF)
            if layer == 0 and h == 0:
                terms, up_got = ordered(terms, up_got)
                up_weight = pass_on(0, up_parts[0], up_got, 0)
            if h == 1:
                terms, down_sent, *fresh = ordered(terms, down_parts[1], *fresh)
                cache = to_rows(fresh)
                down_weight = weight_of(layer, (down_parts[0], down_sent), 1)
            after.append(x_in[h] + pick(table[0], kinds_h[h], 2) * summed(terms))
        inner = []
        for h in range(halves):
            entry = normed(after[h], statistics(after[h]), table[1], kinds_h[h])
            if layer == 0 and h == 0:
                entry, parts = ordered_parts(entry, qkv_parts)
                qkv_weight = weight_of(1, parts, 0)
            entry = gather_wide(entry)
            up = jnp.dot(entry, select(layer, up_weight), preferred_element_type=F32).astype(BF)
            size = chunk // 2
            got = to_partner(lax.dynamic_slice_in_dim(up, (1 - high) * size, size, 0))
            up = lax.dynamic_slice_in_dim(up, high * size, size, 0).astype(F32) + got.astype(F32)
            inner.append(jax.nn.gelu(up, approximate=True).astype(BF))
        layer_in = []
        for h in range(halves):
            got = to_partner(inner[h])
            if h == 1:
                got, cache = ordered(got, cache)
                caches.append(cache)
            first = jnp.where(lower, inner[h], got)
            second = jnp.where(lower, got, inner[h])
            whole = jnp.concatenate([first, second], axis=0)
            terms = jnp.dot(whole, select(layer, down_weight), preferred_element_type=F32).astype(BF)
            if layer == 0 and h == 0:
                terms, parts = ordered_parts(terms, out_parts)
                out_weight = weight_of(1, parts, 1)
                terms, parts = ordered_parts(terms, up_parts)
                up_weight = weight_of(1, parts, 0)
                qkv_now = select(1, qkv_weight)
            gate = pick(table[1], kinds_h[h], 2)
            if layer == 1:
                mine = after[h][:, :feat_a] + gate[:, :feat_a] * summed_mine(terms)
                layer_in.append(mine.astype(BF))
            else:
                layer_in.append((after[h] + gate * summed(terms)).astype(BF))
        results.append(jnp.concatenate([block[:, :feat_a] for block in layer_in], axis=0))
    return (by_layer(results, lead), by_layer(caches, lead))


def features_split(
    hidden_in,
    row_kind,
    positions,
    timesteps,
    stale_cache,
    w_qkv,
    qk_norm,
    w_out,
    ada_weight,
    w_up,
    w_down,
):
    n_wide = lax.axis_size("wide")
    n_narrow = lax.axis_size("narrow")
    wide_idx = lax.axis_index("wide")
    narrow_idx = lax.axis_index("narrow")
    section = lax.axis_index("section")
    patch_count, rows_a, feat_a = hidden_in.shape
    total_rows = rows_a * n_wide
    rows_b = total_rows // n_narrow
    heads_local = stale_cache.shape[3]
    pair = stale_cache.shape[4]
    head_dim = pair // 2
    model_width = feat_a * n_narrow
    heads = heads_local
    lead = section == 0

    def both_layers(own):
        other = swap(own)
        return (jnp.where(lead, own, other), jnp.where(lead, other, own))

    qkv_weights = both_layers(w_qkv)
    out_weights = both_layers(w_out)
    up_weights = both_layers(w_up)
    down_weights = both_layers(w_down)
    norm_rows = both_layers(qk_norm)

    activated = jax.nn.silu(time_features(timesteps, ada_weight.shape[1])).astype(BF)
    modulation = jnp.einsum("re,kesd->krsd", activated, ada_weight, preferred_element_type=F32)
    tables = both_layers(modulation.reshape(2, 4, 3, feat_a))

    kinds = lax.dynamic_slice_in_dim(row_kind, section, 1, 0)[0]
    kinds_other = lax.dynamic_slice_in_dim(row_kind, 1 - section, 1, 0)[0]
    own_mask = key_mask(kinds, head_dim)
    other_mask = key_mask(kinds_other, head_dim)
    kinds_a = lax.dynamic_slice_in_dim(kinds, wide_idx * rows_a, rows_a)
    places = lax.dynamic_slice_in_dim(positions, section, 1, 1)[:, 0]
    places = lax.dynamic_slice_in_dim(places, narrow_idx * rows_b, rows_b, 1)
    kinds_q = lax.dynamic_slice_in_dim(kinds, narrow_idx * rows_b, rows_b)
    cosine, sine = rotary_tables(places, head_dim)

    stale = lax.all_gather(stale_cache[0, 1].transpose(1, 0, 2), "narrow", axis=1, tiled=True)

    def normalize(values):
        moments = lax.psum(
            jnp.stack([jnp.sum(values, axis=1), jnp.sum(values * values, axis=1)]), "narrow"
        )
        row_mean = moments[0] / model_width
        variance = moments[1] / model_width - row_mean * row_mean
        return (values - row_mean[:, None]) * lax.rsqrt(variance + EPS_ROW)[:, None]

    layer_in = lax.dynamic_slice_in_dim(hidden_in, section, 1, 0)[0]
    results = []
    caches = []
    for layer in range(2):
        table = tables[layer]
        x_in = layer_in.astype(F32)
        entry = modulate(normalize(x_in), table[0], kinds_a)
        qkv_terms = jnp.dot(
            lax.all_gather(entry, "wide", axis=0, tiled=True),
            qkv_weights[layer],
            preferred_element_type=F32,
        ).astype(BF)
        qkv = lax.psum_scatter(qkv_terms, "narrow", scatter_dimension=0, tiled=True)
        queries, fresh = prepare(
            qkv, cosine, sine, kinds_q, norm_pairs(norm_rows[layer]), heads, head_dim
        )
        caches.append(fresh.transpose(1, 0, 2))
        fresh = lax.all_gather(fresh, "narrow", axis=1, tiled=True)
        if layer == 0:
            other = jnp.where(lead, stale, swap(fresh))
        else:
            other = swap(jnp.where(lead, fresh, stale))
        attended = attend(queries, fresh, other, own_mask, other_mask, head_dim)
        attended = lax.all_gather(attended, "narrow", axis=0, tiled=True)
        proj_terms = jnp.dot(attended, out_weights[layer], preferred_element_type=F32).astype(BF)
        projected = lax.psum_scatter(proj_terms, "wide", scatter_dimension=0, tiled=True)
        after = x_in + pick(table[0], kinds_a, 2) * projected.astype(F32)
        entry = modulate(normalize(after), table[1], kinds_a)
        up_terms = jnp.dot(
            lax.all_gather(entry, "wide", axis=0, tiled=True),
            up_weights[layer],
            preferred_element_type=F32,
        ).astype(BF)
        up_sum = lax.psum_scatter(up_terms, "narrow", scatter_dimension=0, tiled=True)
        inner = jax.nn.gelu(up_sum.astype(F32), approximate=True).astype(BF)
        down_terms = jnp.dot(
            lax.all_gather(inner, "narrow", axis=0, tiled=True),
            down_weights[layer],
            preferred_element_type=F32,
        ).astype(BF)
        down_sum = lax.psum_scatter(down_terms, "wide", scatter_dimension=0, tiled=True)
        layer_in = (after + pick(table[1], kinds_a, 2) * down_sum.astype(F32)).astype(BF)
        results.append(layer_in)

    return (by_layer(results, lead), by_layer(caches, lead))


def solution(mesh):
    in_specs = (
        P(None, "wide", "narrow"),
        P(),
        P(),
        P(),
        P("section", None, "narrow", "wide", None),
        P("section", "narrow", "wide"),
        P("section", None, None),
        P("section", "wide", "narrow"),
        P("section", None, None, None, "narrow"),
        P("section", "narrow", "wide"),
        P("section", "wide", "narrow"),
    )
    out_specs = (P("section", None, "wide", "narrow"), P("section", None, "narrow", "wide", None))
    return jax.shard_map(
        per_device, mesh=mesh, in_specs=in_specs, out_specs=out_specs, check_vma=False
    )
```
